32 devices in a mesh: replica: 4 (over y, core), fsdp: 8 (over z, x).
Axes of the slice: x: 2, y: 2, z: 4, core: 2. Of those that a mesh axis runs over, the one named last changes fastest.
Arguments:
- local_weights: bfloat16 [4, 2048, 512], P('replica', 'fsdp'), may hold values from -0.125 to 0.125
- global_weights: bfloat16 [2048, 512], P('fsdp'), may hold values from -0.125 to 0.125
- momentum: float32 [2048, 512], P('fsdp', 'replica'), may hold values from -0.12 to 0.12
- activations: bfloat16 [4, 2048, 2048], P('replica', 'fsdp'), may hold values from -6 to 6
- kv_cotangent: bfloat16 [4, 2048, 512], P('replica', 'fsdp'), may hold values from -6 to 6
Outputs:
- kv_rows: bfloat16 [4, 2048, 512], P('replica', 'fsdp')
- input_grad: bfloat16 [4, 2048, 2048], P('replica', 'fsdp')
- weight_grad: bfloat16 [4, 2048, 512], P('replica', 'fsdp')
- new_global: bfloat16 [2048, 512], P('fsdp')
- new_momentum: float32 [2048, 512], P('fsdp', 'replica')
The draws below stay inside these ranges and needn't reach their ends.
All inputs are finite; a program needn't handle non-finite values. Where the reference program divides by a largest or mean magnitude, that divisor is 1e-20 or more.
Results may differ from the reference program's by a relative error of at most 0.0038.
Values may be sent and summed in bfloat16 or wider, within the bound.
No kernel may reach another device: no remote copies, remote signals or barrier semaphores. Data moves between devices by JAX's collectives and lax.ppermute only.
A program may use at most 64 MiB of HBM per device.

```python
import jax
import jax.numpy as jnp
from jax import lax

D = 2048
KV = 512
BLOCK = 64
TOKENS = 2048
N_REPLICA = 4


def raised(drawn, rng, source, target, shards_of, factor):
    owner, partner = [(jnp.arange(drawn.shape[dim]) // (drawn.shape[dim] // shards_of)).reshape([-1 if axis == dim else 1 for axis in range(drawn.ndim)]) for dim in (source, target)]
    chosen = jax.random.permutation(rng, shards_of)[partner]
    strong = (owner == chosen) | (owner == (partner + shards_of // 2) % shards_of)
    return jnp.where(strong, factor * drawn, drawn)


def block_levels(key, shape, shards, smallest, largest):
    def one(position, parts):
        heights = jax.random.uniform(jax.random.fold_in(jax.random.fold_in(key, 6), position), (parts,), jnp.float32, smallest / len(shards), largest / len(shards))
        return jnp.repeat(jnp.exp(heights), shape[position] // parts).reshape((-1,) + (1,) * (len(shape) - position - 1))

    factor_of = one(*shards[0])
    for cut in shards[1:]:
        factor_of = factor_of * one(*cut)
    return factor_of


def bell_draw(rng, dims, scale, limit, split=(), held_as=jnp.bfloat16):
    level = block_levels(rng, dims, split, -0.22, 0.18) if split else 1.0
    entries = jax.random.normal(rng, dims, jnp.float32) * scale * level
    return jnp.minimum(jnp.maximum(entries, -limit), limit).astype(held_as)


def gaussian_with(rng, dims, deviation, limit, split, heavy, dtype=jnp.bfloat16):
    entries = deviation * jax.random.normal(rng, dims, jnp.float32)
    if split:
        entries = entries * block_levels(rng, dims, split, -0.22, 0.18)
    return jnp.clip(raised(entries, jax.random.fold_in(rng, 3), *heavy), -limit, limit).astype(dtype)


def setup_inputs(seed: int = 0) -> dict:
    splits = jax.random.split(jax.random.key(seed), 6)
    local_weights = bell_draw(splits[0], (N_REPLICA, D, KV), D ** -0.5, 0.125, ((0, 4), (1, 8)))
    global_weights = bell_draw(splits[1], (D, KV), D ** -0.5, 0.125, ((0, 8),))
    momentum = bell_draw(splits[2], (D, KV), 0.02, 0.12, ((0, 8), (1, 4)), jnp.float32)
    activations = gaussian_with(splits[3], (N_REPLICA, TOKENS, D), 1.0, 6.0, ((0, 4), (1, 8)), (1, 2, 8, 2.0))
    kv_cotangent = bell_draw(splits[4], (N_REPLICA, TOKENS, KV), 1.0, 6.0, ((0, 4), (1, 8)))
    return {"local_weights": local_weights, "global_weights": global_weights, "momentum": momentum, "activations": activations, "kv_cotangent": kv_cotangent}


outer_rate = 0.7
outer_momentum = 0.9
scale_epsilon = 1e-6


def reference(local_weights, global_weights, momentum, activations, kv_cotangent):
    token_weight = 1.0 / TOKENS

    def inner_step(items):
        weights_one, inputs_one, cotangent_one = items
        kv_one = jnp.dot(inputs_one, weights_one, preferred_element_type=jnp.float32).astype(jnp.bfloat16)
        grad_in = jnp.dot(cotangent_one, weights_one.T, preferred_element_type=jnp.float32).astype(jnp.bfloat16)
        summed = jnp.dot(inputs_one.T, cotangent_one, preferred_element_type=jnp.float32) * token_weight
        return kv_one, grad_in, summed.astype(jnp.bfloat16)

    kv_rows, input_grad, weight_grad = lax.map(inner_step, (local_weights, activations, kv_cotangent))

    drift = global_weights.astype(jnp.float32)[None] - local_weights.astype(jnp.float32)
    drift_blocks = drift.reshape(N_REPLICA, D, KV // BLOCK, BLOCK)
    block_scale = (jnp.max(jnp.abs(drift_blocks), axis=3) + scale_epsilon).astype(jnp.bfloat16)
    block_scale = lax.optimization_barrier(block_scale)
    quantized = (drift_blocks / block_scale.astype(jnp.float32)[..., None]).astype(jnp.bfloat16)
    quantized = lax.optimization_barrier(quantized)
    dequantized = quantized.astype(jnp.float32) * block_scale.astype(jnp.float32)[..., None]
    mean_grad = jnp.sum(dequantized, axis=0).reshape(D, KV) / N_REPLICA
    new_momentum = outer_momentum * momentum + mean_grad
    new_global = (global_weights.astype(jnp.float32) - outer_rate * (mean_grad + outer_momentum * new_momentum)).astype(jnp.bfloat16)
    return kv_rows, input_grad, weight_grad, new_global, new_momentum
```

```python
import functools

import jax
import jax.numpy as jnp
from jax import lax
from jax.experimental import pallas as pl
from jax.experimental.pallas import tpu as pltpu
from jax.sharding import PartitionSpec as P

BLOCK = 64

outer_rate = 0.7
outer_momentum = 0.9
scale_epsilon = 1e-06

F32 = jnp.float32
BF16 = jnp.bfloat16


def ring_order(size):
    return list(range(0, size, 2)) + list(range(1, size, 2))[::-1]


def ring_place(index, size):
    return jnp.where(index % 2 == 0, index // 2, size - 1 - index // 2)


def ring_index(place, size):
    place = (place + size) % size
    evens = (size + 1) // 2
    return jnp.where(place < evens, 2 * place, 2 * (size - 1 - place) + 1)


def vmem_call(kernel, out_shape, operands, flops, name):
    moved = sum(x.size * x.dtype.itemsize for x in operands)
    return pl.pallas_call(
        kernel,
        out_shape=out_shape,
        in_specs=[pl.BlockSpec(memory_space=pltpu.VMEM)] * len(operands),
        out_specs=jax.tree.map(lambda _: pl.BlockSpec(memory_space=pltpu.VMEM), out_shape),
        compiler_params=pltpu.CompilerParams(vmem_limit_bytes=32 * 2**20),
        cost_estimate=pl.CostEstimate(flops=flops, bytes_accessed=moved, transcendentals=0),
        name=name,
    )(*operands)


def outer_kernel(replicas, share_cols, *refs):
    local_refs = refs[:replicas]
    global_ref, momentum_ref, share_ref, new_momentum_ref = refs[replicas:]
    rows, window = global_ref.shape
    old = global_ref[...].astype(F32)
    lane = lax.broadcasted_iota(jnp.int32, (rows, window), 1) // BLOCK
    total = jnp.zeros((rows, window), F32)
    for local_ref in local_refs:
        drift = old - local_ref[...].astype(F32)
        size = jnp.abs(drift)
        scale = jnp.zeros((rows, window), F32)
        for block in range(window // BLOCK):
            top = jnp.max(jnp.where(lane == block, size, 0.0), axis=1, keepdims=True)
            top = (top + scale_epsilon).astype(BF16).astype(F32)
            scale = jnp.where(lane == block, top, scale)
        total = total + (drift / scale).astype(BF16).astype(F32) * scale
    mean_grad = total / replicas
    shares = window // share_cols
    mean_here, old_here = mean_grad[:, :share_cols], old[:, :share_cols]
    mine = lax.axis_index("replica") % shares
    for share in range(1, shares):
        columns = slice(share * share_cols, (share + 1) * share_cols)
        mean_here = jnp.where(mine == share, mean_grad[:, columns], mean_here)
        old_here = jnp.where(mine == share, old[:, columns], old_here)
    new_momentum = outer_momentum * momentum_ref[...] + mean_here
    new_momentum_ref[...] = new_momentum
    share_ref[...] = (old_here - outer_rate * (mean_here + outer_momentum * new_momentum)).astype(BF16)


def join_kernel(*refs):
    *share_refs, out_ref = refs
    me = lax.axis_index("replica")
    count = len(share_refs)
    width = out_ref.shape[1] // count
    pieces = [ref[...] for ref in share_refs]
    bit = 1
    while bit < count:
        odd = (me & bit) != 0
        pieces = [jnp.where(odd, pieces[at ^ bit], pieces[at]) for at in range(count)]
        bit *= 2
    for at in range(count):
        out_ref[:, at * width : (at + 1) * width] = pieces[at]


def outer_step(local_shard, global_weights, momentum):
    rows, kv_width = local_shard.shape
    replicas = lax.axis_size("replica")
    me = lax.axis_index("replica")
    share_cols = kv_width // replicas
    window = max(share_cols, BLOCK)

    def window_of(array, owner):
        return lax.dynamic_slice_in_dim(array, owner * share_cols // window * window, window, 1)

    def swap(array, bits):
        return lax.ppermute(array, "replica", [(at, at ^ bits) for at in range(replicas)])

    locals_here = [window_of(local_shard, me)]
    for bits in range(1, replicas):
        locals_here.append(swap(window_of(local_shard, me ^ bits), bits))
    new_share, new_momentum = vmem_call(
        functools.partial(outer_kernel, replicas, share_cols),
        (jax.ShapeDtypeStruct((rows, share_cols), BF16), jax.ShapeDtypeStruct((rows, share_cols), F32)),
        locals_here + [window_of(global_weights, me), momentum],
        20 * replicas * rows * window,
        "outer_update",
    )
    shares = [new_share] + [swap(new_share, bits) for bits in range(1, replicas)]
    new_global = vmem_call(
        join_kernel, jax.ShapeDtypeStruct((rows, kv_width), BF16), shares, rows * kv_width, "join_shares"
    )
    return new_global, new_momentum


def products_kernel(size, inputs_ref, cotangent_ref, *refs):
    *block_refs, rows_ref, grad_ref = refs
    depth = grad_ref.shape[1] // size
    place = ring_place(lax.axis_index("fsdp"), size)
    total = jnp.zeros(rows_ref.shape, F32)
    for step, block_ref in enumerate(block_refs):
        at = pl.multiple_of(ring_index(place + step, size) * depth, depth)
        block = block_ref[...]
        total = total + jnp.dot(inputs_ref[:, pl.ds(at, depth)], block, preferred_element_type=F32)
        grad_ref[:, pl.ds(at, depth)] = lax.dot_general(
            cotangent_ref[...], block, (((1,), (1,)), ((), ())), preferred_element_type=F32
        ).astype(BF16)
    rows_ref[...] = total.astype(BF16)


def products(inputs_here, cotangent, blocks):
    tokens, width = inputs_here.shape
    size = len(blocks)
    depth, kv_width = blocks[0].shape
    if depth % 128 == 0:
        return vmem_call(
            functools.partial(products_kernel, size),
            (jax.ShapeDtypeStruct((tokens, kv_width), BF16), jax.ShapeDtypeStruct((tokens, width), BF16)),
            [inputs_here, cotangent] + blocks,
            4 * tokens * width * kv_width,
            "projection_products",
        )
    place = ring_place(lax.axis_index("fsdp"), size)
    gathered = jnp.zeros((width, kv_width), BF16)
    for step, block in enumerate(blocks):
        gathered = lax.dynamic_update_slice_in_dim(gathered, block, ring_index(place + step, size) * depth, 0)
    rows = jnp.dot(inputs_here, gathered, preferred_element_type=F32).astype(BF16)
    grad = lax.dot_general(cotangent, gathered, (((1,), (1,)), ((), ())), preferred_element_type=F32)
    return rows, grad.astype(BF16)


def per_device(local_weights, global_weights, momentum, activations, kv_cotangent):
    local_shard = local_weights[0]
    inputs_here = activations[0]
    cotangent = kv_cotangent[0]
    depth = local_shard.shape[0]
    size = lax.axis_size("fsdp")
    token_weight = 1.0 / (inputs_here.shape[0] * size)
    order = ring_order(size)
    up = [(order[at], order[(at + 1) % size]) for at in range(size)]
    down = [(target, source) for source, target in up]
    place = ring_place(lax.axis_index("fsdp"), size)
    far = size // 2
    cut = depth // 2

    blocks = [None] * size
    blocks[0] = local_shard
    from_below = from_above = local_shard
    for step in range(1, far):
        from_below = lax.ppermute(from_below, "fsdp", up)
        from_above = lax.ppermute(from_above, "fsdp", down)
        blocks[size - step] = from_below
        blocks[step] = from_above
    blocks[far] = jnp.concatenate(
        [lax.ppermute(from_below[:cut], "fsdp", up), lax.ppermute(from_above[cut:], "fsdp", down)]
    )

    def terms(offset):
        columns = lax.dynamic_slice_in_dim(inputs_here, ring_index(place + offset, size) * depth, depth, 1)
        return (
            lax.dot_general(columns, cotangent, (((0,), (0,)), ((), ())), preferred_element_type=F32) * token_weight
        )

    farthest = terms(far).astype(BF16)
    sum_up = lax.ppermute(farthest[:cut], "fsdp", up)
    sum_down = lax.ppermute(farthest[cut:], "fsdp", down)
    sum_up = jnp.concatenate([sum_up, jnp.zeros_like(sum_up)])
    sum_down = jnp.concatenate([jnp.zeros_like(sum_down), sum_down])
    for step in range(far - 1, 0, -1):
        sum_up = lax.ppermute((terms(step) + sum_up.astype(F32)).astype(BF16), "fsdp", up)
        sum_down = lax.ppermute((terms(-step) + sum_down.astype(F32)).astype(BF16), "fsdp", down)
    grad_rows = (terms(0) + sum_up.astype(F32) + sum_down.astype(F32)).astype(BF16)

    new_global, new_momentum = outer_step(local_shard, global_weights, momentum)
    kv_rows, grad_in = products(inputs_here, cotangent, blocks)
    return kv_rows[None], grad_in[None], grad_rows[None], new_global, new_momentum


def solution(mesh):
    placed = (
        P("replica", "fsdp", None),
        P("fsdp", None),
        P("fsdp", "replica"),
        P("replica", "fsdp", None),
        P("replica", "fsdp", None),
    )
    return jax.shard_map(
        per_device,
        mesh=mesh,
        in_specs=placed,
        out_specs=(
            P("replica", "fsdp", None),
            P("replica", "fsdp", None),
            P("replica", "fsdp", None),
            P("fsdp", None),
            P("fsdp", "replica"),
        ),
        check_vma=False,
    )
```

```python
import functools

import jax
import jax.numpy as jnp
from jax import lax
from jax.experimental import pallas as pl
from jax.experimental.pallas import tpu as pltpu
from jax.sharding import PartitionSpec as P

BLOCK = 64

outer_rate = 0.7
outer_momentum = 0.9
scale_epsilon = 1e-06

F32 = jnp.float32
BF16 = jnp.bfloat16
LANES = 128
ROWS_BYTES = 8 * 2**20


def ring_order(size):
    return list(range(0, size, 2)) + list(range(1, size, 2))[::-1]


def ring_place(index, size):
    return jnp.where((index & 1) == 0, index >> 1, size - 1 - (index >> 1))


def ring_index(place, size):
    place = lax.rem(place + size, size)
    evens = (size + 1) // 2
    return jnp.where(place < evens, 2 * place, 2 * (size - 1 - place) + 1)


def block_start(offset, size, depth):
    start = ring_index(ring_place(lax.axis_index("fsdp"), size) + offset, size) * depth
    return pl.multiple_of(start, depth)


def vmem_call(kernel, out_shape, operands, flops, name, after=(), moved=None):
    def body(*refs):
        kernel(*refs[: len(operands)], *refs[len(operands) + len(after) :])

    moved = moved or sum(x.size * x.dtype.itemsize for x in operands)
    whole = pl.BlockSpec(memory_space=pltpu.VMEM)
    return pl.pallas_call(
        body,
        out_shape=out_shape,
        in_specs=[whole] * len(operands) + [pl.BlockSpec(memory_space=pl.ANY)] * len(after),
        out_specs=jax.tree.map(lambda _: whole, out_shape),
        compiler_params=pltpu.CompilerParams(vmem_limit_bytes=32 * 2**20),
        cost_estimate=pl.CostEstimate(flops=flops, bytes_accessed=moved, transcendentals=0),
        name=name,
    )(*operands, *after)


def shape_of(rows, columns, dtype):
    return jax.ShapeDtypeStruct((rows, columns), dtype)


def outer_kernel(replicas, share_cols, *refs):
    local_refs = refs[:replicas]
    global_ref, momentum_ref, share_ref, new_momentum_ref = refs[replicas:]
    rows, window = global_ref.shape
    old = global_ref[...].astype(F32)
    lane = lax.broadcasted_iota(jnp.int32, (rows, window), 1) // BLOCK
    total = jnp.zeros((rows, window), F32)
    for local_ref in local_refs:
        drift = old - local_ref[...].astype(F32)
        size = jnp.abs(drift)
        scale = jnp.zeros((rows, window), F32)
        for block in range(window // BLOCK):
            top = jnp.max(jnp.where(lane == block, size, 0.0), axis=1, keepdims=True)
            top = (top + scale_epsilon).astype(BF16).astype(F32)
            scale = jnp.where(lane == block, top, scale)
        total = total + (drift / scale).astype(BF16).astype(F32) * scale
    mean_grad = total / replicas
    shares = window // share_cols
    mean_here, old_here = mean_grad[:, :share_cols], old[:, :share_cols]
    mine = lax.axis_index("replica") % shares
    for share in range(1, shares):
        columns = slice(share * share_cols, (share + 1) * share_cols)
        mean_here = jnp.where(mine == share, mean_grad[:, columns], mean_here)
        old_here = jnp.where(mine == share, old[:, columns], old_here)
    new_momentum = outer_momentum * momentum_ref[...] + mean_here
    new_momentum_ref[...] = new_momentum
    share_ref[...] = (old_here - outer_rate * (mean_here + outer_momentum * new_momentum)).astype(BF16)


def join_kernel(*refs):
    *share_refs, out_ref = refs
    me = lax.axis_index("replica")
    count = len(share_refs)
    width = out_ref.shape[1] // count
    if width % LANES == 0:
        for bits, share_ref in enumerate(share_refs):
            out_ref[:, pl.ds(pl.multiple_of((me ^ bits) * width, width), width)] = share_ref[...]
        return
    pieces = [ref[...] for ref in share_refs]
    bit = 1
    while bit < count:
        odd = (me & bit) != 0
        pieces = [jnp.where(odd, pieces[at ^ bit], pieces[at]) for at in range(count)]
        bit *= 2
    for at in range(count):
        out_ref[:, at * width : (at + 1) * width] = pieces[at]


def windows_kernel(width, array_ref, *out_refs):
    me = lax.axis_index("replica")
    for bits, out_ref in enumerate(out_refs, 1):
        out_ref[...] = array_ref[:, pl.ds(pl.multiple_of((me ^ bits) * width, width), width)]


def swap(array, bits):
    return lax.ppermute(array, "replica", [(at, at ^ bits) for at in range(lax.axis_size("replica"))])


def send_windows(local_shard, after):
    rows, kv_width = local_shard.shape
    replicas = lax.axis_size("replica")
    me = lax.axis_index("replica")
    share_cols = kv_width // replicas
    window = max(share_cols, BLOCK)

    def window_of(owner):
        return lax.dynamic_slice_in_dim(local_shard, owner * share_cols // window * window, window, 1)

    if window == share_cols and window % LANES == 0:
        leaving = vmem_call(
            functools.partial(windows_kernel, window),
            [shape_of(rows, window, BF16)] * (replicas - 1),
            [local_shard],
            rows * kv_width,
            "outer_windows",
            after,
        )
    else:
        leaving = [window_of(me ^ bits) for bits in range(1, replicas)]
    return [window_of(me)] + [swap(array, bits) for bits, array in enumerate(leaving, 1)]


def update_share(windows, global_weights, momentum, after):
    rows, share_cols = momentum.shape
    replicas = len(windows)
    window = windows[0].shape[1]
    start = lax.axis_index("replica") * share_cols // window * window
    new_share, new_momentum = vmem_call(
        functools.partial(outer_kernel, replicas, share_cols),
        (shape_of(rows, share_cols, BF16), shape_of(rows, share_cols, F32)),
        windows + [lax.dynamic_slice_in_dim(global_weights, start, window, 1), momentum],
        20 * replicas * rows * window,
        "outer_update",
        after,
    )
    return [new_share] + [swap(new_share, bits) for bits in range(1, replicas)], new_momentum


def rows_kernel(size, offsets, inputs_ref, *refs):
    *block_refs, total_ref = refs
    depth = inputs_ref.shape[1] // size
    total = jnp.zeros(total_ref.shape, F32)
    if len(block_refs) > len(offsets):
        total = block_refs.pop()[...]
    for offset, block_ref in zip(offsets, block_refs):
        columns = pl.ds(block_start(offset, size, depth), depth)
        total = total + jnp.dot(inputs_ref[:, columns], block_ref[...], preferred_element_type=F32)
    total_ref[...] = total


def grads_kernel(size, offsets, cotangent_ref, *refs):
    *block_refs, grad_ref = refs
    depth = grad_ref.shape[1] // size
    for offset, block_ref in zip(offsets, block_refs):
        grad_ref[:, pl.ds(block_start(offset, size, depth), depth)] = lax.dot_general(
            cotangent_ref[...], block_ref[...], (((1,), (1,)), ((), ())), preferred_element_type=F32
        ).astype(BF16)


def last_products_kernel(at_ref, inputs_ref, cotangent_ref, total_ref, upper_ref, lower_ref, _, rows_ref, grad_ref):
    cut = upper_ref.shape[0]
    upper, lower = upper_ref[...], lower_ref[...]
    rows_ref[...] = (
        total_ref[...]
        + jnp.dot(inputs_ref[:, :cut], upper, preferred_element_type=F32)
        + jnp.dot(inputs_ref[:, cut:], lower, preferred_element_type=F32)
    ).astype(BF16)
    for columns, half in ((slice(0, cut), upper), (slice(cut, 2 * cut), lower)):
        grad_ref[:, columns] = lax.dot_general(
            cotangent_ref[...], half, (((1,), (1,)), ((), ())), preferred_element_type=F32
        ).astype(BF16)


def add_rows(inputs_here, blocks, total, size, after):
    tokens, width = inputs_here.shape
    kv_width = blocks[max(blocks)].shape[1]
    operands = [inputs_here] + list(blocks.values()) + ([] if total is None else [total])
    return vmem_call(
        functools.partial(rows_kernel, size, list(blocks)),
        shape_of(tokens, kv_width, F32),
        operands,
        2 * tokens * width // size * len(blocks) * kv_width,
        "add_rows",
        after,
        ROWS_BYTES,
    )


def near_grads(cotangent, blocks, width, size, after):
    tokens, kv_width = cotangent.shape
    return vmem_call(
        functools.partial(grads_kernel, size, list(blocks)),
        shape_of(tokens, width, BF16),
        [cotangent] + list(blocks.values()),
        2 * tokens * width * kv_width,
        "near_grads",
        after,
    )


def last_products(inputs_here, cotangent, total, grad, upper, lower, size):
    tokens, width = inputs_here.shape
    kv_width = cotangent.shape[1]
    depth = width // size
    at = ring_index(ring_place(lax.axis_index("fsdp"), size) + size // 2, size)
    chosen = pl.BlockSpec((tokens, depth), lambda step, at_ref: (0, at_ref[0]))

    def fixed(array):
        return pl.BlockSpec(array.shape, lambda step, at_ref: (0, 0))

    return pl.pallas_call(
        last_products_kernel,
        out_shape=(shape_of(tokens, kv_width, BF16), shape_of(tokens, width, BF16)),
        grid_spec=pltpu.PrefetchScalarGridSpec(
            num_scalar_prefetch=1,
            grid=(1,),
            in_specs=[chosen, fixed(cotangent), fixed(total), fixed(upper), fixed(lower)]
            + [pl.BlockSpec(memory_space=pl.ANY)],
            out_specs=(fixed(total), chosen),
        ),
        input_output_aliases={6: 1},
        compiler_params=pltpu.CompilerParams(vmem_limit_bytes=32 * 2**20),
        cost_estimate=pl.CostEstimate(
            flops=4 * tokens * depth * kv_width, bytes_accessed=6 * tokens * kv_width, transcendentals=0
        ),
        name="last_products",
    )(at.reshape(1).astype(jnp.int32), inputs_here, cotangent, total, upper, lower, grad)


def all_products(inputs_here, cotangent, blocks, size):
    depth, kv_width = blocks[0].shape
    place = ring_place(lax.axis_index("fsdp"), size)
    gathered = jnp.zeros((depth * size, kv_width), BF16)
    for offset, block in blocks.items():
        gathered = lax.dynamic_update_slice_in_dim(gathered, block, ring_index(place + offset, size) * depth, 0)
    rows = jnp.dot(inputs_here, gathered, preferred_element_type=F32).astype(BF16)
    grad = lax.dot_general(cotangent, gathered, (((1,), (1,)), ((), ())), preferred_element_type=F32)
    return rows, grad.astype(BF16)


def terms_kernel(size, offsets, token_weight, inputs_ref, cotangent_ref, *out_refs):
    depth = inputs_ref.shape[1] // size
    at = 0
    for offset in offsets:
        columns = inputs_ref[:, pl.ds(block_start(offset, size, depth), depth)]
        terms = (
            lax.dot_general(columns, cotangent_ref[...], (((0,), (0,)), ((), ())), preferred_element_type=F32)
            * token_weight
        )
        filled = 0
        while filled < depth:
            count = out_refs[at].shape[0]
            out_refs[at][...] = terms[filled : filled + count].astype(out_refs[at].dtype)
            filled += count
            at += 1


def token_terms(inputs_here, cotangent, size, offsets, out_shape, token_weight, name):
    tokens, width = inputs_here.shape
    kv_width = cotangent.shape[1]
    depth = width // size
    if depth % LANES == 0:
        return vmem_call(
            functools.partial(terms_kernel, size, offsets, token_weight),
            out_shape,
            [inputs_here, cotangent],
            2 * tokens * depth * len(offsets) * kv_width,
            name,
        )
    place = ring_place(lax.axis_index("fsdp"), size)
    out = []
    for offset in offsets:
        columns = lax.dynamic_slice_in_dim(inputs_here, ring_index(place + offset, size) * depth, depth, 1)
        terms = (
            lax.dot_general(columns, cotangent, (((0,), (0,)), ((), ())), preferred_element_type=F32) * token_weight
        )
        filled = 0
        while filled < depth:
            like = out_shape[len(out)]
            out.append(terms[filled : filled + like.shape[0]].astype(like.dtype))
            filled += like.shape[0]
    return out


def add_kernel(up_terms_ref, down_terms_ref, up_ref, down_ref, up_out, down_out):
    depth = up_terms_ref.shape[0]
    count = up_ref.shape[0]
    up_out[:count] = (up_terms_ref[:count] + up_ref[...].astype(F32)).astype(BF16)
    down_out[depth - count :] = (down_terms_ref[depth - count :] + down_ref[...].astype(F32)).astype(BF16)
    if count < depth:
        up_out[count:] = up_terms_ref[count:].astype(BF16)
        down_out[: depth - count] = down_terms_ref[: depth - count].astype(BF16)


def end_kernel(terms_ref, up_ref, down_ref, out_ref):
    count = up_ref.shape[0]
    if count == terms_ref.shape[0]:
        out_ref[...] = (terms_ref[...] + up_ref[...].astype(F32) + down_ref[...].astype(F32)).astype(BF16)
    else:
        out_ref[:count] = (terms_ref[:count] + up_ref[...].astype(F32)).astype(BF16)
        out_ref[count:] = (terms_ref[count:] + down_ref[...].astype(F32)).astype(BF16)


def per_device(local_weights, global_weights, momentum, activations, kv_cotangent):
    local_shard = local_weights[0]
    inputs_here = activations[0]
    cotangent = kv_cotangent[0]
    depth, kv_width = local_shard.shape
    size = lax.axis_size("fsdp")
    token_weight = 1.0 / (inputs_here.shape[0] * size)
    order = ring_order(size)
    up = [(order[at], order[(at + 1) % size]) for at in range(size)]
    down = [(target, source) for source, target in up]
    far = size // 2
    cut = depth // 2
    whole, half = shape_of(depth, kv_width, F32), shape_of(cut, kv_width, BF16)

    blocks = {0: local_shard}
    from_below, from_above = lax.ppermute(local_shard, "fsdp", up), lax.ppermute(local_shard, "fsdp", down)
    farthest = token_terms(inputs_here, cotangent, size, [far], [half, half], token_weight, "farthest_terms")
    sum_up, sum_down = lax.ppermute(farthest[0], "fsdp", up), lax.ppermute(farthest[1], "fsdp", down)
    offsets = [sign * step for step in range(far - 1, 0, -1) for sign in (1, -1)] + [0]
    terms = token_terms(inputs_here, cotangent, size, offsets, [whole] * len(offsets), token_weight, "near_terms")
    terms = dict(zip(offsets, terms))
    wide = depth % (2 * LANES) == 0
    total = None
    sums = []
    for step in range(1, far):
        blocks[-step], blocks[step] = from_below, from_above
        near = far - step
        after = (from_below, from_above)
        if wide:
            news = {at: blocks[at] for at in ((0, -1, 1) if step == 1 else (-step, step))}
            total = add_rows(inputs_here, news, total, size, (shares[0],) if step == far - 1 else ())
            after = (total,)
        sums.append(
            vmem_call(
                add_kernel,
                [shape_of(depth, kv_width, BF16)] * 2,
                [terms[near], terms[-near], sum_up, sum_down],
                2 * depth * kv_width,
                "add_terms",
                after,
            )
        )
        if step < far - 1:
            from_below, from_above = lax.ppermute(from_below, "fsdp", up), lax.ppermute(from_above, "fsdp", down)
        else:
            from_below = lax.ppermute(from_below[:cut], "fsdp", up)
            from_above = lax.ppermute(from_above[cut:], "fsdp", down)
        sum_up, sum_down = lax.ppermute(sums[-1][0], "fsdp", up), lax.ppermute(sums[-1][1], "fsdp", down)
        if step == 1:
            windows = send_windows(local_shard, sums[-1])
        if step == min(2, far - 1):
            shares, new_momentum = update_share(windows, global_weights, momentum, sums[-1])
    grad_rows = vmem_call(
        end_kernel,
        shape_of(depth, kv_width, BF16),
        [terms[0], sum_up, sum_down],
        2 * depth * kv_width,
        "end_terms",
    )

    new_global = vmem_call(
        join_kernel, shape_of(depth, kv_width, BF16), shares, depth * kv_width, "join_shares", sums[-1]
    )

    if wide:
        grad = near_grads(cotangent, blocks, inputs_here.shape[1], size, sums[-1])
        kv_rows, grad_in = last_products(inputs_here, cotangent, total, grad, from_below, from_above, size)
    else:
        blocks[far] = jnp.concatenate([from_below, from_above])
        kv_rows, grad_in = all_products(inputs_here, cotangent, blocks, size)
    return kv_rows[None], grad_in[None], grad_rows[None], new_global, new_momentum


def solution(mesh):
    placed = (
        P("replica", "fsdp", None),
        P("fsdp", None),
        P("fsdp", "replica"),
        P("replica", "fsdp", None),
        P("replica", "fsdp", None),
    )
    return jax.shard_map(
        per_device,
        mesh=mesh,
        in_specs=placed,
        out_specs=(
            P("replica", "fsdp", None),
            P("replica", "fsdp", None),
            P("replica", "fsdp", None),
            P("fsdp", None),
            P("fsdp", "replica"),
        ),
        check_vma=False,
    )
```

```python
import functools

import jax
import jax.numpy as jnp
from jax import lax
from jax.experimental import pallas as pl
from jax.experimental.pallas import tpu as pltpu
from jax.sharding import PartitionSpec as P

BLOCK = 64

outer_rate = 0.7
outer_momentum = 0.9
scale_epsilon = 1e-06

F32 = jnp.float32
BF16 = jnp.bfloat16
LANES = 128
VMEM_BYTES = 8 * 2**20
PRODUCTS_BYTES = 8 * 2**20


def ring_order(size):
    return list(range(0, size, 2)) + list(range(1, size, 2))[::-1]


def ring_place(index, size):
    return jnp.where((index & 1) == 0, index >> 1, size - 1 - (index >> 1))


def ring_index(place, size):
    place = lax.rem(place + size, size)
    evens = (size + 1) // 2
    return jnp.where(place < evens, 2 * place, 2 * (size - 1 - place) + 1)


def block_start(offset, size, depth):
    start = ring_index(ring_place(lax.axis_index("fsdp"), size) + offset, size) * depth
    return pl.multiple_of(start, depth)


def vmem_call(kernel, out_shape, operands, flops, name, after=(), moved=None):
    def body(*refs):
        kernel(*refs[: len(operands)], *refs[len(operands) + len(after) :])

    moved = moved or sum(x.size * x.dtype.itemsize for x in operands)
    whole = pl.BlockSpec(memory_space=pltpu.VMEM)
    return pl.pallas_call(
        body,
        out_shape=out_shape,
        in_specs=[whole] * len(operands) + [pl.BlockSpec(memory_space=pl.ANY)] * len(after),
        out_specs=jax.tree.map(lambda _: whole, out_shape),
        compiler_params=pltpu.CompilerParams(vmem_limit_bytes=VMEM_BYTES),
        cost_estimate=pl.CostEstimate(flops=flops, bytes_accessed=moved, transcendentals=0),
        name=name,
    )(*operands, *after)


def shape_of(rows, columns, dtype):
    return jax.ShapeDtypeStruct((rows, columns), dtype)


def column_window(array, start, width):
    if isinstance(array, jax.Array):
        return lax.dynamic_slice_in_dim(array, start, width, array.ndim - 1)
    return array[..., pl.ds(pl.multiple_of(start, width), width)]


def outer_kernel(replicas, share_cols, *refs):
    *held_refs, global_ref, momentum_ref, share_ref, new_momentum_ref = refs
    rows, window = held_refs[-1].shape[-2:]
    me = lax.axis_index("replica")

    def windows_of(ref):
        here = me * share_cols // window * window % ref.shape[-1]
        return ref[...] if ref.shape[-1] == window else column_window(ref, here, window)

    old = windows_of(global_ref).astype(F32)
    lane = lax.broadcasted_iota(jnp.int32, (rows, window), 1) // BLOCK
    total = jnp.zeros((rows, window), F32)
    for held_ref in held_refs:
        held = windows_of(held_ref).astype(F32)
        for local in [held] if held.ndim == 2 else list(held):
            drift = old - local
            size = jnp.abs(drift)
            scale = jnp.zeros((rows, window), F32)
            for block in range(window // BLOCK):
                top = jnp.max(jnp.where(lane == block, size, 0.0), axis=1, keepdims=True)
                top = (top + scale_epsilon).astype(BF16).astype(F32)
                scale = jnp.where(lane == block, top, scale)
            total = total + (drift / scale).astype(BF16).astype(F32) * scale
    mean_grad = total / replicas
    shares = window // share_cols
    mean_here, old_here = mean_grad[:, :share_cols], old[:, :share_cols]
    mine = me % shares
    for share in range(1, shares):
        columns = slice(share * share_cols, (share + 1) * share_cols)
        mean_here = jnp.where(mine == share, mean_grad[:, columns], mean_here)
        old_here = jnp.where(mine == share, old[:, columns], old_here)
    new_momentum = outer_momentum * momentum_ref[...] + mean_here
    new_momentum_ref[...] = new_momentum
    share_ref[...] = (old_here - outer_rate * (mean_here + outer_momentum * new_momentum)).astype(BF16)


def swap(array, bits):
    return lax.ppermute(array, "replica", [(at, at ^ bits) for at in range(lax.axis_size("replica"))])


def partner_kernel(bits, share_cols, width, *refs):
    *held_refs, out_ref = refs
    start = (lax.axis_index("replica") ^ bits) * share_cols // width * width
    at = 0
    for held_ref in held_refs:
        part = column_window(held_ref, start % held_ref.shape[-1], width)
        count = 1 if part.ndim == 2 else part.shape[0]
        out_ref[at : at + count] = part.reshape((count,) + part.shape[-2:])
        at += count


def send_windows(held, bits, kv_width, after):
    replicas = lax.axis_size("replica")
    share_cols = kv_width // replicas
    width = max(bits * share_cols, BLOCK)
    rows = held[0].shape[-2]
    count = sum(1 if array.ndim == 2 else array.shape[0] for array in held)
    if width % LANES == 0:
        leaving = vmem_call(
            functools.partial(partner_kernel, bits, share_cols, width),
            jax.ShapeDtypeStruct((count, rows, width), BF16),
            held,
            0,
            "partner_columns",
            after,
        )
    else:
        start = (lax.axis_index("replica") ^ bits) * share_cols // width * width
        parts = [column_window(array, start % array.shape[-1], width).reshape(-1, rows, width) for array in held]
        leaving = jnp.concatenate(parts)
    return held + [swap(leaving, bits)]


def update_share(held, global_weights, momentum, after):
    rows, share_cols = momentum.shape
    replicas = lax.axis_size("replica")
    window = held[-1].shape[-1]
    if window % LANES:
        start = lax.axis_index("replica") * share_cols // window * window
        held = [column_window(array, start % array.shape[-1], window) for array in held]
        global_weights = column_window(global_weights, start, window)
    return vmem_call(
        functools.partial(outer_kernel, replicas, share_cols),
        (shape_of(rows, share_cols, BF16), shape_of(rows, share_cols, F32)),
        held + [global_weights, momentum],
        0,
        "outer_update",
        after,
    )


def join_kernel(bits, mine_ref, other_ref, out_ref):
    width = mine_ref.shape[1]
    first = (lax.axis_index("replica") & bits) == 0

    @pl.when(first)
    def _():
        out_ref[:, :width] = mine_ref[...]
        out_ref[:, width:] = other_ref[...]

    @pl.when(jnp.logical_not(first))
    def _():
        out_ref[:, :width] = other_ref[...]
        out_ref[:, width:] = mine_ref[...]


def join_shares(mine, bits, after):
    rows, width = mine.shape
    return vmem_call(
        functools.partial(join_kernel, bits),
        shape_of(rows, 2 * width, BF16),
        [mine, swap(mine, bits)],
        0,
        "join_shares",
        after,
    )


def distinct(arrays):
    found = []
    for array in arrays:
        if not any(array is other for other in found):
            found.append(array)
    return found


def positions(pieces, arrays):
    index = {id(array): at for at, array in enumerate(arrays)}
    return [(index[id(array)], row, place, half) for array, row, place, half in pieces]


def piece_columns(place, half, size, depth):
    cut = depth // 2
    return pl.ds(pl.multiple_of(block_start(place, size, depth) + half * cut, cut), cut)


def products_kernel(size, pieces, count, first, last, inputs_ref, cotangent_ref, *refs):
    piece_refs, refs = refs[:count], refs[count:]
    total_ref, refs = (None, refs) if first else (refs[0], refs[2:])
    rows_ref, grad_ref, mark_ref, held, sems = refs
    depth = inputs_ref.shape[1] // size
    copies = []
    for number, (at, row, place, half) in enumerate(pieces):
        piece = piece_refs[at][row : row + depth // 2]
        held[number] = lax.dot_general(
            cotangent_ref[...], piece, (((1,), (1,)), ((), ())), preferred_element_type=F32
        ).astype(BF16)
        columns = piece_columns(place, half, size, depth)
        copies.append(pltpu.make_async_copy(held.at[number], grad_ref.at[:, columns], sems.at[number]))
        copies[-1].start()
    total = jnp.zeros(rows_ref.shape, F32) if first else total_ref[...]
    for at, row, place, half in pieces:
        piece = piece_refs[at][row : row + depth // 2]
        columns = inputs_ref[:, piece_columns(place, half, size, depth)]
        total = total + jnp.dot(columns, piece, preferred_element_type=F32)
    rows_ref[...] = total.astype(rows_ref.dtype)
    mark_ref[...] = jnp.zeros_like(mark_ref)
    for copy in copies:
        copy.wait()


def products(inputs_here, cotangent, pieces, before, size, last=False):
    tokens, width = inputs_here.shape
    kv_width = cotangent.shape[1]
    depth = width // size
    arrays = distinct(array for array, *_ in pieces)
    first = before is None
    operands = [inputs_here, cotangent] + arrays + ([] if first else list(before[:2]))
    whole, anywhere = pl.BlockSpec(memory_space=pltpu.VMEM), pl.BlockSpec(memory_space=pl.ANY)
    return pl.pallas_call(
        functools.partial(products_kernel, size, positions(pieces, arrays), len(arrays), first, last),
        out_shape=(
            shape_of(tokens, kv_width, BF16 if last else F32),
            shape_of(tokens, width, BF16),
            shape_of(8, LANES, F32),
        ),
        in_specs=[whole] * (2 + len(arrays)) + ([] if first else [whole, anywhere]),
        out_specs=(whole, anywhere, whole),
        scratch_shapes=[
            pltpu.VMEM((len(pieces), tokens, depth // 2), BF16),
            pltpu.SemaphoreType.DMA((len(pieces),)),
        ],
        input_output_aliases={} if first else {len(operands) - 1: 1},
        compiler_params=pltpu.CompilerParams(vmem_limit_bytes=VMEM_BYTES),
        cost_estimate=pl.CostEstimate(
            flops=2 * tokens * depth * len(pieces) * kv_width, bytes_accessed=PRODUCTS_BYTES * (4 if last else 1), transcendentals=0
        ),
        name="last_products" if last else "products",
    )(*operands)


def all_products(inputs_here, cotangent, pieces, size):
    width = inputs_here.shape[1]
    depth = width // size
    here = ring_place(lax.axis_index("fsdp"), size)
    gathered = jnp.zeros((width, cotangent.shape[1]), BF16)
    for array, row, place, half in pieces:
        start = ring_index(here + place, size) * depth + half * (depth // 2)
        gathered = lax.dynamic_update_slice_in_dim(gathered, array[row : row + depth // 2], start, 0)
    rows = jnp.dot(inputs_here, gathered, preferred_element_type=F32).astype(BF16)
    grad = lax.dot_general(cotangent, gathered, (((1,), (1,)), ((), ())), preferred_element_type=F32)
    return rows, grad.astype(BF16)


def terms_kernel(size, offsets, token_weight, inputs_ref, cotangent_ref, *out_refs):
    depth = inputs_ref.shape[1] // size
    at = 0
    for offset in offsets:
        columns = inputs_ref[:, pl.ds(block_start(offset, size, depth), depth)]
        terms = (
            lax.dot_general(columns, cotangent_ref[...], (((0,), (0,)), ((), ())), preferred_element_type=F32)
            * token_weight
        )
        filled = 0
        while filled < depth:
            count = out_refs[at].shape[0]
            out_refs[at][...] = terms[filled : filled + count].astype(out_refs[at].dtype)
            filled += count
            at += 1


def token_terms(inputs_here, cotangent, size, offsets, out_shape, token_weight, name, after=()):
    tokens, width = inputs_here.shape
    kv_width = cotangent.shape[1]
    depth = width // size
    if depth % LANES == 0:
        return vmem_call(
            functools.partial(terms_kernel, size, offsets, token_weight),
            out_shape,
            [inputs_here, cotangent],
            2 * tokens * depth * len(offsets) * kv_width,
            name,
            after,
        )
    place = ring_place(lax.axis_index("fsdp"), size)
    out = []
    for offset in offsets:
        columns = lax.dynamic_slice_in_dim(inputs_here, ring_index(place + offset, size) * depth, depth, 1)
        terms = (
            lax.dot_general(columns, cotangent, (((0,), (0,)), ((), ())), preferred_element_type=F32) * token_weight
        )
        filled = 0
        while filled < depth:
            like = out_shape[len(out)]
            out.append(terms[filled : filled + like.shape[0]].astype(like.dtype))
            filled += like.shape[0]
    return out


def add_kernel(up_terms_ref, down_terms_ref, up_ref, down_ref, up_out, down_out):
    depth = up_terms_ref.shape[0]
    count = up_ref.shape[0]
    up_out[:count] = (up_terms_ref[:count] + up_ref[...].astype(F32)).astype(BF16)
    down_out[depth - count :] = (down_terms_ref[depth - count :] + down_ref[...].astype(F32)).astype(BF16)
    if count < depth:
        up_out[count:] = up_terms_ref[count:].astype(BF16)
        down_out[: depth - count] = down_terms_ref[: depth - count].astype(BF16)


def end_kernel(terms_ref, up_ref, down_ref, out_ref):
    count = up_ref.shape[0]
    if count == terms_ref.shape[0]:
        out_ref[...] = (terms_ref[...] + up_ref[...].astype(F32) + down_ref[...].astype(F32)).astype(BF16)
    else:
        out_ref[:count] = (terms_ref[:count] + up_ref[...].astype(F32)).astype(BF16)
        out_ref[count:] = (terms_ref[count:] + down_ref[...].astype(F32)).astype(BF16)


def per_device(local_weights, global_weights, momentum, activations, kv_cotangent):
    local_shard = local_weights[0]
    inputs_here = activations[0]
    cotangent = kv_cotangent[0]
    depth, kv_width = local_shard.shape
    size = lax.axis_size("fsdp")
    token_weight = 1.0 / (inputs_here.shape[0] * size)
    wide = depth % (2 * LANES) == 0
    order = ring_order(size)
    up = [(order[at], order[(at + 1) % size]) for at in range(size)]
    down = [(target, source) for source, target in up]
    far = size // 2
    cut = depth // 2
    whole, half = shape_of(depth, kv_width, F32), shape_of(cut, kv_width, BF16)

    from_below, from_above = lax.ppermute(local_shard, "fsdp", up), lax.ppermute(local_shard, "fsdp", down)
    farthest = token_terms(inputs_here, cotangent, size, [far], [half, half], token_weight, "farthest_terms")
    sum_up, sum_down = lax.ppermute(farthest[0], "fsdp", up), lax.ppermute(farthest[1], "fsdp", down)
    offsets = [sign * step for step in range(far - 1, 0, -1) for sign in (1, -1)] + [0]
    terms = [whole] * len(offsets)
    terms = token_terms(inputs_here, cotangent, size, offsets, terms, token_weight, "near_terms", farthest)
    terms = dict(zip(offsets, terms))

    bits = lax.axis_size("replica") // 2
    held = send_windows([local_shard], bits, kv_width, (terms[0],))
    pieces = [(local_shard, 0, 0, 0), (local_shard, cut, 0, 1)]
    made = None

    def around(step):
        return [
            (from_below, 0, -step, 0),
            (from_below, cut, 1 - step, 1),
            (from_above, 0, step - 1, 0),
            (from_above, cut, step, 1),
        ]

    for step in range(1, far):
        near = far - step
        if step == 1:
            latest = [
                (array, half * cut, place, half) for array, place in ((from_below, -1), (from_above, 1)) for half in (0, 1)
            ]
            upward, downward = from_below[:cut], from_above[cut:]
            behind_up, behind_down = from_below[cut:], from_above[:cut]
        elif step == 2:
            latest = [(from_below, 0, -2, 0), (from_above, 0, 2, 1)]
            upward, downward = jnp.concatenate([from_below, behind_up]), jnp.concatenate([behind_down, from_above])
        else:
            latest = around(step)
            upward, downward = from_below, from_above
        pieces += latest
        after = (from_below, from_above)
        if wide:
            made = products(inputs_here, cotangent, pieces if step == 1 else latest, made, size)
            after = (made[2],)
        if step == min(2, far - 1):
            new_share, new_momentum = update_share(held, global_weights, momentum, after)
            new_global = new_share
            after += (new_share,)
        elif step == min(3, far - 1):
            while new_global.shape[1] < kv_width // 2:
                new_global = join_shares(new_global, bits, after)
                bits *= 2
            after += (new_global,)
        sums = vmem_call(
            add_kernel,
            [shape_of(depth, kv_width, BF16)] * 2,
            [terms[near], terms[-near], sum_up, sum_down],
            0,
            "add_terms",
            after,
        )
        while step == 1 and bits > 1:
            bits //= 2
            held = send_windows(held, bits, kv_width, sums)
        from_below, from_above = lax.ppermute(upward, "fsdp", up), lax.ppermute(downward, "fsdp", down)
        sum_up, sum_down = lax.ppermute(sums[0], "fsdp", up), lax.ppermute(sums[1], "fsdp", down)
    latest = around(far)
    while new_global.shape[1] < kv_width:
        new_global = join_shares(new_global, bits, ())
        bits *= 2
    if wide:
        kv_rows, grad_in, mark = products(inputs_here, cotangent, latest, made, size, last=True)
        after = (mark,)
    else:
        kv_rows, grad_in = all_products(inputs_here, cotangent, pieces + latest, size)
        after = ()
    grad_rows = vmem_call(
        end_kernel,
        shape_of(depth, kv_width, BF16),
        [terms[0], sum_up, sum_down],
        0,
        "end_terms",
        after,
    )
    return kv_rows[None], grad_in[None], grad_rows[None], new_global, new_momentum


def solution(mesh):
    placed = (
        P("replica", "fsdp", None),
        P("fsdp", None),
        P("fsdp", "replica"),
        P("replica", "fsdp", None),
        P("replica", "fsdp", None),
    )
    return jax.shard_map(
        per_device,
        mesh=mesh,
        in_specs=placed,
        out_specs=(
            P("replica", "fsdp", None),
            P("replica", "fsdp", None),
            P("replica", "fsdp", None),
            P("fsdp", None),
            P("fsdp", "replica"),
        ),
        check_vma=False,
    )
```

```python
import functools

import jax
import jax.numpy as jnp
from jax import lax
from jax.experimental import pallas as pl
from jax.experimental.pallas import tpu as pltpu
from jax.sharding import PartitionSpec as P

BLOCK = 64

outer_rate = 0.7
outer_momentum = 0.9
scale_epsilon = 1e-06

F32 = jnp.float32
BF16 = jnp.bfloat16
LANES = 128
VMEM_BYTES = 8 * 2**20
PRODUCTS_BYTES = 8 * 2**20


def ring_order(size):
    return list(range(0, size, 2)) + list(range(1, size, 2))[::-1]


def ring_place(index, size):
    return jnp.where((index & 1) == 0, index >> 1, size - 1 - (index >> 1))


def ring_index(place, size):
    place = lax.rem(place + size, size)
    evens = (size + 1) // 2
    return jnp.where(place < evens, 2 * place, 2 * (size - 1 - place) + 1)


def block_start(offset, size, depth):
    start = ring_index(ring_place(lax.axis_index("fsdp"), size) + offset, size) * depth
    return pl.multiple_of(start, depth)


def vmem_call(kernel, out_shape, operands, flops, name, after=(), moved=None):
    def body(*refs):
        kernel(*refs[: len(operands)], *refs[len(operands) + len(after) :])

    moved = moved or sum(x.size * x.dtype.itemsize for x in operands)
    whole = pl.BlockSpec(memory_space=pltpu.VMEM)
    return pl.pallas_call(
        body,
        out_shape=out_shape,
        in_specs=[whole] * len(operands) + [pl.BlockSpec(memory_space=pl.ANY)] * len(after),
        out_specs=jax.tree.map(lambda _: whole, out_shape),
        compiler_params=pltpu.CompilerParams(vmem_limit_bytes=VMEM_BYTES),
        cost_estimate=pl.CostEstimate(flops=flops, bytes_accessed=moved, transcendentals=0),
        name=name,
    )(*operands, *after)


def shape_of(rows, columns, dtype):
    return jax.ShapeDtypeStruct((rows, columns), dtype)


def column_window(array, start, width):
    if isinstance(array, jax.Array):
        return lax.dynamic_slice_in_dim(array, start, width, array.ndim - 1)
    return array[..., pl.ds(pl.multiple_of(start, width), width)]


def outer_kernel(replicas, share_cols, *refs):
    *held_refs, global_ref, momentum_ref, share_ref, new_momentum_ref = refs
    rows, window = held_refs[-1].shape[-2:]
    me = lax.axis_index("replica")

    def windows_of(ref):
        here = me * share_cols // window * window % ref.shape[-1]
        return ref[...] if ref.shape[-1] == window else column_window(ref, here, window)

    old = windows_of(global_ref).astype(F32)
    lane = lax.broadcasted_iota(jnp.int32, (rows, window), 1) // BLOCK
    total = jnp.zeros((rows, window), F32)
    for held_ref in held_refs:
        held = windows_of(held_ref).astype(F32)
        for local in [held] if held.ndim == 2 else list(held):
            drift = old - local
            size = jnp.abs(drift)
            scale = jnp.zeros((rows, window), F32)
            for block in range(window // BLOCK):
                top = jnp.max(jnp.where(lane == block, size, 0.0), axis=1, keepdims=True)
                top = (top + scale_epsilon).astype(BF16).astype(F32)
                scale = jnp.where(lane == block, top, scale)
            total = total + (drift / scale).astype(BF16).astype(F32) * scale
    mean_grad = total / replicas
    shares = window // share_cols
    mean_here, old_here = mean_grad[:, :share_cols], old[:, :share_cols]
    mine = me % shares
    for share in range(1, shares):
        columns = slice(share * share_cols, (share + 1) * share_cols)
        mean_here = jnp.where(mine == share, mean_grad[:, columns], mean_here)
        old_here = jnp.where(mine == share, old[:, columns], old_here)
    new_momentum = outer_momentum * momentum_ref[...] + mean_here
    new_momentum_ref[...] = new_momentum
    share_ref[...] = (old_here - outer_rate * (mean_here + outer_momentum * new_momentum)).astype(BF16)


def swap(array, bits):
    return lax.ppermute(array, "replica", [(at, at ^ bits) for at in range(lax.axis_size("replica"))])


def partner_kernel(bits, share_cols, width, *refs):
    *held_refs, out_ref = refs
    start = (lax.axis_index("replica") ^ bits) * share_cols // width * width
    at = 0
    for held_ref in held_refs:
        part = column_window(held_ref, start % held_ref.shape[-1], width)
        count = 1 if part.ndim == 2 else part.shape[0]
        out_ref[at : at + count] = part.reshape((count,) + part.shape[-2:])
        at += count


def send_windows(held, bits, kv_width, after):
    replicas = lax.axis_size("replica")
    share_cols = kv_width // replicas
    width = max(bits * share_cols, BLOCK)
    rows = held[0].shape[-2]
    count = sum(1 if array.ndim == 2 else array.shape[0] for array in held)
    if width % LANES == 0:
        leaving = vmem_call(
            functools.partial(partner_kernel, bits, share_cols, width),
            jax.ShapeDtypeStruct((count, rows, width), BF16),
            held,
            0,
            "partner_columns",
            after,
        )
    else:
        start = (lax.axis_index("replica") ^ bits) * share_cols // width * width
        parts = [column_window(array, start % array.shape[-1], width).reshape(-1, rows, width) for array in held]
        leaving = jnp.concatenate(parts)
    return held + [swap(leaving, bits)]


def update_share(held, global_weights, momentum, after):
    rows, share_cols = momentum.shape
    replicas = lax.axis_size("replica")
    window = held[-1].shape[-1]
    if window % LANES:
        start = lax.axis_index("replica") * share_cols // window * window
        held = [column_window(array, start % array.shape[-1], window) for array in held]
        global_weights = column_window(global_weights, start, window)
    return vmem_call(
        functools.partial(outer_kernel, replicas, share_cols),
        (shape_of(rows, share_cols, BF16), shape_of(rows, share_cols, F32)),
        held + [global_weights, momentum],
        0,
        "outer_update",
        after,
    )


def join_kernel(places, *refs):
    *held_refs, out_ref = refs
    width = out_ref.shape[1] // len(places)
    me = lax.axis_index("replica")
    at = 0
    for held_ref in held_refs:
        for start in range(0, held_ref.shape[1], width):
            columns = pl.ds(pl.multiple_of((me ^ places[at]) * width, width), width)
            out_ref[:, columns] = held_ref[:, start : start + width]
            at += 1


def join_shares(held, places, kv_width, after):
    rows = held[0].shape[0]
    width = kv_width // len(places)
    if width % LANES == 0:
        return vmem_call(
            functools.partial(join_kernel, places), shape_of(rows, kv_width, BF16), held, 0, "join_shares", after
        )
    whole = jnp.concatenate(held, axis=1)
    joined = jnp.zeros_like(whole)
    for at, place in enumerate(places):
        start = (lax.axis_index("replica") ^ place) * width
        joined = lax.dynamic_update_slice_in_dim(joined, whole[:, at * width : (at + 1) * width], start, 1)
    return joined


def distinct(arrays):
    found = []
    for array in arrays:
        if not any(array is other for other in found):
            found.append(array)
    return found


def positions(pieces, arrays):
    index = {id(array): at for at, array in enumerate(arrays)}
    return [(index[id(array)], row, place, half) for array, row, place, half in pieces]


def piece_columns(place, half, size, depth):
    cut = depth // 2
    return pl.ds(pl.multiple_of(block_start(place, size, depth) + half * cut, cut), cut)


def products_kernel(size, pieces, count, first, last, inputs_ref, cotangent_ref, *refs):
    piece_refs, refs = refs[:count], refs[count:]
    total_ref, refs = (None, refs) if first else (refs[0], refs[2:])
    rows_ref, grad_ref, mark_ref, held, sems = refs
    depth = inputs_ref.shape[1] // size
    copies = []
    for number, (at, row, place, half) in enumerate(pieces):
        piece = piece_refs[at][row : row + depth // 2]
        held[number] = lax.dot_general(
            cotangent_ref[...], piece, (((1,), (1,)), ((), ())), preferred_element_type=F32
        ).astype(BF16)
        columns = piece_columns(place, half, size, depth)
        copies.append(pltpu.make_async_copy(held.at[number], grad_ref.at[:, columns], sems.at[number]))
        copies[-1].start()
    total = jnp.zeros(rows_ref.shape, F32) if first else total_ref[...]
    for at, row, place, half in pieces:
        piece = piece_refs[at][row : row + depth // 2]
        columns = inputs_ref[:, piece_columns(place, half, size, depth)]
        total = total + jnp.dot(columns, piece, preferred_element_type=F32)
    rows_ref[...] = total.astype(rows_ref.dtype)
    mark_ref[...] = jnp.zeros_like(mark_ref)
    for copy in copies:
        copy.wait()


def products(inputs_here, cotangent, pieces, before, size, last=False):
    tokens, width = inputs_here.shape
    kv_width = cotangent.shape[1]
    depth = width // size
    arrays = distinct(array for array, *_ in pieces)
    first = before is None
    operands = [inputs_here, cotangent] + arrays + ([] if first else list(before[:2]))
    whole, anywhere = pl.BlockSpec(memory_space=pltpu.VMEM), pl.BlockSpec(memory_space=pl.ANY)
    return pl.pallas_call(
        functools.partial(products_kernel, size, positions(pieces, arrays), len(arrays), first, last),
        out_shape=(
            shape_of(tokens, kv_width, BF16 if last else F32),
            shape_of(tokens, width, BF16),
            shape_of(8, LANES, F32),
        ),
        in_specs=[whole] * (2 + len(arrays)) + ([] if first else [whole, anywhere]),
        out_specs=(whole, anywhere, whole),
        scratch_shapes=[
            pltpu.VMEM((len(pieces), tokens, depth // 2), BF16),
            pltpu.SemaphoreType.DMA((len(pieces),)),
        ],
        input_output_aliases={} if first else {len(operands) - 1: 1},
        compiler_params=pltpu.CompilerParams(vmem_limit_bytes=VMEM_BYTES),
        cost_estimate=pl.CostEstimate(
            flops=2 * tokens * depth * len(pieces) * kv_width, bytes_accessed=PRODUCTS_BYTES * (4 if last else 1), transcendentals=0
        ),
        name="last_products" if last else "products",
    )(*operands)


def all_products(inputs_here, cotangent, pieces, size):
    width = inputs_here.shape[1]
    depth = width // size
    here = ring_place(lax.axis_index("fsdp"), size)
    gathered = jnp.zeros((width, cotangent.shape[1]), BF16)
    for array, row, place, half in pieces:
        start = ring_index(here + place, size) * depth + half * (depth // 2)
        gathered = lax.dynamic_update_slice_in_dim(gathered, array[row : row + depth // 2], start, 0)
    rows = jnp.dot(inputs_here, gathered, preferred_element_type=F32).astype(BF16)
    grad = lax.dot_general(cotangent, gathered, (((1,), (1,)), ((), ())), preferred_element_type=F32)
    return rows, grad.astype(BF16)


def terms_kernel(size, offsets, token_weight, inputs_ref, cotangent_ref, *out_refs):
    depth = inputs_ref.shape[1] // size
    at = 0
    for offset in offsets:
        columns = inputs_ref[:, pl.ds(block_start(offset, size, depth), depth)]
        terms = (
            lax.dot_general(columns, cotangent_ref[...], (((0,), (0,)), ((), ())), preferred_element_type=F32)
            * token_weight
        )
        filled = 0
        while filled < depth:
            count = out_refs[at].shape[0]
            out_refs[at][...] = terms[filled : filled + count].astype(out_refs[at].dtype)
            filled += count
            at += 1


def token_terms(inputs_here, cotangent, size, offsets, out_shape, token_weight, name, after=()):
    tokens, width = inputs_here.shape
    kv_width = cotangent.shape[1]
    depth = width // size
    if depth % LANES == 0:
        return vmem_call(
            functools.partial(terms_kernel, size, offsets, token_weight),
            out_shape,
            [inputs_here, cotangent],
            2 * tokens * depth * len(offsets) * kv_width,
            name,
            after,
        )
    place = ring_place(lax.axis_index("fsdp"), size)
    out = []
    for offset in offsets:
        columns = lax.dynamic_slice_in_dim(inputs_here, ring_index(place + offset, size) * depth, depth, 1)
        terms = (
            lax.dot_general(columns, cotangent, (((0,), (0,)), ((), ())), preferred_element_type=F32) * token_weight
        )
        filled = 0
        while filled < depth:
            like = out_shape[len(out)]
            out.append(terms[filled : filled + like.shape[0]].astype(like.dtype))
            filled += like.shape[0]
    return out


def add_kernel(up_terms_ref, down_terms_ref, up_ref, down_ref, up_out, down_out):
    depth = up_terms_ref.shape[0]
    count = up_ref.shape[0]
    up_out[:count] = (up_terms_ref[:count] + up_ref[...].astype(F32)).astype(BF16)
    down_out[depth - count :] = (down_terms_ref[depth - count :] + down_ref[...].astype(F32)).astype(BF16)
    if count < depth:
        up_out[count:] = up_terms_ref[count:].astype(BF16)
        down_out[: depth - count] = down_terms_ref[: depth - count].astype(BF16)


def end_kernel(terms_ref, up_ref, down_ref, out_ref):
    count = up_ref.shape[0]
    if count == terms_ref.shape[0]:
        out_ref[...] = (terms_ref[...] + up_ref[...].astype(F32) + down_ref[...].astype(F32)).astype(BF16)
    else:
        out_ref[:count] = (terms_ref[:count] + up_ref[...].astype(F32)).astype(BF16)
        out_ref[count:] = (terms_ref[count:] + down_ref[...].astype(F32)).astype(BF16)


def per_device(local_weights, global_weights, momentum, activations, kv_cotangent):
    local_shard = local_weights[0]
    inputs_here = activations[0]
    cotangent = kv_cotangent[0]
    depth, kv_width = local_shard.shape
    size = lax.axis_size("fsdp")
    token_weight = 1.0 / (inputs_here.shape[0] * size)
    wide = depth % (2 * LANES) == 0
    order = ring_order(size)
    up = [(order[at], order[(at + 1) % size]) for at in range(size)]
    down = [(target, source) for source, target in up]
    far = size // 2
    cut = depth // 2
    whole, half = shape_of(depth, kv_width, F32), shape_of(cut, kv_width, BF16)

    from_below, from_above = lax.ppermute(local_shard, "fsdp", up), lax.ppermute(local_shard, "fsdp", down)
    farthest = token_terms(inputs_here, cotangent, size, [far], [half, half], token_weight, "farthest_terms")
    sum_up, sum_down = lax.ppermute(farthest[0], "fsdp", up), lax.ppermute(farthest[1], "fsdp", down)
    offsets = [sign * step for step in range(far - 1, 0, -1) for sign in (1, -1)] + [0]
    terms = [whole] * len(offsets)
    terms = token_terms(inputs_here, cotangent, size, offsets, terms, token_weight, "near_terms", farthest)
    terms = dict(zip(offsets, terms))

    bits = lax.axis_size("replica") // 2
    held = send_windows([local_shard], bits, kv_width, (terms[0],))
    pieces = [(local_shard, 0, 0, 0), (local_shard, cut, 0, 1)]
    made = None

    def around(step):
        return [
            (from_below, 0, -step, 0),
            (from_below, cut, 1 - step, 1),
            (from_above, 0, step - 1, 0),
            (from_above, cut, step, 1),
        ]

    for step in range(1, far):
        near = far - step
        if step == 1:
            latest = [
                (array, half * cut, place, half) for array, place in ((from_below, -1), (from_above, 1)) for half in (0, 1)
            ]
            upward, downward = from_below[:cut], from_above[cut:]
            behind_up, behind_down = from_below[cut:], from_above[:cut]
        elif step == 2:
            latest = [(from_below, 0, -2, 0), (from_above, 0, 2, 1)]
            upward, downward = jnp.concatenate([from_below, behind_up]), jnp.concatenate([behind_down, from_above])
        else:
            latest = around(step)
            upward, downward = from_below, from_above
        pieces += latest
        after = (from_below, from_above)
        if wide:
            made = products(inputs_here, cotangent, pieces if step == 1 else latest, made, size)
            after = (made[2],)
        if step == min(2, far - 1):
            new_share, new_momentum = update_share(held, global_weights, momentum, after)
            after += (new_share,)
            bits = lax.axis_size("replica") // 2
            shares, places = [new_share, swap(new_share, bits)], [0, bits]
        elif step == min(3, far - 1):
            while bits > 1:
                bits //= 2
                shares = [jnp.concatenate(shares, axis=1)]
                after += (shares[0],)
                shares.append(swap(shares[0], bits))
                places += [place ^ bits for place in places]
        sums = vmem_call(
            add_kernel,
            [shape_of(depth, kv_width, BF16)] * 2,
            [terms[near], terms[-near], sum_up, sum_down],
            0,
            "add_terms",
            after,
        )
        while step == 1 and bits > 1:
            bits //= 2
            held = send_windows(held, bits, kv_width, sums)
        from_below, from_above = lax.ppermute(upward, "fsdp", up), lax.ppermute(downward, "fsdp", down)
        sum_up, sum_down = lax.ppermute(sums[0], "fsdp", up), lax.ppermute(sums[1], "fsdp", down)
    latest = around(far)
    if wide:
        kv_rows, grad_in, mark = products(inputs_here, cotangent, latest, made, size, last=True)
        after = (mark,)
    else:
        kv_rows, grad_in = all_products(inputs_here, cotangent, pieces + latest, size)
        after = ()
    new_global = join_shares(shares, places, kv_width, after)
    grad_rows = vmem_call(
        end_kernel,
        shape_of(depth, kv_width, BF16),
        [terms[0], sum_up, sum_down],
        0,
        "end_terms",
        after,
    )
    return kv_rows[None], grad_in[None], grad_rows[None], new_global, new_momentum


def solution(mesh):
    placed = (
        P("replica", "fsdp", None),
        P("fsdp", None),
        P("fsdp", "replica"),
        P("replica", "fsdp", None),
        P("replica", "fsdp", None),
    )
    return jax.shard_map(
        per_device,
        mesh=mesh,
        in_specs=placed,
        out_specs=(
            P("replica", "fsdp", None),
            P("replica", "fsdp", None),
            P("replica", "fsdp", None),
            P("fsdp", None),
            P("fsdp", "replica"),
        ),
        check_vma=False,
    )
```

```python
import functools

import jax
import jax.numpy as jnp
from jax import lax
from jax.experimental import pallas as pl
from jax.experimental.pallas import tpu as pltpu
from jax.sharding import PartitionSpec as P

BLOCK = 64

outer_rate = 0.7
outer_momentum = 0.9
scale_epsilon = 1e-06

F32 = jnp.float32
BF16 = jnp.bfloat16
LANES = 128
VMEM_BYTES = 8 * 2**20
PRODUCTS_BYTES = 8 * 2**20


def ring_order(size):
    return list(range(0, size, 2)) + list(range(1, size, 2))[::-1]


def ring_place(index, size):
    return jnp.where((index & 1) == 0, index >> 1, size - 1 - (index >> 1))


def ring_index(place, size):
    place = lax.rem(place + size, size)
    evens = (size + 1) // 2
    return jnp.where(place < evens, 2 * place, 2 * (size - 1 - place) + 1)


def block_start(offset, size, depth):
    start = ring_index(ring_place(lax.axis_index("fsdp"), size) + offset, size) * depth
    return pl.multiple_of(start, depth)


def vmem_call(kernel, out_shape, operands, flops, name, after=(), moved=None):
    def body(*refs):
        kernel(*refs[: len(operands)], *refs[len(operands) + len(after) :])

    moved = moved or sum(x.size * x.dtype.itemsize for x in operands)
    whole = pl.BlockSpec(memory_space=pltpu.VMEM)
    return pl.pallas_call(
        body,
        out_shape=out_shape,
        in_specs=[whole] * len(operands) + [pl.BlockSpec(memory_space=pl.ANY)] * len(after),
        out_specs=jax.tree.map(lambda _: whole, out_shape),
        compiler_params=pltpu.CompilerParams(vmem_limit_bytes=VMEM_BYTES),
        cost_estimate=pl.CostEstimate(flops=flops, bytes_accessed=moved, transcendentals=0),
        name=name,
    )(*operands, *after)


def shape_of(rows, columns, dtype):
    return jax.ShapeDtypeStruct((rows, columns), dtype)


def column_window(array, start, width):
    if isinstance(array, jax.Array):
        return lax.dynamic_slice_in_dim(array, start, width, array.ndim - 1)
    return array[..., pl.ds(pl.multiple_of(start, width), width)]


def outer_kernel(replicas, share_cols, *refs):
    *held_refs, global_ref, momentum_ref, share_ref, new_momentum_ref = refs
    rows, window = held_refs[-1].shape[-2:]
    me = lax.axis_index("replica")

    def windows_of(ref):
        here = me * share_cols // window * window % ref.shape[-1]
        return ref[...] if ref.shape[-1] == window else column_window(ref, here, window)

    old = windows_of(global_ref).astype(F32)
    lane = lax.broadcasted_iota(jnp.int32, (rows, window), 1) // BLOCK
    total = jnp.zeros((rows, window), F32)
    for held_ref in held_refs:
        held = windows_of(held_ref).astype(F32)
        for local in [held] if held.ndim == 2 else list(held):
            drift = old - local
            size = jnp.abs(drift)
            scale = jnp.zeros((rows, window), F32)
            for block in range(window // BLOCK):
                top = jnp.max(jnp.where(lane == block, size, 0.0), axis=1, keepdims=True)
                top = (top + scale_epsilon).astype(BF16).astype(F32)
                scale = jnp.where(lane == block, top, scale)
            total = total + (drift / scale).astype(BF16).astype(F32) * scale
    mean_grad = total / replicas
    shares = window // share_cols
    mean_here, old_here = mean_grad[:, :share_cols], old[:, :share_cols]
    mine = me % shares
    for share in range(1, shares):
        columns = slice(share * share_cols, (share + 1) * share_cols)
        mean_here = jnp.where(mine == share, mean_grad[:, columns], mean_here)
        old_here = jnp.where(mine == share, old[:, columns], old_here)
    new_momentum = outer_momentum * momentum_ref[...] + mean_here
    new_momentum_ref[...] = new_momentum
    share_ref[...] = (old_here - outer_rate * (mean_here + outer_momentum * new_momentum)).astype(BF16)


def swap(array, bits):
    return lax.ppermute(array, "replica", [(at, at ^ bits) for at in range(lax.axis_size("replica"))])


def partner_kernel(bits, share_cols, width, *refs):
    *held_refs, out_ref = refs
    start = (lax.axis_index("replica") ^ bits) * share_cols // width * width
    at = 0
    for held_ref in held_refs:
        part = column_window(held_ref, start % held_ref.shape[-1], width)
        count = 1 if part.ndim == 2 else part.shape[0]
        out_ref[at : at + count] = part.reshape((count,) + part.shape[-2:])
        at += count


def send_windows(held, bits, kv_width, after):
    replicas = lax.axis_size("replica")
    share_cols = kv_width // replicas
    width = max(bits * share_cols, BLOCK)
    rows = held[0].shape[-2]
    count = sum(1 if array.ndim == 2 else array.shape[0] for array in held)
    if width % LANES == 0:
        leaving = vmem_call(
            functools.partial(partner_kernel, bits, share_cols, width),
            jax.ShapeDtypeStruct((count, rows, width), BF16),
            held,
            0,
            "partner_columns",
            after,
        )
    else:
        start = (lax.axis_index("replica") ^ bits) * share_cols // width * width
        parts = [column_window(array, start % array.shape[-1], width).reshape(-1, rows, width) for array in held]
        leaving = jnp.concatenate(parts)
    return held + [swap(leaving, bits)]


def update_share(held, global_weights, momentum, after):
    rows, share_cols = momentum.shape
    replicas = lax.axis_size("replica")
    window = held[-1].shape[-1]
    if window % LANES:
        start = lax.axis_index("replica") * share_cols // window * window
        held = [column_window(array, start % array.shape[-1], window) for array in held]
        global_weights = column_window(global_weights, start, window)
    return vmem_call(
        functools.partial(outer_kernel, replicas, share_cols),
        (shape_of(rows, share_cols, BF16), shape_of(rows, share_cols, F32)),
        held + [global_weights, momentum],
        0,
        "outer_update",
        after,
    )


def join_kernel(places, *refs):
    *held_refs, out_ref = refs
    width = out_ref.shape[1] // len(places)
    me = lax.axis_index("replica")
    at = 0
    for held_ref in held_refs:
        for start in range(0, held_ref.shape[1], width):
            columns = pl.ds(pl.multiple_of((me ^ places[at]) * width, width), width)
            out_ref[:, columns] = held_ref[:, start : start + width]
            at += 1


def join_shares(held, places, kv_width, after):
    rows = held[0].shape[0]
    width = kv_width // len(places)
    if width % LANES == 0:
        return vmem_call(
            functools.partial(join_kernel, places), shape_of(rows, kv_width, BF16), held, 0, "join_shares", after
        )
    whole = jnp.concatenate(held, axis=1)
    joined = jnp.zeros_like(whole)
    for at, place in enumerate(places):
        start = (lax.axis_index("replica") ^ place) * width
        joined = lax.dynamic_update_slice_in_dim(joined, whole[:, at * width : (at + 1) * width], start, 1)
    return joined


def products_kernel(size, places, first, inputs_ref, cotangent_ref, *refs):
    block_refs, refs = refs[: len(places)], refs[len(places) :]
    total_ref = None if first else refs[0]
    rows_ref, grad_ref, mark_ref, held, sems = refs[-5:]
    depth = inputs_ref.shape[1] // size
    copies = []
    for number, (place, block_ref) in enumerate(zip(places, block_refs)):
        held[number] = lax.dot_general(
            cotangent_ref[...], block_ref[...], (((1,), (1,)), ((), ())), preferred_element_type=F32
        ).astype(BF16)
        columns = pl.ds(block_start(place, size, depth), depth)
        copies.append(pltpu.make_async_copy(held.at[number], grad_ref.at[:, columns], sems.at[number]))
        copies[-1].start()
    total = jnp.zeros(rows_ref.shape, F32) if first else total_ref[...]
    for place, block_ref in zip(places, block_refs):
        columns = inputs_ref[:, pl.ds(block_start(place, size, depth), depth)]
        total = total + jnp.dot(columns, block_ref[...], preferred_element_type=F32)
    rows_ref[...] = total.astype(rows_ref.dtype)
    mark_ref[...] = jnp.zeros_like(mark_ref)
    for copy in copies:
        copy.wait()


def products(inputs_here, cotangent, blocks, before, size, last=False, after=()):
    tokens, width = inputs_here.shape
    kv_width = cotangent.shape[1]
    depth = width // size
    first = before is None
    operands = [inputs_here, cotangent] + list(blocks.values()) + ([] if first else list(before[:2]))
    whole, anywhere = pl.BlockSpec(memory_space=pltpu.VMEM), pl.BlockSpec(memory_space=pl.ANY)
    return pl.pallas_call(
        functools.partial(products_kernel, size, list(blocks), first),
        out_shape=(
            shape_of(tokens, kv_width, BF16 if last else F32),
            shape_of(tokens, width, BF16),
            shape_of(8, LANES, F32),
        ),
        in_specs=[whole] * (2 + len(blocks)) + ([] if first else [whole, anywhere]) + [anywhere] * len(after),
        out_specs=(whole, anywhere, whole),
        scratch_shapes=[
            pltpu.VMEM((len(blocks), tokens, depth), BF16),
            pltpu.SemaphoreType.DMA((len(blocks),)),
        ],
        input_output_aliases={} if first else {len(operands) - 1: 1},
        compiler_params=pltpu.CompilerParams(vmem_limit_bytes=VMEM_BYTES),
        cost_estimate=pl.CostEstimate(
            flops=4 * tokens * depth * len(blocks) * kv_width,
            bytes_accessed=PRODUCTS_BYTES * (4 if last else 1),
            transcendentals=0,
        ),
        name="last_products" if last else "products",
    )(*operands, *after)


def all_products(inputs_here, cotangent, blocks, size):
    width = inputs_here.shape[1]
    depth = width // size
    here = ring_place(lax.axis_index("fsdp"), size)
    gathered = jnp.zeros((width, cotangent.shape[1]), BF16)
    for place, block in blocks.items():
        gathered = lax.dynamic_update_slice_in_dim(gathered, block, ring_index(here + place, size) * depth, 0)
    rows = jnp.dot(inputs_here, gathered, preferred_element_type=F32).astype(BF16)
    grad = lax.dot_general(cotangent, gathered, (((1,), (1,)), ((), ())), preferred_element_type=F32)
    return rows, grad.astype(BF16)


def own_terms(columns, cotangent, token_weight):
    return (
        lax.dot_general(columns, cotangent, (((0,), (0,)), ((), ())), preferred_element_type=F32) * token_weight
    )


def terms_kernel(size, places, token_weight, inputs_ref, cotangent_ref, *out_refs):
    depth = inputs_ref.shape[1] // size
    for place, out_ref in zip(places, out_refs):
        columns = inputs_ref[:, pl.ds(block_start(place, size, depth), depth)]
        out_ref[...] = own_terms(columns, cotangent_ref[...], token_weight).astype(out_ref.dtype)


def token_terms(inputs_here, cotangent, size, places, dtypes, token_weight):
    tokens, width = inputs_here.shape
    kv_width = cotangent.shape[1]
    depth = width // size
    if depth % LANES == 0:
        return vmem_call(
            functools.partial(terms_kernel, size, places, token_weight),
            [shape_of(depth, kv_width, dtype) for dtype in dtypes],
            [inputs_here, cotangent],
            2 * tokens * depth * len(places) * kv_width,
            "token_terms",
        )
    here = ring_place(lax.axis_index("fsdp"), size)
    out = []
    for place, dtype in zip(places, dtypes):
        columns = lax.dynamic_slice_in_dim(inputs_here, ring_index(here + place, size) * depth, depth, 1)
        out.append(own_terms(columns, cotangent, token_weight).astype(dtype))
    return out


def add_kernel(count, *refs):
    for one_ref, other_ref, out_ref in zip(refs[:count], refs[count : 2 * count], refs[2 * count :]):
        out_ref[...] = (one_ref[...] + other_ref[...].astype(F32)).astype(BF16)


def add_terms(terms, sums, after):
    rows, columns = terms[0].shape
    shapes = [shape_of(rows, columns, BF16)] * len(sums)
    return vmem_call(functools.partial(add_kernel, len(sums)), shapes, terms + sums, 0, "add_terms", after)


def end_kernel(terms_ref, up_ref, down_ref, out_ref):
    out_ref[...] = (terms_ref[...] + up_ref[...].astype(F32) + down_ref[...].astype(F32)).astype(BF16)


def per_device(local_weights, global_weights, momentum, activations, kv_cotangent):
    local_shard = local_weights[0]
    inputs_here = activations[0]
    cotangent = kv_cotangent[0]
    depth, kv_width = local_shard.shape
    size = lax.axis_size("fsdp")
    token_weight = 1.0 / (inputs_here.shape[0] * size)
    wide = depth % LANES == 0
    order = ring_order(size)
    far = size // 2

    def upward(array):
        return lax.ppermute(array, "fsdp", [(order[at - 1], order[at]) for at in range(size)])

    def downward(array):
        return lax.ppermute(array, "fsdp", [(order[at], order[at - 1]) for at in range(size)])

    from_below, from_above = upward(local_shard), downward(local_shard)
    places = [-far, far - 1] + [1 - far] + [sign * step for step in range(far - 2, 0, -1) for sign in (1, -1)] + [0]
    dtypes = [BF16] * 2 + [F32] * (len(places) - 2)
    terms = dict(zip(places, token_terms(inputs_here, cotangent, size, places, dtypes, token_weight)))
    sum_down, sum_up = downward(terms[-far]), upward(terms[far - 1])

    bits = lax.axis_size("replica") // 2
    held = send_windows([local_shard], bits, kv_width, (terms[0],))
    blocks = {0: local_shard}
    made = None
    for step in range(1, far):
        near = far - step
        latest = {-step: from_below, step: from_above}
        blocks.update(latest)
        after = (from_below, from_above)
        order_after = ()
        if step == min(3, far - 1):
            while bits > 1:
                bits //= 2
                shares = [jnp.concatenate(shares, axis=1)]
                shares.append(swap(shares[0], bits))
                joined += [place ^ bits for place in joined]
            order_after = (shares[0],)
        if wide:
            made = products(inputs_here, cotangent, blocks if step == 1 else latest, made, size, after=order_after)
            after = (made[2],)
        if step == min(2, far - 1):
            new_share, new_momentum = update_share(held, global_weights, momentum, after)
            bits = lax.axis_size("replica") // 2
            shares, joined = [new_share, swap(new_share, bits)], [0, bits]
            after += (new_share,)
        if near > 1:
            from_below, from_above = upward(from_below), downward(from_above)
            totals = add_terms([terms[near - 1], terms[-near]], [sum_up, sum_down], after)
            sum_up, sum_down = upward(totals[0]), downward(totals[1])
        else:
            from_below = upward(from_below)
            totals = add_terms([terms[-near]], [sum_down], after)
            sum_down = downward(totals[0])
        while step == 1 and bits > 1:
            bits //= 2
            held = send_windows(held, bits, kv_width, totals)
    latest = {-far: from_below}
    if wide:
        kv_rows, grad_in, mark = products(inputs_here, cotangent, latest, made, size, last=True)
        after = (mark,)
    else:
        kv_rows, grad_in = all_products(inputs_here, cotangent, {**blocks, **latest}, size)
        after = ()
    new_global = join_shares(shares, joined, kv_width, after)
    grad_rows = vmem_call(
        end_kernel, shape_of(depth, kv_width, BF16), [terms[0], sum_up, sum_down], 0, "end_terms", after
    )
    return kv_rows[None], grad_in[None], grad_rows[None], new_global, new_momentum


def solution(mesh):
    placed = (
        P("replica", "fsdp", None),
        P("fsdp", None),
        P("fsdp", "replica"),
        P("replica", "fsdp", None),
        P("replica", "fsdp", None),
    )
    return jax.shard_map(
        per_device,
        mesh=mesh,
        in_specs=placed,
        out_specs=(
            P("replica", "fsdp", None),
            P("replica", "fsdp", None),
            P("replica", "fsdp", None),
            P("fsdp", None),
            P("fsdp", "replica"),
        ),
        check_vma=False,
    )
```

```python
import functools

import jax
import jax.numpy as jnp
from jax import lax
from jax.experimental import pallas as pl
from jax.experimental.pallas import tpu as pltpu
from jax.sharding import PartitionSpec as P

BLOCK = 64

outer_rate = 0.7
outer_momentum = 0.9
scale_epsilon = 1e-06

F32 = jnp.float32
BF16 = jnp.bfloat16
LANES = 128
VMEM_BYTES = 8 * 2**20
PRODUCTS_BYTES = 8 * 2**20


def ring_order(size):
    return list(range(0, size, 2)) + list(range(1, size, 2))[::-1]


def ring_place(index, size):
    return jnp.where((index & 1) == 0, index >> 1, size - 1 - (index >> 1))


def ring_index(place, size):
    place = lax.rem(place + size, size)
    evens = (size + 1) // 2
    return jnp.where(place < evens, 2 * place, 2 * (size - 1 - place) + 1)


def block_start(offset, size, depth, other=0):
    me = lax.axis_index("fsdp")
    row = ring_index(ring_place(me >> 1, size // 2) + offset, size // 2)
    return pl.multiple_of((2 * row + ((me & 1) ^ other)) * depth, depth)


def vmem_call(kernel, out_shape, operands, flops, name, after=(), moved=None):
    def body(*refs):
        kernel(*refs[: len(operands)], *refs[len(operands) + len(after) :])

    moved = moved or sum(x.size * x.dtype.itemsize for x in operands)
    whole = pl.BlockSpec(memory_space=pltpu.VMEM)
    return pl.pallas_call(
        body,
        out_shape=out_shape,
        in_specs=[whole] * len(operands) + [pl.BlockSpec(memory_space=pl.ANY)] * len(after),
        out_specs=jax.tree.map(lambda _: whole, out_shape),
        compiler_params=pltpu.CompilerParams(vmem_limit_bytes=VMEM_BYTES),
        cost_estimate=pl.CostEstimate(flops=flops, bytes_accessed=moved, transcendentals=0),
        name=name,
    )(*operands, *after)


def shape_of(rows, columns, dtype):
    return jax.ShapeDtypeStruct((rows, columns), dtype)


def column_window(array, start, width):
    if isinstance(array, jax.Array):
        return lax.dynamic_slice_in_dim(array, start, width, array.ndim - 1)
    return array[..., pl.ds(pl.multiple_of(start, width), width)]


def outer_kernel(replicas, share_cols, *refs):
    *held_refs, global_ref, momentum_ref, share_ref, new_momentum_ref = refs
    rows, window = held_refs[-1].shape[-2:]
    me = lax.axis_index("replica")

    def windows_of(ref):
        here = me * share_cols // window * window % ref.shape[-1]
        return ref[...] if ref.shape[-1] == window else column_window(ref, here, window)

    old = windows_of(global_ref).astype(F32)
    lane = lax.broadcasted_iota(jnp.int32, (rows, window), 1) // BLOCK
    total = jnp.zeros((rows, window), F32)
    for held_ref in held_refs:
        held = windows_of(held_ref).astype(F32)
        for local in [held] if held.ndim == 2 else list(held):
            drift = old - local
            size = jnp.abs(drift)
            scale = jnp.zeros((rows, window), F32)
            for block in range(window // BLOCK):
                top = jnp.max(jnp.where(lane == block, size, 0.0), axis=1, keepdims=True)
                top = (top + scale_epsilon).astype(BF16).astype(F32)
                scale = jnp.where(lane == block, top, scale)
            total = total + (drift / scale).astype(BF16).astype(F32) * scale
    mean_grad = total / replicas
    shares = window // share_cols
    mean_here, old_here = mean_grad[:, :share_cols], old[:, :share_cols]
    mine = me % shares
    for share in range(1, shares):
        columns = slice(share * share_cols, (share + 1) * share_cols)
        mean_here = jnp.where(mine == share, mean_grad[:, columns], mean_here)
        old_here = jnp.where(mine == share, old[:, columns], old_here)
    new_momentum = outer_momentum * momentum_ref[...] + mean_here
    new_momentum_ref[...] = new_momentum
    share_ref[...] = (old_here - outer_rate * (mean_here + outer_momentum * new_momentum)).astype(BF16)


def swap(array, bits):
    return lax.ppermute(array, "replica", [(at, at ^ bits) for at in range(lax.axis_size("replica"))])


def partner_kernel(bits, share_cols, width, *refs):
    *held_refs, out_ref = refs
    start = (lax.axis_index("replica") ^ bits) * share_cols // width * width
    at = 0
    for held_ref in held_refs:
        part = column_window(held_ref, start % held_ref.shape[-1], width)
        count = 1 if part.ndim == 2 else part.shape[0]
        out_ref[at : at + count] = part.reshape((count,) + part.shape[-2:])
        at += count


def send_windows(held, bits, kv_width, after):
    replicas = lax.axis_size("replica")
    share_cols = kv_width // replicas
    width = max(bits * share_cols, BLOCK)
    rows = held[0].shape[-2]
    count = sum(1 if array.ndim == 2 else array.shape[0] for array in held)
    if width % LANES == 0:
        leaving = vmem_call(
            functools.partial(partner_kernel, bits, share_cols, width),
            jax.ShapeDtypeStruct((count, rows, width), BF16),
            held,
            0,
            "partner_columns",
            after,
        )
    else:
        start = (lax.axis_index("replica") ^ bits) * share_cols // width * width
        parts = [column_window(array, start % array.shape[-1], width).reshape(-1, rows, width) for array in held]
        leaving = jnp.concatenate(parts)
    return held + [swap(leaving, bits)]


def update_share(held, global_weights, momentum, after):
    rows, share_cols = momentum.shape
    replicas = lax.axis_size("replica")
    window = held[-1].shape[-1]
    if window % LANES:
        start = lax.axis_index("replica") * share_cols // window * window
        held = [column_window(array, start % array.shape[-1], window) for array in held]
        global_weights = column_window(global_weights, start, window)
    return vmem_call(
        functools.partial(outer_kernel, replicas, share_cols),
        (shape_of(rows, share_cols, BF16), shape_of(rows, share_cols, F32)),
        held + [global_weights, momentum],
        0,
        "outer_update",
        after,
    )


def join_kernel(places, *refs):
    *held_refs, out_ref = refs
    width = out_ref.shape[1] // len(places)
    me = lax.axis_index("replica")
    at = 0
    for held_ref in held_refs:
        for start in range(0, held_ref.shape[1], width):
            columns = pl.ds(pl.multiple_of((me ^ places[at]) * width, width), width)
            out_ref[:, columns] = held_ref[:, start : start + width]
            at += 1


def join_shares(held, places, kv_width, after):
    rows = held[0].shape[0]
    width = kv_width // len(places)
    if width % LANES == 0:
        return vmem_call(
            functools.partial(join_kernel, places), shape_of(rows, kv_width, BF16), held, 0, "join_shares", after
        )
    whole = jnp.concatenate(held, axis=1)
    joined = jnp.zeros_like(whole)
    for at, place in enumerate(places):
        start = (lax.axis_index("replica") ^ place) * width
        joined = lax.dynamic_update_slice_in_dim(joined, whole[:, at * width : (at + 1) * width], start, 1)
    return joined


PARTNER = {2: (0, 0), 1: (0, 1), 3: (1, 0), 0: (1, 1)}


def pack_kernel(size, inputs_ref, *out_refs):
    depth = inputs_ref.shape[1] // size
    for offset, (at, slot) in PARTNER.items():
        out_refs[at][slot] = inputs_ref[:, pl.ds(block_start(offset, size, depth, 1), depth)]


def pack(inputs_here, size):
    tokens, width = inputs_here.shape
    shapes = [jax.ShapeDtypeStruct((2, tokens, width // size), BF16)] * 2
    return vmem_call(functools.partial(pack_kernel, size), shapes, [inputs_here], 0, "pack_columns")


def terms_kernel(size, offsets, token_weight, inputs_ref, cotangent_ref, partner_ref, partner_cotangent_ref, *out_refs):
    depth = inputs_ref.shape[1] // size
    for offset, out_ref in zip(offsets, out_refs):
        here = inputs_ref[:, pl.ds(block_start(offset, size, depth), depth)]
        there = partner_ref[PARTNER[offset][1]]
        total = 0.0
        for columns, cotangent in ((here, cotangent_ref[...]), (there, partner_cotangent_ref[...])):
            total = total + lax.dot_general(
                columns, cotangent, (((0,), (0,)), ((), ())), preferred_element_type=F32
            )
        out_ref[...] = (total * token_weight).astype(out_ref.dtype)


def token_terms(operands, size, offsets, dtype, token_weight, after=()):
    tokens, width = operands[0].shape
    kv_width = operands[1].shape[1]
    depth = width // size
    return vmem_call(
        functools.partial(terms_kernel, size, offsets, token_weight),
        [shape_of(depth, kv_width, dtype)] * len(offsets),
        operands,
        4 * tokens * depth * len(offsets) * kv_width,
        "token_terms",
        after,
    )


def add_kernel(terms_ref, sum_ref, out_ref):
    out_ref[...] = (terms_ref[...] + sum_ref[...].astype(F32)).astype(BF16)


def end_kernel(terms_ref, up_ref, down_ref, out_ref):
    out_ref[...] = (terms_ref[...] + up_ref[...].astype(F32) + down_ref[...].astype(F32)).astype(BF16)


def products_kernel(size, offsets, last, inputs_ref, cotangent_ref, partner_cotangent_ref, *refs):
    partner_refs, block_refs, refs = refs[:2], refs[2 : 2 + len(offsets)], refs[2 + len(offsets) :]
    total_refs = refs[:2] if last else ()
    here_ref, there_ref, leaving_ref, grad_ref, mark_ref, held, sems = refs[-7:]
    depth = inputs_ref.shape[1] // size
    copies = []
    for number, (offset, block_ref) in enumerate(zip(offsets, block_refs)):
        for cotangent, out_ref in ((partner_cotangent_ref, leaving_ref), (cotangent_ref, held)):
            out_ref[number] = lax.dot_general(
                cotangent[...], block_ref[...], (((1,), (1,)), ((), ())), preferred_element_type=F32
            ).astype(BF16)
        columns = pl.ds(block_start(offset, size, depth), depth)
        copies.append(pltpu.make_async_copy(held.at[number], grad_ref.at[:, columns], sems.at[number]))
        copies[-1].start()
    there, here = (total_refs[1][...], total_refs[0][...]) if last else (0.0, 0.0)
    for offset, block_ref in zip(offsets, block_refs):
        at, slot = PARTNER[offset]
        there = there + jnp.dot(partner_refs[at][slot], block_ref[...], preferred_element_type=F32)
        columns = inputs_ref[:, pl.ds(block_start(offset, size, depth), depth)]
        here = here + jnp.dot(columns, block_ref[...], preferred_element_type=F32)
    here_ref[...] = here
    if last:
        for part in range(there.shape[1] // depth):
            leaving_ref[len(offsets) + part] = there[:, part * depth : (part + 1) * depth].astype(BF16)
    else:
        there_ref[...] = there
    mark_ref[...] = jnp.zeros_like(mark_ref)
    for copy in copies:
        copy.wait()


def products(inputs_here, cotangent, partner_cotangent, partner_inputs, blocks, size, before=None):
    tokens, width = inputs_here.shape
    kv_width = cotangent.shape[1]
    depth = width // size
    last = before is not None
    leaving = len(blocks) + (kv_width // depth if last else 0)
    operands = [inputs_here, cotangent, partner_cotangent, *partner_inputs, *blocks.values()]
    operands += [before[0], before[1], before[3]] if last else []
    whole, anywhere = pl.BlockSpec(memory_space=pltpu.VMEM), pl.BlockSpec(memory_space=pl.ANY)
    total = shape_of(tokens, kv_width, F32)
    mark = shape_of(8, LANES, F32)
    return pl.pallas_call(
        functools.partial(products_kernel, size, list(blocks), last),
        out_shape=(
            total,
            mark if last else total,
            jax.ShapeDtypeStruct((leaving, tokens, depth), BF16),
            shape_of(tokens, width, BF16),
            mark,
        ),
        in_specs=[whole] * (5 + len(blocks)) + ([whole, whole, anywhere] if last else []),
        out_specs=(whole, whole, whole, anywhere, whole),
        scratch_shapes=[
            pltpu.VMEM((len(blocks), tokens, depth), BF16),
            pltpu.SemaphoreType.DMA((len(blocks),)),
        ],
        input_output_aliases={len(operands) - 1: 3} if last else {},
        compiler_params=pltpu.CompilerParams(vmem_limit_bytes=VMEM_BYTES),
        cost_estimate=pl.CostEstimate(
            flops=8 * tokens * depth * len(blocks) * kv_width, bytes_accessed=PRODUCTS_BYTES, transcendentals=0
        ),
        name="last_products" if last else "products",
    )(*operands)


def collect_kernel(size, offsets, total_ref, early_ref, late_ref, _, rows_ref, grad_ref, mark_ref, sems):
    depth = early_ref.shape[-1]
    parts = total_ref.shape[1] // depth
    copies = []
    for number, offset in enumerate(offsets):
        late = number - early_ref.shape[0]
        source = early_ref.at[number] if late < 0 else late_ref.at[late]
        columns = pl.ds(block_start(offset, size, depth, 1), depth)
        copies.append(pltpu.make_async_copy(source, grad_ref.at[:, columns], sems.at[number]))
        copies[-1].start()
    for part in range(parts):
        columns = slice(part * depth, (part + 1) * depth)
        arrived = late_ref[late_ref.shape[0] - parts + part].astype(F32)
        rows_ref[:, columns] = (total_ref[:, columns] + arrived).astype(BF16)
    mark_ref[...] = jnp.zeros_like(mark_ref)
    for copy in copies:
        copy.wait()


def collect(total, early, late, grad, offsets, size):
    tokens, kv_width = total.shape
    whole, anywhere = pl.BlockSpec(memory_space=pltpu.VMEM), pl.BlockSpec(memory_space=pl.ANY)
    return pl.pallas_call(
        functools.partial(collect_kernel, size, offsets),
        out_shape=(shape_of(tokens, kv_width, BF16), shape_of(*grad.shape, BF16), shape_of(8, LANES, F32)),
        in_specs=[whole] * 3 + [anywhere],
        out_specs=(whole, anywhere, whole),
        scratch_shapes=[pltpu.SemaphoreType.DMA((len(offsets),))],
        input_output_aliases={3: 1},
        compiler_params=pltpu.CompilerParams(vmem_limit_bytes=VMEM_BYTES),
        cost_estimate=pl.CostEstimate(flops=tokens * kv_width, bytes_accessed=PRODUCTS_BYTES, transcendentals=0),
        name="collect",
    )(total, early, late, grad)


def inner_and_outer(local_shard, global_weights, momentum, inputs_here, cotangent):
    depth, kv_width = local_shard.shape
    size = lax.axis_size("fsdp")
    ring = size // 2
    token_weight = 1.0 / (inputs_here.shape[0] * size)
    order = ring_order(ring)
    pairs = [(2 * order[at - 1] + side, 2 * order[at] + side) for at in range(ring) for side in (0, 1)]

    def upward(array):
        return lax.ppermute(array, "fsdp", pairs)

    def downward(array):
        return lax.ppermute(array, "fsdp", [(target, source) for source, target in pairs])

    def across(array):
        return lax.ppermute(array, "fsdp", [(at, at ^ 1) for at in range(size)])

    from_below, from_above = upward(local_shard), downward(local_shard)
    partner_cotangent = across(cotangent)
    packed = pack(inputs_here, size)
    partner_inputs = [across(part) for part in packed]

    bits = lax.axis_size("replica") // 2
    held = send_windows([local_shard], bits, kv_width, packed)

    blocks = {0: local_shard, 3: from_below, 1: from_above}
    operands = [inputs_here, cotangent, partner_inputs[0], partner_cotangent]
    first = token_terms(operands, size, [2, 1], BF16, token_weight)
    sum_down, sum_up = downward(first[0]), upward(first[1])
    farthest = upward(from_below)
    while bits > 1:
        bits //= 2
        held = send_windows(held, bits, kv_width, first)
    operands[2] = partner_inputs[1]
    terms = token_terms(operands, size, [3, 0], F32, token_weight)
    made = products(inputs_here, cotangent, partner_cotangent, partner_inputs, blocks, size)
    early = across(made[2])
    new_share, new_momentum = update_share(held, global_weights, momentum, (made[4],))
    bits = lax.axis_size("replica") // 2
    shares, joined = [new_share, swap(new_share, bits)], [0, bits]
    total_down = vmem_call(
        add_kernel, shape_of(depth, kv_width, BF16), [terms[0], sum_down], 0, "add_terms", (new_share,)
    )
    sum_down = downward(total_down)
    made = products(inputs_here, cotangent, partner_cotangent, partner_inputs, {2: farthest}, size, made)
    late = across(made[2])
    while bits > 1:
        bits //= 2
        shares = [jnp.concatenate(shares, axis=1)]
        shares.append(swap(shares[0], bits))
        joined += [place ^ bits for place in joined]
    new_global = join_shares(shares, joined, kv_width, (made[4],))
    grad_rows = vmem_call(
        end_kernel, shape_of(depth, kv_width, BF16), [terms[1], sum_up, sum_down], 0, "end_terms", ()
    )
    kv_rows, grad_in, mark = collect(made[0], early, late, made[3], [*blocks, 2], size)
    return kv_rows, grad_in, grad_rows, new_global, new_momentum


def plain_inner_and_outer(local_shard, global_weights, momentum, inputs_here, cotangent):
    depth, kv_width = local_shard.shape
    token_weight = 1.0 / (inputs_here.shape[0] * lax.axis_size("fsdp"))
    gathered = lax.all_gather(local_shard, "fsdp", axis=0, tiled=True)
    kv_rows = jnp.dot(inputs_here, gathered, preferred_element_type=F32).astype(BF16)
    grad_in = lax.dot_general(cotangent, gathered, (((1,), (1,)), ((), ())), preferred_element_type=F32).astype(BF16)
    terms = lax.dot_general(inputs_here, cotangent, (((0,), (0,)), ((), ())), preferred_element_type=F32)
    grad_rows = lax.psum_scatter(terms * token_weight, "fsdp", scatter_dimension=0, tiled=True).astype(BF16)
    bits = lax.axis_size("replica")
    held = [local_shard]
    while bits > 1:
        bits //= 2
        held = send_windows(held, bits, kv_width, ())
    new_share, new_momentum = update_share(held, global_weights, momentum, ())
    shares, joined = [new_share], [0]
    bits = lax.axis_size("replica")
    while bits > 1:
        bits //= 2
        shares = [jnp.concatenate(shares, axis=1)]
        shares.append(swap(shares[0], bits))
        joined += [place ^ bits for place in joined]
    return kv_rows, grad_in, grad_rows, join_shares(shares, joined, kv_width, ()), new_momentum


def per_device(local_weights, global_weights, momentum, activations, kv_cotangent):
    depth = local_weights.shape[1]
    pairs_fit = lax.axis_size("fsdp") == 8 and depth % LANES == 0 and local_weights.shape[2] % depth == 0
    step = inner_and_outer if pairs_fit else plain_inner_and_outer
    kv_rows, grad_in, grad_rows, new_global, new_momentum = step(
        local_weights[0], global_weights, momentum, activations[0], kv_cotangent[0]
    )
    return kv_rows[None], grad_in[None], grad_rows[None], new_global, new_momentum


def solution(mesh):
    placed = (
        P("replica", "fsdp", None),
        P("fsdp", None),
        P("fsdp", "replica"),
        P("replica", "fsdp", None),
        P("replica", "fsdp", None),
    )
    return jax.shard_map(
        per_device,
        mesh=mesh,
        in_specs=placed,
        out_specs=(
            P("replica", "fsdp", None),
            P("replica", "fsdp", None),
            P("replica", "fsdp", None),
            P("fsdp", None),
            P("fsdp", "replica"),
        ),
        check_vma=False,
    )
```

```python
import functools

import jax
import jax.numpy as jnp
from jax import lax
from jax.experimental import pallas as pl
from jax.experimental.pallas import tpu as pltpu
from jax.sharding import PartitionSpec as P

BLOCK = 64

outer_rate = 0.7
outer_momentum = 0.9
scale_epsilon = 1e-06

F32 = jnp.float32
BF16 = jnp.bfloat16
LANES = 128
VMEM_BYTES = 8 * 2**20


def ring_order(size):
    return list(range(0, size, 2)) + list(range(1, size, 2))[::-1]


def ring_place(index, size):
    return jnp.where((index & 1) == 0, index >> 1, size - 1 - (index >> 1))


def ring_index(place, size):
    place = lax.rem(place + size, size)
    evens = (size + 1) // 2
    return jnp.where(place < evens, 2 * place, 2 * (size - 1 - place) + 1)


def block_start(offset, size, depth, other=0):
    me = lax.axis_index("fsdp")
    row = ring_index(ring_place(me >> 1, size // 2) + offset, size // 2)
    return pl.multiple_of((2 * row + ((me & 1) ^ other)) * depth, depth)


def vmem_call(kernel, out_shape, operands, flops, name, after=(), moved=None):
    def body(*refs):
        kernel(*refs[: len(operands)], *refs[len(operands) + len(after) :])

    moved = moved or sum(x.size * x.dtype.itemsize for x in operands)
    whole = pl.BlockSpec(memory_space=pltpu.VMEM)
    return pl.pallas_call(
        body,
        out_shape=out_shape,
        in_specs=[whole] * len(operands) + [pl.BlockSpec(memory_space=pl.ANY)] * len(after),
        out_specs=jax.tree.map(lambda _: whole, out_shape),
        compiler_params=pltpu.CompilerParams(vmem_limit_bytes=VMEM_BYTES),
        cost_estimate=pl.CostEstimate(flops=flops, bytes_accessed=moved, transcendentals=0),
        name=name,
    )(*operands, *after)


def shape_of(rows, columns, dtype):
    return jax.ShapeDtypeStruct((rows, columns), dtype)


def column_window(array, start, width):
    if isinstance(array, jax.Array):
        return lax.dynamic_slice_in_dim(array, start, width, array.ndim - 1)
    return array[..., pl.ds(pl.multiple_of(start, width), width)]


def outer_kernel(replicas, share_cols, *refs):
    *held_refs, global_ref, momentum_ref, share_ref, new_momentum_ref = refs
    rows, window = held_refs[-1].shape[-2:]
    me = lax.axis_index("replica")

    def windows_of(ref):
        here = me * share_cols // window * window % ref.shape[-1]
        return ref[...] if ref.shape[-1] == window else column_window(ref, here, window)

    old = windows_of(global_ref).astype(F32)
    lane = lax.broadcasted_iota(jnp.int32, (rows, window), 1) // BLOCK
    total = jnp.zeros((rows, window), F32)
    for held_ref in held_refs:
        held = windows_of(held_ref).astype(F32)
        for local in [held] if held.ndim == 2 else list(held):
            drift = old - local
            size = jnp.abs(drift)
            scale = jnp.zeros((rows, window), F32)
            for block in range(window // BLOCK):
                top = jnp.max(jnp.where(lane == block, size, 0.0), axis=1, keepdims=True)
                top = (top + scale_epsilon).astype(BF16).astype(F32)
                scale = jnp.where(lane == block, top, scale)
            total = total + (drift / scale).astype(BF16).astype(F32) * scale
    mean_grad = total / replicas
    shares = window // share_cols
    mean_here, old_here = mean_grad[:, :share_cols], old[:, :share_cols]
    mine = me % shares
    for share in range(1, shares):
        columns = slice(share * share_cols, (share + 1) * share_cols)
        mean_here = jnp.where(mine == share, mean_grad[:, columns], mean_here)
        old_here = jnp.where(mine == share, old[:, columns], old_here)
    new_momentum = outer_momentum * momentum_ref[...] + mean_here
    new_momentum_ref[...] = new_momentum
    share_ref[...] = (old_here - outer_rate * (mean_here + outer_momentum * new_momentum)).astype(BF16)


def swap(array, bits):
    return lax.ppermute(array, "replica", [(at, at ^ bits) for at in range(lax.axis_size("replica"))])


def partner_kernel(bits, share_cols, width, *refs):
    *held_refs, out_ref = refs
    start = (lax.axis_index("replica") ^ bits) * share_cols // width * width
    at = 0
    for held_ref in held_refs:
        part = column_window(held_ref, start % held_ref.shape[-1], width)
        count = 1 if part.ndim == 2 else part.shape[0]
        out_ref[at : at + count] = part.reshape((count,) + part.shape[-2:])
        at += count


def send_windows(held, bits, kv_width, after):
    replicas = lax.axis_size("replica")
    share_cols = kv_width // replicas
    width = max(bits * share_cols, BLOCK)
    rows = held[0].shape[-2]
    count = sum(1 if array.ndim == 2 else array.shape[0] for array in held)
    if width % LANES == 0:
        leaving = vmem_call(
            functools.partial(partner_kernel, bits, share_cols, width),
            jax.ShapeDtypeStruct((count, rows, width), BF16),
            held,
            0,
            "partner_columns",
            after,
        )
    else:
        start = (lax.axis_index("replica") ^ bits) * share_cols // width * width
        parts = [column_window(array, start % array.shape[-1], width).reshape(-1, rows, width) for array in held]
        leaving = jnp.concatenate(parts)
    return held + [swap(leaving, bits)]


def update_share(held, global_weights, momentum, after):
    rows, share_cols = momentum.shape
    replicas = lax.axis_size("replica")
    window = held[-1].shape[-1]
    if window % LANES:
        start = lax.axis_index("replica") * share_cols // window * window
        held = [column_window(array, start % array.shape[-1], window) for array in held]
        global_weights = column_window(global_weights, start, window)
    return vmem_call(
        functools.partial(outer_kernel, replicas, share_cols),
        (shape_of(rows, share_cols, BF16), shape_of(rows, share_cols, F32)),
        held + [global_weights, momentum],
        0,
        "outer_update",
        after,
    )


def join_kernel(places, *refs):
    *held_refs, out_ref = refs
    width = out_ref.shape[1] // len(places)
    me = lax.axis_index("replica")
    at = 0
    for held_ref in held_refs:
        for start in range(0, held_ref.shape[1], width):
            columns = pl.ds(pl.multiple_of((me ^ places[at]) * width, width), width)
            out_ref[:, columns] = held_ref[:, start : start + width]
            at += 1


def join_shares(held, places, kv_width, after):
    rows = held[0].shape[0]
    width = kv_width // len(places)
    if width % LANES == 0:
        return vmem_call(
            functools.partial(join_kernel, places), shape_of(rows, kv_width, BF16), held, 0, "join_shares", after
        )
    whole = jnp.concatenate(held, axis=1)
    joined = jnp.zeros_like(whole)
    for at, place in enumerate(places):
        start = (lax.axis_index("replica") ^ place) * width
        joined = lax.dynamic_update_slice_in_dim(joined, whole[:, at * width : (at + 1) * width], start, 1)
    return joined


PARTNER = {2: (0, 0), 1: (0, 1), 3: (1, 0), 0: (1, 1)}


def pack_kernel(size, part, inputs_ref, out_ref):
    depth = inputs_ref.shape[1] // size
    for offset, (at, slot) in PARTNER.items():
        if at == part:
            out_ref[slot] = inputs_ref[:, pl.ds(block_start(offset, size, depth, 1), depth)]


def pack(inputs_here, size, part, after=()):
    tokens, width = inputs_here.shape
    shape = jax.ShapeDtypeStruct((2, tokens, width // size), BF16)
    return vmem_call(functools.partial(pack_kernel, size, part), shape, [inputs_here], 0, "pack_columns", after)


def terms_kernel(size, offsets, token_weight, inputs_ref, cotangent_ref, partner_ref, partner_cotangent_ref, *out_refs):
    depth = inputs_ref.shape[1] // size
    for offset, out_ref in zip(offsets, out_refs):
        here = inputs_ref[:, pl.ds(block_start(offset, size, depth), depth)]
        there = partner_ref[PARTNER[offset][1]]
        total = 0.0
        for columns, cotangent in ((here, cotangent_ref[...]), (there, partner_cotangent_ref[...])):
            total = total + lax.dot_general(
                columns, cotangent, (((0,), (0,)), ((), ())), preferred_element_type=F32
            )
        out_ref[...] = (total * token_weight).astype(out_ref.dtype)


def token_terms(operands, size, offsets, dtype, token_weight, after=()):
    tokens, width = operands[0].shape
    kv_width = operands[1].shape[1]
    depth = width // size
    return vmem_call(
        functools.partial(terms_kernel, size, offsets, token_weight),
        [shape_of(depth, kv_width, dtype)] * len(offsets),
        operands,
        4 * tokens * depth * len(offsets) * kv_width,
        "token_terms",
        after,
    )


def add_kernel(terms_ref, sum_ref, out_ref):
    out_ref[...] = (terms_ref[...] + sum_ref[...].astype(F32)).astype(BF16)


def end_kernel(terms_ref, up_ref, down_ref, out_ref):
    out_ref[...] = (terms_ref[...] + up_ref[...].astype(F32) + down_ref[...].astype(F32)).astype(BF16)


def back_product(cotangent, block):
    return lax.dot_general(cotangent, block, (((1,), (1,)), ((), ())), preferred_element_type=F32).astype(BF16)


def grads_kernel(cotangent_ref, partner_cotangent_ref, *refs):
    *block_refs, here_ref, leaving_ref = refs
    for number, block_ref in enumerate(block_refs):
        here_ref[number] = back_product(cotangent_ref[...], block_ref[...])
        leaving_ref[number] = back_product(partner_cotangent_ref[...], block_ref[...])


def near_grads(cotangent, partner_cotangent, blocks, after):
    tokens, kv_width = cotangent.shape
    depth = blocks[0].shape[0]
    shape = jax.ShapeDtypeStruct((len(blocks), tokens, depth), BF16)
    operands = [cotangent, partner_cotangent, *blocks.values()]
    flops = 4 * tokens * depth * len(blocks) * kv_width
    return vmem_call(grads_kernel, [shape] * 2, operands, flops, "near_grads", after)


def rows_kernel(size, offsets, inputs_ref, *refs):
    partner_refs, block_refs, (here_ref, there_ref) = refs[:2], refs[2:-2], refs[-2:]
    depth = inputs_ref.shape[1] // size
    here = there = 0.0
    for offset, block_ref in zip(offsets, block_refs):
        at, slot = PARTNER[offset]
        columns = inputs_ref[:, pl.ds(block_start(offset, size, depth), depth)]
        here = here + jnp.dot(columns, block_ref[...], preferred_element_type=F32)
        there = there + jnp.dot(partner_refs[at][slot], block_ref[...], preferred_element_type=F32)
    here_ref[...], there_ref[...] = here, there


def near_rows(inputs_here, partner_inputs, blocks, size, after):
    tokens, kv_width = inputs_here.shape[0], blocks[0].shape[1]
    return vmem_call(
        functools.partial(rows_kernel, size, list(blocks)),
        [shape_of(tokens, kv_width, F32)] * 2,
        [inputs_here, *partner_inputs, *blocks.values()],
        4 * tokens * blocks[0].shape[0] * len(blocks) * kv_width,
        "near_rows",
        after,
    )


def last_kernel(
    size, offset, inputs_ref, cotangent_ref, partner_ref, partner_cotangent_ref, block_ref, here_ref, there_ref, *outs
):
    rows_ref, grad_ref, leaving_ref = outs
    depth = block_ref.shape[0]
    leaving_ref[0] = back_product(partner_cotangent_ref[...], block_ref[...])
    there = there_ref[...] + jnp.dot(
        partner_ref[PARTNER[offset][1]], block_ref[...], preferred_element_type=F32
    )
    for part in range(there.shape[1] // depth):
        leaving_ref[1 + part] = there[:, part * depth : (part + 1) * depth].astype(BF16)
    grad_ref[0] = back_product(cotangent_ref[...], block_ref[...])
    columns = inputs_ref[:, pl.ds(block_start(offset, size, depth), depth)]
    rows_ref[...] = here_ref[...] + jnp.dot(columns, block_ref[...], preferred_element_type=F32)


def last_products(inputs_here, cotangent, partner_inputs, partner_cotangent, block, totals, size, offset):
    tokens = inputs_here.shape[0]
    depth, kv_width = block.shape
    return vmem_call(
        functools.partial(last_kernel, size, offset),
        [
            shape_of(tokens, kv_width, F32),
            jax.ShapeDtypeStruct((1, tokens, depth), BF16),
            jax.ShapeDtypeStruct((1 + kv_width // depth, tokens, depth), BF16),
        ],
        [inputs_here, cotangent, partner_inputs[PARTNER[offset][0]], partner_cotangent, block, *totals],
        8 * tokens * depth * kv_width,
        "last_products",
    )


def write_columns(size, sources, grad_ref, sems):
    depth = grad_ref.shape[1] // size
    copies = []
    for source_ref, number, offset, other in sources:
        columns = pl.ds(block_start(offset, size, depth, other), depth)
        copies.append(pltpu.make_async_copy(source_ref.at[number], grad_ref.at[:, columns], sems.at[len(copies)]))
        copies[-1].start()
    return copies


def collect_kernel(size, offsets, near_ref, last_ref, early_ref, *refs):
    grad_ref, mark_ref, sems = refs[-3:]
    sources = [(near_ref, number, offset, 0) for number, offset in enumerate(offsets[:-1])]
    sources += [(last_ref, 0, offsets[-1], 0)]
    sources += [(early_ref, number, offset, 1) for number, offset in enumerate(offsets[:-1])]
    copies = write_columns(size, sources, grad_ref, sems)
    mark_ref[...] = jnp.zeros_like(mark_ref)
    for copy in copies:
        copy.wait()


def collect_last_kernel(size, offset, total_ref, late_ref, _, rows_ref, grad_ref, sems):
    copies = write_columns(size, [(late_ref, 0, offset, 1)], grad_ref, sems)
    depth = late_ref.shape[-1]
    for part in range(total_ref.shape[1] // depth):
        columns = slice(part * depth, (part + 1) * depth)
        rows_ref[:, columns] = (total_ref[:, columns] + late_ref[1 + part].astype(F32)).astype(BF16)
    for copy in copies:
        copy.wait()


def collect(kernel, out_shape, operands, grad, count, name, after=()):
    whole, anywhere = pl.BlockSpec(memory_space=pltpu.VMEM), pl.BlockSpec(memory_space=pl.ANY)
    given = [] if grad is None else [grad]
    return pl.pallas_call(
        kernel,
        out_shape=out_shape,
        in_specs=[whole] * len(operands) + [anywhere] * (len(given) + len(after)),
        out_specs=(anywhere, whole) if grad is None else (whole, anywhere),
        scratch_shapes=[pltpu.SemaphoreType.DMA((count,))],
        input_output_aliases={} if grad is None else {len(operands): 1},
        compiler_params=pltpu.CompilerParams(vmem_limit_bytes=VMEM_BYTES),
        cost_estimate=pl.CostEstimate(flops=0, bytes_accessed=2**20, transcendentals=0),
        name=name,
    )(*operands, *given, *after)


def inner_and_outer(local_shard, global_weights, momentum, inputs_here, cotangent):
    depth, kv_width = local_shard.shape
    tokens, width = inputs_here.shape
    size = lax.axis_size("fsdp")
    ring = size // 2
    token_weight = 1.0 / (tokens * size)
    order = ring_order(ring)
    pairs = [(2 * order[at - 1] + side, 2 * order[at] + side) for at in range(ring) for side in (0, 1)]

    def upward(array):
        return lax.ppermute(array, "fsdp", pairs)

    def downward(array):
        return lax.ppermute(array, "fsdp", [(target, source) for source, target in pairs])

    def across(array):
        return lax.ppermute(array, "fsdp", [(at, at ^ 1) for at in range(size)])

    from_below, from_above = upward(local_shard), downward(local_shard)
    partner_cotangent = across(cotangent)
    packed = pack(inputs_here, size, 0)
    partner_inputs = [across(packed), across(pack(inputs_here, size, 1, (partner_cotangent,)))]

    bits = lax.axis_size("replica") // 2
    held = send_windows([local_shard], bits, kv_width, (packed,))

    blocks = {0: local_shard, 3: from_below, 1: from_above}
    farthest = upward(from_below)
    operands = [inputs_here, cotangent, partner_inputs[0], partner_cotangent]
    first = token_terms(operands, size, [2, 1], BF16, token_weight)
    sum_down, sum_up = downward(first[0]), upward(first[1])
    while bits > 1:
        bits //= 2
        held = send_windows(held, bits, kv_width, first)
    grads, leaving = near_grads(cotangent, partner_cotangent, blocks, first)
    early = across(leaving)
    operands[2] = partner_inputs[1]
    terms = token_terms(operands, size, [3, 0], F32, token_weight, (leaving,))
    totals = near_rows(inputs_here, partner_inputs, blocks, size, (leaving,))
    rows, last_grads, leaving = last_products(
        inputs_here, cotangent, partner_inputs, partner_cotangent, farthest, totals, size, 2
    )
    late = across(leaving)
    total_down = vmem_call(
        add_kernel, shape_of(depth, kv_width, BF16), [terms[0], sum_down], 0, "add_terms", (leaving,)
    )
    sum_down = downward(total_down)
    new_share, new_momentum = update_share(held, global_weights, momentum, (total_down,))
    bits = lax.axis_size("replica")
    shares, joined = [new_share], [0]
    while bits > 1:
        bits //= 2
        shares = [shares[0] if len(shares) == 1 else jnp.concatenate(shares, axis=1)]
        shares.append(swap(shares[0], bits))
        joined += [place ^ bits for place in joined]
    offsets = [*blocks, 2]
    grad, mark = collect(
        functools.partial(collect_kernel, size, offsets),
        (shape_of(tokens, width, BF16), shape_of(8, LANES, F32)),
        [grads, last_grads, early],
        None,
        2 * len(offsets) - 1,
        "collect",
    )
    new_global = join_shares(shares, joined, kv_width, (mark,))
    grad_rows = vmem_call(
        end_kernel, shape_of(depth, kv_width, BF16), [terms[1], sum_up, sum_down], 0, "end_terms", ()
    )
    kv_rows, grad_in = collect(
        functools.partial(collect_last_kernel, size, offsets[-1]),
        (shape_of(tokens, kv_width, BF16), shape_of(tokens, width, BF16)),
        [rows, late],
        grad,
        1,
        "collect_last",
    )
    return kv_rows, grad_in, grad_rows, new_global, new_momentum


def plain_inner_and_outer(local_shard, global_weights, momentum, inputs_here, cotangent):
    depth, kv_width = local_shard.shape
    token_weight = 1.0 / (inputs_here.shape[0] * lax.axis_size("fsdp"))
    gathered = lax.all_gather(local_shard, "fsdp", axis=0, tiled=True)
    kv_rows = jnp.dot(inputs_here, gathered, preferred_element_type=F32).astype(BF16)
    grad_in = lax.dot_general(cotangent, gathered, (((1,), (1,)), ((), ())), preferred_element_type=F32).astype(BF16)
    terms = lax.dot_general(inputs_here, cotangent, (((0,), (0,)), ((), ())), preferred_element_type=F32)
    grad_rows = lax.psum_scatter(terms * token_weight, "fsdp", scatter_dimension=0, tiled=True).astype(BF16)
    bits = lax.axis_size("replica")
    held = [local_shard]
    while bits > 1:
        bits //= 2
        held = send_windows(held, bits, kv_width, ())
    new_share, new_momentum = update_share(held, global_weights, momentum, ())
    shares, joined = [new_share], [0]
    bits = lax.axis_size("replica")
    while bits > 1:
        bits //= 2
        shares = [jnp.concatenate(shares, axis=1)]
        shares.append(swap(shares[0], bits))
        joined += [place ^ bits for place in joined]
    return kv_rows, grad_in, grad_rows, join_shares(shares, joined, kv_width, ()), new_momentum


def per_device(local_weights, global_weights, momentum, activations, kv_cotangent):
    depth = local_weights.shape[1]
    pairs_fit = lax.axis_size("fsdp") == 8 and depth % LANES == 0 and local_weights.shape[2] % depth == 0
    step = inner_and_outer if pairs_fit else plain_inner_and_outer
    kv_rows, grad_in, grad_rows, new_global, new_momentum = step(
        local_weights[0], global_weights, momentum, activations[0], kv_cotangent[0]
    )
    return kv_rows[None], grad_in[None], grad_rows[None], new_global, new_momentum


def solution(mesh):
    placed = (
        P("replica", "fsdp", None),
        P("fsdp", None),
        P("fsdp", "replica"),
        P("replica", "fsdp", None),
        P("replica", "fsdp", None),
    )
    return jax.shard_map(
        per_device,
        mesh=mesh,
        in_specs=placed,
        out_specs=(
            P("replica", "fsdp", None),
            P("replica", "fsdp", None),
            P("replica", "fsdp", None),
            P("fsdp", None),
            P("fsdp", "replica"),
        ),
        check_vma=False,
    )
```

```python
import functools

import jax
import jax.numpy as jnp
from jax import lax
from jax.experimental import pallas as pl
from jax.experimental.pallas import tpu as pltpu
from jax.sharding import PartitionSpec as P

BLOCK = 64

outer_rate = 0.7
outer_momentum = 0.9
scale_epsilon = 1e-06

F32 = jnp.float32
BF16 = jnp.bfloat16
LANES = 128
VMEM_BYTES = 8 * 2**20


def ring_order(size):
    return list(range(0, size, 2)) + list(range(1, size, 2))[::-1]


def ring_place(index, size):
    return jnp.where((index & 1) == 0, index >> 1, size - 1 - (index >> 1))


def ring_index(place, size):
    place = lax.rem(place + size, size)
    evens = (size + 1) // 2
    return jnp.where(place < evens, 2 * place, 2 * (size - 1 - place) + 1)


def block_start(offset, size, depth, other=0):
    me = lax.axis_index("fsdp")
    row = ring_index(ring_place(me >> 1, size // 2) + offset, size // 2)
    return pl.multiple_of((2 * row + ((me & 1) ^ other)) * depth, depth)


def vmem_call(kernel, out_shape, operands, flops, name, after=(), moved=None):
    def body(*refs):
        kernel(*refs[: len(operands)], *refs[len(operands) + len(after) :])

    moved = moved or sum(x.size * x.dtype.itemsize for x in operands)
    whole = pl.BlockSpec(memory_space=pltpu.VMEM)
    return pl.pallas_call(
        body,
        out_shape=out_shape,
        in_specs=[whole] * len(operands) + [pl.BlockSpec(memory_space=pl.ANY)] * len(after),
        out_specs=jax.tree.map(lambda _: whole, out_shape),
        compiler_params=pltpu.CompilerParams(vmem_limit_bytes=VMEM_BYTES),
        cost_estimate=pl.CostEstimate(flops=flops, bytes_accessed=moved, transcendentals=0),
        name=name,
    )(*operands, *after)


def shape_of(rows, columns, dtype):
    return jax.ShapeDtypeStruct((rows, columns), dtype)


def column_window(array, start, width):
    if isinstance(array, jax.Array):
        return lax.dynamic_slice_in_dim(array, start, width, array.ndim - 1)
    return array[..., pl.ds(pl.multiple_of(start, width), width)]


def outer_kernel(replicas, share_cols, *refs):
    *held_refs, global_ref, momentum_ref, share_ref, new_momentum_ref = refs
    rows, window = held_refs[-1].shape[-2:]
    me = lax.axis_index("replica")

    def windows_of(ref):
        here = me * share_cols // window * window % ref.shape[-1]
        return ref[...] if ref.shape[-1] == window else column_window(ref, here, window)

    old = windows_of(global_ref).astype(F32)
    lane = lax.broadcasted_iota(jnp.int32, (rows, window), 1) // BLOCK
    total = jnp.zeros((rows, window), F32)
    for held_ref in held_refs:
        held = windows_of(held_ref).astype(F32)
        for local in [held] if held.ndim == 2 else list(held):
            drift = old - local
            size = jnp.abs(drift)
            scale = jnp.zeros((rows, window), F32)
            for block in range(window // BLOCK):
                top = jnp.max(jnp.where(lane == block, size, 0.0), axis=1, keepdims=True)
                top = (top + scale_epsilon).astype(BF16).astype(F32)
                scale = jnp.where(lane == block, top, scale)
            total = total + (drift / scale).astype(BF16).astype(F32) * scale
    mean_grad = total / replicas
    shares = window // share_cols
    mean_here, old_here = mean_grad[:, :share_cols], old[:, :share_cols]
    mine = me % shares
    for share in range(1, shares):
        columns = slice(share * share_cols, (share + 1) * share_cols)
        mean_here = jnp.where(mine == share, mean_grad[:, columns], mean_here)
        old_here = jnp.where(mine == share, old[:, columns], old_here)
    new_momentum = outer_momentum * momentum_ref[...] + mean_here
    new_momentum_ref[...] = new_momentum
    share_ref[...] = (old_here - outer_rate * (mean_here + outer_momentum * new_momentum)).astype(BF16)


def swap(array, bits):
    return lax.ppermute(array, "replica", [(at, at ^ bits) for at in range(lax.axis_size("replica"))])


def partner_kernel(bits, share_cols, width, *refs):
    *held_refs, out_ref = refs
    start = (lax.axis_index("replica") ^ bits) * share_cols // width * width
    at = 0
    for held_ref in held_refs:
        part = column_window(held_ref, start % held_ref.shape[-1], width)
        count = 1 if part.ndim == 2 else part.shape[0]
        out_ref[at : at + count] = part.reshape((count,) + part.shape[-2:])
        at += count


def send_windows(held, bits, kv_width, after):
    replicas = lax.axis_size("replica")
    share_cols = kv_width // replicas
    width = max(bits * share_cols, BLOCK)
    rows = held[0].shape[-2]
    count = sum(1 if array.ndim == 2 else array.shape[0] for array in held)
    if width % LANES == 0:
        leaving = vmem_call(
            functools.partial(partner_kernel, bits, share_cols, width),
            jax.ShapeDtypeStruct((count, rows, width), BF16),
            held,
            0,
            "partner_columns",
            after,
        )
    else:
        start = (lax.axis_index("replica") ^ bits) * share_cols // width * width
        parts = [column_window(array, start % array.shape[-1], width).reshape(-1, rows, width) for array in held]
        leaving = jnp.concatenate(parts)
    return held + [swap(leaving, bits)]


def update_share(held, global_weights, momentum, after):
    rows, share_cols = momentum.shape
    replicas = lax.axis_size("replica")
    window = held[-1].shape[-1]
    if window % LANES:
        start = lax.axis_index("replica") * share_cols // window * window
        held = [column_window(array, start % array.shape[-1], window) for array in held]
        global_weights = column_window(global_weights, start, window)
    return vmem_call(
        functools.partial(outer_kernel, replicas, share_cols),
        (shape_of(rows, share_cols, BF16), shape_of(rows, share_cols, F32)),
        held + [global_weights, momentum],
        0,
        "outer_update",
        after,
    )


def join_kernel(places, *refs):
    *held_refs, out_ref = refs
    width = out_ref.shape[1] // len(places)
    me = lax.axis_index("replica")
    at = 0
    for held_ref in held_refs:
        for start in range(0, held_ref.shape[1], width):
            columns = pl.ds(pl.multiple_of((me ^ places[at]) * width, width), width)
            out_ref[:, columns] = held_ref[:, start : start + width]
            at += 1


def join_shares(held, places, kv_width, after):
    rows = held[0].shape[0]
    width = kv_width // len(places)
    if width % LANES == 0:
        return vmem_call(
            functools.partial(join_kernel, places), shape_of(rows, kv_width, BF16), held, 0, "join_shares", after
        )
    whole = jnp.concatenate(held, axis=1)
    joined = jnp.zeros_like(whole)
    for at, place in enumerate(places):
        start = (lax.axis_index("replica") ^ place) * width
        joined = lax.dynamic_update_slice_in_dim(joined, whole[:, at * width : (at + 1) * width], start, 1)
    return joined


PARTNER = {2: (0, 0), 1: (0, 1), 3: (1, 0), 0: (1, 1)}


def pack_kernel(size, part, inputs_ref, out_ref):
    depth = inputs_ref.shape[1] // size
    for offset, (at, slot) in PARTNER.items():
        if at == part:
            out_ref[slot] = inputs_ref[:, pl.ds(block_start(offset, size, depth, 1), depth)]


def pack(inputs_here, size, part, after=()):
    tokens, width = inputs_here.shape
    shape = jax.ShapeDtypeStruct((2, tokens, width // size), BF16)
    return vmem_call(functools.partial(pack_kernel, size, part), shape, [inputs_here], 0, "pack_columns", after)


def terms_kernel(size, offsets, token_weight, inputs_ref, cotangent_ref, partner_ref, partner_cotangent_ref, *out_refs):
    depth = inputs_ref.shape[1] // size
    for offset, out_ref in zip(offsets, out_refs):
        here = inputs_ref[:, pl.ds(block_start(offset, size, depth), depth)]
        there = partner_ref[PARTNER[offset][1]]
        total = 0.0
        for columns, cotangent in ((here, cotangent_ref[...]), (there, partner_cotangent_ref[...])):
            total = total + lax.dot_general(
                columns, cotangent, (((0,), (0,)), ((), ())), preferred_element_type=F32
            )
        out_ref[...] = (total * token_weight).astype(out_ref.dtype)


def token_terms(operands, size, offsets, dtype, token_weight, after=()):
    tokens, width = operands[0].shape
    kv_width = operands[1].shape[1]
    depth = width // size
    return vmem_call(
        functools.partial(terms_kernel, size, offsets, token_weight),
        [shape_of(depth, kv_width, dtype)] * len(offsets),
        operands,
        4 * tokens * depth * len(offsets) * kv_width,
        "token_terms",
        after,
    )


def add_kernel(terms_ref, sum_ref, out_ref):
    out_ref[...] = (terms_ref[...] + sum_ref[...].astype(F32)).astype(BF16)


def back_product(cotangent, block):
    return lax.dot_general(cotangent, block, (((1,), (1,)), ((), ())), preferred_element_type=F32).astype(BF16)


def grads_kernel(cotangent_ref, partner_cotangent_ref, *refs):
    *block_refs, here_ref, leaving_ref = refs
    for number, block_ref in enumerate(block_refs):
        here_ref[number] = back_product(cotangent_ref[...], block_ref[...])
        leaving_ref[number] = back_product(partner_cotangent_ref[...], block_ref[...])


def near_grads(cotangent, partner_cotangent, blocks, after):
    tokens, kv_width = cotangent.shape
    depth = blocks[0].shape[0]
    shape = jax.ShapeDtypeStruct((len(blocks), tokens, depth), BF16)
    operands = [cotangent, partner_cotangent, *blocks.values()]
    flops = 4 * tokens * depth * len(blocks) * kv_width
    return vmem_call(grads_kernel, [shape] * 2, operands, flops, "near_grads", after)


def rows_kernel(size, offsets, inputs_ref, *refs):
    partner_refs, block_refs, (here_ref, there_ref) = refs[:2], refs[2:-2], refs[-2:]
    depth = inputs_ref.shape[1] // size
    here = there = 0.0
    for offset, block_ref in zip(offsets, block_refs):
        at, slot = PARTNER[offset]
        columns = inputs_ref[:, pl.ds(block_start(offset, size, depth), depth)]
        here = here + jnp.dot(columns, block_ref[...], preferred_element_type=F32)
        there = there + jnp.dot(partner_refs[at][slot], block_ref[...], preferred_element_type=F32)
    here_ref[...], there_ref[...] = here, there


def near_rows(inputs_here, partner_inputs, blocks, size, after):
    tokens, kv_width = inputs_here.shape[0], blocks[0].shape[1]
    return vmem_call(
        functools.partial(rows_kernel, size, list(blocks)),
        [shape_of(tokens, kv_width, F32)] * 2,
        [inputs_here, *partner_inputs, *blocks.values()],
        4 * tokens * blocks[0].shape[0] * len(blocks) * kv_width,
        "near_rows",
        after,
    )


def last_kernel(size, offsets, inputs_ref, cotangent_ref, partner_ref, partner_cotangent_ref, *refs):
    block_refs, (here_ref, there_ref, rows_ref, grad_ref, leaving_ref) = refs[: len(offsets)], refs[len(offsets) :]
    depth = block_refs[0].shape[0]
    for number, block_ref in enumerate(block_refs):
        leaving_ref[number] = back_product(partner_cotangent_ref[...], block_ref[...])
    last = block_refs[-1][...]
    there = there_ref[...] + jnp.dot(partner_ref[PARTNER[offsets[-1]][1]], last, preferred_element_type=F32)
    for part in range(there.shape[1] // depth):
        leaving_ref[len(offsets) + part] = there[:, part * depth : (part + 1) * depth].astype(BF16)
    for number, block_ref in enumerate(block_refs):
        grad_ref[number] = back_product(cotangent_ref[...], block_ref[...])
    columns = inputs_ref[:, pl.ds(block_start(offsets[-1], size, depth), depth)]
    rows_ref[...] = here_ref[...] + jnp.dot(columns, last, preferred_element_type=F32)


def last_products(inputs_here, cotangent, partner_inputs, partner_cotangent, blocks, totals, size):
    tokens = inputs_here.shape[0]
    offsets = list(blocks)
    depth, kv_width = blocks[offsets[-1]].shape
    partner = partner_inputs[PARTNER[offsets[-1]][0]]
    return vmem_call(
        functools.partial(last_kernel, size, offsets),
        [
            shape_of(tokens, kv_width, F32),
            jax.ShapeDtypeStruct((len(blocks), tokens, depth), BF16),
            jax.ShapeDtypeStruct((len(blocks) + kv_width // depth, tokens, depth), BF16),
        ],
        [inputs_here, cotangent, partner, partner_cotangent, *blocks.values(), *totals],
        8 * tokens * depth * kv_width,
        "last_products",
    )


def write_columns(size, sources, grad_ref, sems):
    depth = grad_ref.shape[1] // size
    copies = []
    for source_ref, number, offset, other in sources:
        columns = pl.ds(block_start(offset, size, depth, other), depth)
        copies.append(pltpu.make_async_copy(source_ref.at[number], grad_ref.at[:, columns], sems.at[len(copies)]))
        copies[-1].start()
    return copies


def collect_kernel(size, early, late, near_ref, last_ref, early_ref, grad_ref, mark_ref, sems):
    sources = [(near_ref, number, offset, 0) for number, offset in enumerate(early)]
    sources += [(last_ref, number, offset, 0) for number, offset in enumerate(late)]
    sources += [(early_ref, number, offset, 1) for number, offset in enumerate(early)]
    copies = write_columns(size, sources, grad_ref, sems)
    mark_ref[...] = jnp.zeros_like(mark_ref)
    for copy in copies:
        copy.wait()


def collect(grads, width, size, early, late):
    whole, anywhere = pl.BlockSpec(memory_space=pltpu.VMEM), pl.BlockSpec(memory_space=pl.ANY)
    return pl.pallas_call(
        functools.partial(collect_kernel, size, early, late),
        out_shape=(shape_of(grads[0].shape[1], width, BF16), shape_of(8, LANES, F32)),
        in_specs=[whole] * len(grads),
        out_specs=(anywhere, whole),
        scratch_shapes=[pltpu.SemaphoreType.DMA((2 * len(early) + len(late),))],
        compiler_params=pltpu.CompilerParams(vmem_limit_bytes=VMEM_BYTES),
        cost_estimate=pl.CostEstimate(flops=0, bytes_accessed=2**20, transcendentals=0),
        name="collect",
    )(*grads)


def finish_kernel(size, late, total_ref, late_ref, terms_ref, up_ref, down_ref, _, *refs):
    rows_ref, grad_ref, sum_ref, rows_held, sum_held, sems, sem_rows, sem_sum = refs
    copies = write_columns(size, [(late_ref, number, offset, 1) for number, offset in enumerate(late)], grad_ref, sems)
    depth = late_ref.shape[-1]
    for part in range(total_ref.shape[1] // depth):
        columns = slice(part * depth, (part + 1) * depth)
        rows_held[:, columns] = (total_ref[:, columns] + late_ref[len(late) + part].astype(F32)).astype(BF16)
    copies.append(pltpu.make_async_copy(rows_held, rows_ref, sem_rows))
    copies[-1].start()
    sum_held[...] = (terms_ref[...] + up_ref[...].astype(F32) + down_ref[...].astype(F32)).astype(BF16)
    copies.append(pltpu.make_async_copy(sum_held, sum_ref, sem_sum))
    copies[-1].start()
    for copy in copies:
        copy.wait()


def finish(total, late, sums, grad, size, offsets):
    whole, anywhere = pl.BlockSpec(memory_space=pltpu.VMEM), pl.BlockSpec(memory_space=pl.ANY)
    rows, summed = shape_of(*total.shape, BF16), shape_of(*sums[0].shape, BF16)
    return pl.pallas_call(
        functools.partial(finish_kernel, size, offsets),
        out_shape=(rows, shape_of(*grad.shape, BF16), summed),
        in_specs=[whole] * 5 + [anywhere],
        out_specs=(anywhere,) * 3,
        scratch_shapes=[
            pltpu.VMEM(rows.shape, BF16),
            pltpu.VMEM(summed.shape, BF16),
            pltpu.SemaphoreType.DMA((len(offsets),)),
            pltpu.SemaphoreType.DMA,
            pltpu.SemaphoreType.DMA,
        ],
        input_output_aliases={5: 1},
        compiler_params=pltpu.CompilerParams(vmem_limit_bytes=VMEM_BYTES),
        cost_estimate=pl.CostEstimate(flops=0, bytes_accessed=2**20, transcendentals=0),
        name="finish",
    )(total, late, *sums, grad)


def inner_and_outer(local_shard, global_weights, momentum, inputs_here, cotangent):
    depth, kv_width = local_shard.shape
    tokens, width = inputs_here.shape
    size = lax.axis_size("fsdp")
    ring = size // 2
    token_weight = 1.0 / (tokens * size)
    order = ring_order(ring)
    pairs = [(2 * order[at - 1] + side, 2 * order[at] + side) for at in range(ring) for side in (0, 1)]

    def upward(array):
        return lax.ppermute(array, "fsdp", pairs)

    def downward(array):
        return lax.ppermute(array, "fsdp", [(target, source) for source, target in pairs])

    def across(array):
        return lax.ppermute(array, "fsdp", [(at, at ^ 1) for at in range(size)])

    from_below, from_above = upward(local_shard), downward(local_shard)
    partner_cotangent = across(cotangent)
    packed = pack(inputs_here, size, 0)

    bits = lax.axis_size("replica") // 2
    held = send_windows([local_shard], bits, kv_width, (packed,))
    partner_inputs = [across(packed), across(pack(inputs_here, size, 1, (partner_cotangent, from_below)))]

    early_blocks, late_blocks = {0: local_shard, 3: from_below}, {1: from_above, 2: upward(from_below)}
    operands = [inputs_here, cotangent, partner_inputs[0], partner_cotangent]
    first = token_terms(operands, size, [2, 1], BF16, token_weight)
    sum_down, sum_up = downward(first[0]), upward(first[1])
    while bits > 1:
        bits //= 2
        held = send_windows(held, bits, kv_width, first)
    near, leaving = near_grads(cotangent, partner_cotangent, early_blocks, (first[0], held[1]))
    early = across(leaving)
    operands[2] = partner_inputs[1]
    terms = token_terms(operands, size, [3, 0], F32, token_weight, (leaving,))
    totals = near_rows(inputs_here, partner_inputs, {**early_blocks, 1: from_above}, size, (leaving,))
    rows, last, leaving = last_products(
        inputs_here, cotangent, partner_inputs, partner_cotangent, late_blocks, totals, size
    )
    late = across(leaving)
    total_down = vmem_call(
        add_kernel, shape_of(depth, kv_width, BF16), [terms[0], sum_down], 0, "add_terms", (leaving,)
    )
    sum_down = downward(total_down)
    new_share, new_momentum = update_share(held, global_weights, momentum, (total_down, early))
    bits = lax.axis_size("replica")
    shares, joined = [new_share], [0]
    while bits > 1:
        bits //= 2
        shares = [shares[0] if len(shares) == 1 else jnp.concatenate(shares, axis=1)]
        shares.append(swap(shares[0], bits))
        joined += [place ^ bits for place in joined]
    grad, mark = collect([near, last, early], width, size, list(early_blocks), list(late_blocks))
    new_global = join_shares(shares, joined, kv_width, (mark,))
    kv_rows, grad_in, grad_rows = finish(
        rows, late, [terms[1], sum_up, sum_down], grad, size, list(late_blocks)
    )
    return kv_rows, grad_in, grad_rows, new_global, new_momentum


def plain_inner_and_outer(local_shard, global_weights, momentum, inputs_here, cotangent):
    depth, kv_width = local_shard.shape
    token_weight = 1.0 / (inputs_here.shape[0] * lax.axis_size("fsdp"))
    gathered = lax.all_gather(local_shard, "fsdp", axis=0, tiled=True)
    kv_rows = jnp.dot(inputs_here, gathered, preferred_element_type=F32).astype(BF16)
    grad_in = lax.dot_general(cotangent, gathered, (((1,), (1,)), ((), ())), preferred_element_type=F32).astype(BF16)
    terms = lax.dot_general(inputs_here, cotangent, (((0,), (0,)), ((), ())), preferred_element_type=F32)
    grad_rows = lax.psum_scatter(terms * token_weight, "fsdp", scatter_dimension=0, tiled=True).astype(BF16)
    bits = lax.axis_size("replica")
    held = [local_shard]
    while bits > 1:
        bits //= 2
        held = send_windows(held, bits, kv_width, ())
    new_share, new_momentum = update_share(held, global_weights, momentum, ())
    shares, joined = [new_share], [0]
    bits = lax.axis_size("replica")
    while bits > 1:
        bits //= 2
        shares = [jnp.concatenate(shares, axis=1)]
        shares.append(swap(shares[0], bits))
        joined += [place ^ bits for place in joined]
    return kv_rows, grad_in, grad_rows, join_shares(shares, joined, kv_width, ()), new_momentum


def per_device(local_weights, global_weights, momentum, activations, kv_cotangent):
    depth = local_weights.shape[1]
    pairs_fit = lax.axis_size("fsdp") == 8 and depth % LANES == 0 and local_weights.shape[2] % depth == 0
    step = inner_and_outer if pairs_fit else plain_inner_and_outer
    kv_rows, grad_in, grad_rows, new_global, new_momentum = step(
        local_weights[0], global_weights, momentum, activations[0], kv_cotangent[0]
    )
    return kv_rows[None], grad_in[None], grad_rows[None], new_global, new_momentum


def solution(mesh):
    placed = (
        P("replica", "fsdp", None),
        P("fsdp", None),
        P("fsdp", "replica"),
        P("replica", "fsdp", None),
        P("replica", "fsdp", None),
    )
    return jax.shard_map(
        per_device,
        mesh=mesh,
        in_specs=placed,
        out_specs=(
            P("replica", "fsdp", None),
            P("replica", "fsdp", None),
            P("replica", "fsdp", None),
            P("fsdp", None),
            P("fsdp", "replica"),
        ),
        check_vma=False,
    )
```

```python
import functools

import jax
import jax.numpy as jnp
from jax import lax
from jax.experimental import pallas as pl
from jax.experimental.pallas import tpu as pltpu
from jax.sharding import PartitionSpec as P

BLOCK = 64

outer_rate = 0.7
outer_momentum = 0.9
scale_epsilon = 1e-06

F32 = jnp.float32
BF16 = jnp.bfloat16
LANES = 128
VMEM_BYTES = 8 * 2**20


def block_start(offset, size, depth, other=0):
    me = lax.axis_index("fsdp")
    row = lax.rem((me >> 1) + offset + size, size // 2)
    return pl.multiple_of((2 * row + ((me & 1) ^ other)) * depth, depth)


def vmem_call(kernel, out_shape, operands, flops, name, after=(), moved=None):
    def body(*refs):
        kernel(*refs[: len(operands)], *refs[len(operands) + len(after) :])

    moved = moved or sum(x.size * x.dtype.itemsize for x in operands)
    whole = pl.BlockSpec(memory_space=pltpu.VMEM)
    return pl.pallas_call(
        body,
        out_shape=out_shape,
        in_specs=[whole] * len(operands) + [pl.BlockSpec(memory_space=pl.ANY)] * len(after),
        out_specs=jax.tree.map(lambda _: whole, out_shape),
        compiler_params=pltpu.CompilerParams(vmem_limit_bytes=VMEM_BYTES),
        cost_estimate=pl.CostEstimate(flops=flops, bytes_accessed=moved, transcendentals=0),
        name=name,
    )(*operands, *after)


def shape_of(rows, columns, dtype):
    return jax.ShapeDtypeStruct((rows, columns), dtype)


def column_window(array, start, width):
    if isinstance(array, jax.Array):
        return lax.dynamic_slice_in_dim(array, start, width, array.ndim - 1)
    return array[..., pl.ds(pl.multiple_of(start, width), width)]


def outer_kernel(replicas, share_cols, *refs):
    *held_refs, global_ref, momentum_ref, share_ref, new_momentum_ref = refs
    rows, window = held_refs[-1].shape[-2:]
    me = lax.axis_index("replica")

    def windows_of(ref):
        here = me * share_cols // window * window % ref.shape[-1]
        return ref[...] if ref.shape[-1] == window else column_window(ref, here, window)

    old = windows_of(global_ref).astype(F32)
    lane = lax.broadcasted_iota(jnp.int32, (rows, window), 1) // BLOCK
    total = jnp.zeros((rows, window), F32)
    for held_ref in held_refs:
        held = windows_of(held_ref).astype(F32)
        for local in [held] if held.ndim == 2 else list(held):
            drift = old - local
            size = jnp.abs(drift)
            scale = jnp.zeros((rows, window), F32)
            for block in range(window // BLOCK):
                top = jnp.max(jnp.where(lane == block, size, 0.0), axis=1, keepdims=True)
                top = (top + scale_epsilon).astype(BF16).astype(F32)
                scale = jnp.where(lane == block, top, scale)
            total = total + (drift / scale).astype(BF16).astype(F32) * scale
    mean_grad = total / replicas
    shares = window // share_cols
    mean_here, old_here = mean_grad[:, :share_cols], old[:, :share_cols]
    mine = me % shares
    for share in range(1, shares):
        columns = slice(share * share_cols, (share + 1) * share_cols)
        mean_here = jnp.where(mine == share, mean_grad[:, columns], mean_here)
        old_here = jnp.where(mine == share, old[:, columns], old_here)
    new_momentum = outer_momentum * momentum_ref[...] + mean_here
    new_momentum_ref[...] = new_momentum
    share_ref[...] = (old_here - outer_rate * (mean_here + outer_momentum * new_momentum)).astype(BF16)


def swap(array, bits):
    return lax.ppermute(array, "replica", [(at, at ^ bits) for at in range(lax.axis_size("replica"))])


def partner_kernel(bits, share_cols, width, *refs):
    *held_refs, out_ref = refs
    start = (lax.axis_index("replica") ^ bits) * share_cols // width * width
    at = 0
    for held_ref in held_refs:
        part = column_window(held_ref, start % held_ref.shape[-1], width)
        count = 1 if part.ndim == 2 else part.shape[0]
        out_ref[at : at + count] = part.reshape((count,) + part.shape[-2:])
        at += count


def send_windows(held, bits, kv_width, after):
    replicas = lax.axis_size("replica")
    share_cols = kv_width // replicas
    width = max(bits * share_cols, BLOCK)
    rows = held[0].shape[-2]
    count = sum(1 if array.ndim == 2 else array.shape[0] for array in held)
    if width % LANES == 0:
        leaving = vmem_call(
            functools.partial(partner_kernel, bits, share_cols, width),
            jax.ShapeDtypeStruct((count, rows, width), BF16),
            held,
            0,
            "partner_columns",
            after,
        )
    else:
        start = (lax.axis_index("replica") ^ bits) * share_cols // width * width
        parts = [column_window(array, start % array.shape[-1], width).reshape(-1, rows, width) for array in held]
        leaving = jnp.concatenate(parts)
    return held + [swap(leaving, bits)]


def update_share(held, global_weights, momentum, after):
    rows, share_cols = momentum.shape
    replicas = lax.axis_size("replica")
    window = held[-1].shape[-1]
    if window % LANES:
        start = lax.axis_index("replica") * share_cols // window * window
        held = [column_window(array, start % array.shape[-1], window) for array in held]
        global_weights = column_window(global_weights, start, window)
    return vmem_call(
        functools.partial(outer_kernel, replicas, share_cols),
        (shape_of(rows, share_cols, BF16), shape_of(rows, share_cols, F32)),
        held + [global_weights, momentum],
        0,
        "outer_update",
        after,
    )


def join_kernel(places, *refs):
    *held_refs, out_ref = refs
    width = out_ref.shape[1] // len(places)
    me = lax.axis_index("replica")
    at = 0
    for held_ref in held_refs:
        for start in range(0, held_ref.shape[1], width):
            columns = pl.ds(pl.multiple_of((me ^ places[at]) * width, width), width)
            out_ref[:, columns] = held_ref[:, start : start + width]
            at += 1


def join_shares(held, places, kv_width, after):
    rows = held[0].shape[0]
    width = kv_width // len(places)
    if width % LANES == 0:
        return vmem_call(
            functools.partial(join_kernel, places), shape_of(rows, kv_width, BF16), held, 0, "join_shares", after
        )
    whole = jnp.concatenate(held, axis=1)
    joined = jnp.zeros_like(whole)
    for at, place in enumerate(places):
        start = (lax.axis_index("replica") ^ place) * width
        joined = lax.dynamic_update_slice_in_dim(joined, whole[:, at * width : (at + 1) * width], start, 1)
    return joined


PARTNER = {2: (0, 0), 1: (0, 1), 3: (1, 0), 0: (1, 1)}


def pack_kernel(size, part, inputs_ref, out_ref):
    depth = inputs_ref.shape[1] // size
    for offset, (at, slot) in PARTNER.items():
        if at == part:
            out_ref[slot] = inputs_ref[:, pl.ds(block_start(offset, size, depth, 1), depth)]


def pack(inputs_here, size, part, after=()):
    tokens, width = inputs_here.shape
    shape = jax.ShapeDtypeStruct((2, tokens, width // size), BF16)
    return vmem_call(functools.partial(pack_kernel, size, part), shape, [inputs_here], 0, "pack_columns", after)


def terms_kernel(size, offsets, token_weight, inputs_ref, cotangent_ref, partner_ref, partner_cotangent_ref, *out_refs):
    depth = inputs_ref.shape[1] // size
    for offset, out_ref in zip(offsets, out_refs):
        here = inputs_ref[:, pl.ds(block_start(offset, size, depth), depth)]
        there = partner_ref[PARTNER[offset][1]]
        total = 0.0
        for columns, cotangent in ((here, cotangent_ref[...]), (there, partner_cotangent_ref[...])):
            total = total + lax.dot_general(
                columns, cotangent, (((0,), (0,)), ((), ())), preferred_element_type=F32
            )
        out_ref[...] = (total * token_weight).astype(out_ref.dtype)


def token_terms(operands, size, offsets, dtype, token_weight, after=()):
    tokens, width = operands[0].shape
    kv_width = operands[1].shape[1]
    depth = width // size
    return vmem_call(
        functools.partial(terms_kernel, size, offsets, token_weight),
        [shape_of(depth, kv_width, dtype)] * len(offsets),
        operands,
        4 * tokens * depth * len(offsets) * kv_width,
        "token_terms",
        after,
    )


def add_kernel(terms_ref, sum_ref, out_ref):
    out_ref[...] = (terms_ref[...] + sum_ref[...].astype(F32)).astype(BF16)


def back_product(cotangent, block):
    return lax.dot_general(cotangent, block, (((1,), (1,)), ((), ())), preferred_element_type=F32).astype(BF16)


def grads_kernel(cotangent_ref, partner_cotangent_ref, *refs):
    *block_refs, here_ref, leaving_ref = refs
    for number, block_ref in enumerate(block_refs):
        here_ref[number] = back_product(cotangent_ref[...], block_ref[...])
        leaving_ref[number] = back_product(partner_cotangent_ref[...], block_ref[...])


def near_grads(cotangent, partner_cotangent, blocks, after):
    tokens, kv_width = cotangent.shape
    depth = blocks[0].shape[0]
    shape = jax.ShapeDtypeStruct((len(blocks), tokens, depth), BF16)
    operands = [cotangent, partner_cotangent, *blocks.values()]
    flops = 4 * tokens * depth * len(blocks) * kv_width
    return vmem_call(grads_kernel, [shape] * 2, operands, flops, "near_grads", after)


def rows_kernel(size, offsets, inputs_ref, *refs):
    partner_refs, block_refs, (here_ref, there_ref) = refs[:2], refs[2:-2], refs[-2:]
    depth = inputs_ref.shape[1] // size
    here = there = 0.0
    for offset, block_ref in zip(offsets, block_refs):
        at, slot = PARTNER[offset]
        columns = inputs_ref[:, pl.ds(block_start(offset, size, depth), depth)]
        here = here + jnp.dot(columns, block_ref[...], preferred_element_type=F32)
        there = there + jnp.dot(partner_refs[at][slot], block_ref[...], preferred_element_type=F32)
    here_ref[...], there_ref[...] = here, there


def near_rows(inputs_here, partner_inputs, blocks, size, after):
    tokens, kv_width = inputs_here.shape[0], blocks[0].shape[1]
    return vmem_call(
        functools.partial(rows_kernel, size, list(blocks)),
        [shape_of(tokens, kv_width, F32)] * 2,
        [inputs_here, *partner_inputs, *blocks.values()],
        4 * tokens * blocks[0].shape[0] * len(blocks) * kv_width,
        "near_rows",
        after,
    )


def last_kernel(size, offsets, inputs_ref, cotangent_ref, partner_ref, partner_cotangent_ref, *refs):
    block_refs, (here_ref, there_ref, rows_ref, grad_ref, leaving_ref) = refs[: len(offsets)], refs[len(offsets) :]
    depth = block_refs[0].shape[0]
    for number, block_ref in enumerate(block_refs):
        leaving_ref[number] = back_product(partner_cotangent_ref[...], block_ref[...])
    last = block_refs[-1][...]
    there = there_ref[...] + jnp.dot(partner_ref[PARTNER[offsets[-1]][1]], last, preferred_element_type=F32)
    for part in range(there.shape[1] // depth):
        leaving_ref[len(offsets) + part] = there[:, part * depth : (part + 1) * depth].astype(BF16)
    for number, block_ref in enumerate(block_refs):
        grad_ref[number] = back_product(cotangent_ref[...], block_ref[...])
    columns = inputs_ref[:, pl.ds(block_start(offsets[-1], size, depth), depth)]
    rows_ref[...] = here_ref[...] + jnp.dot(columns, last, preferred_element_type=F32)


def last_products(inputs_here, cotangent, partner_inputs, partner_cotangent, blocks, totals, size):
    tokens = inputs_here.shape[0]
    offsets = list(blocks)
    depth, kv_width = blocks[offsets[-1]].shape
    partner = partner_inputs[PARTNER[offsets[-1]][0]]
    return vmem_call(
        functools.partial(last_kernel, size, offsets),
        [
            shape_of(tokens, kv_width, F32),
            jax.ShapeDtypeStruct((len(blocks), tokens, depth), BF16),
            jax.ShapeDtypeStruct((len(blocks) + kv_width // depth, tokens, depth), BF16),
        ],
        [inputs_here, cotangent, partner, partner_cotangent, *blocks.values(), *totals],
        8 * tokens * depth * kv_width,
        "last_products",
    )


def write_columns(size, sources, grad_ref, sems):
    depth = grad_ref.shape[1] // size
    copies = []
    for source_ref, number, offset, other in sources:
        columns = pl.ds(block_start(offset, size, depth, other), depth)
        copies.append(pltpu.make_async_copy(source_ref.at[number], grad_ref.at[:, columns], sems.at[len(copies)]))
        copies[-1].start()
    return copies


def collect_kernel(size, early, late, near_ref, last_ref, early_ref, grad_ref, mark_ref, sems):
    sources = [(near_ref, number, offset, 0) for number, offset in enumerate(early)]
    sources += [(last_ref, number, offset, 0) for number, offset in enumerate(late)]
    sources += [(early_ref, number, offset, 1) for number, offset in enumerate(early)]
    copies = write_columns(size, sources, grad_ref, sems)
    mark_ref[...] = jnp.zeros_like(mark_ref)
    for copy in copies:
        copy.wait()


def collect(grads, width, size, early, late):
    whole, anywhere = pl.BlockSpec(memory_space=pltpu.VMEM), pl.BlockSpec(memory_space=pl.ANY)
    return pl.pallas_call(
        functools.partial(collect_kernel, size, early, late),
        out_shape=(shape_of(grads[0].shape[1], width, BF16), shape_of(8, LANES, F32)),
        in_specs=[whole] * len(grads),
        out_specs=(anywhere, whole),
        scratch_shapes=[pltpu.SemaphoreType.DMA((2 * len(early) + len(late),))],
        compiler_params=pltpu.CompilerParams(vmem_limit_bytes=VMEM_BYTES),
        cost_estimate=pl.CostEstimate(flops=0, bytes_accessed=2**20, transcendentals=0),
        name="collect",
    )(*grads)


def finish_kernel(size, late, total_ref, late_ref, terms_ref, up_ref, down_ref, _, *refs):
    rows_ref, grad_ref, sum_ref, rows_held, sum_held, sems, sem_rows, sem_sum = refs
    copies = write_columns(size, [(late_ref, number, offset, 1) for number, offset in enumerate(late)], grad_ref, sems)
    depth = late_ref.shape[-1]
    for part in range(total_ref.shape[1] // depth):
        columns = slice(part * depth, (part + 1) * depth)
        rows_held[:, columns] = (total_ref[:, columns] + late_ref[len(late) + part].astype(F32)).astype(BF16)
    copies.append(pltpu.make_async_copy(rows_held, rows_ref, sem_rows))
    copies[-1].start()
    sum_held[...] = (terms_ref[...] + up_ref[...].astype(F32) + down_ref[...].astype(F32)).astype(BF16)
    copies.append(pltpu.make_async_copy(sum_held, sum_ref, sem_sum))
    copies[-1].start()
    for copy in copies:
        copy.wait()


def finish(total, late, sums, grad, size, offsets):
    whole, anywhere = pl.BlockSpec(memory_space=pltpu.VMEM), pl.BlockSpec(memory_space=pl.ANY)
    rows, summed = shape_of(*total.shape, BF16), shape_of(*sums[0].shape, BF16)
    return pl.pallas_call(
        functools.partial(finish_kernel, size, offsets),
        out_shape=(rows, shape_of(*grad.shape, BF16), summed),
        in_specs=[whole] * 5 + [anywhere],
        out_specs=(anywhere,) * 3,
        scratch_shapes=[
            pltpu.VMEM(rows.shape, BF16),
            pltpu.VMEM(summed.shape, BF16),
            pltpu.SemaphoreType.DMA((len(offsets),)),
            pltpu.SemaphoreType.DMA,
            pltpu.SemaphoreType.DMA,
        ],
        input_output_aliases={5: 1},
        compiler_params=pltpu.CompilerParams(vmem_limit_bytes=VMEM_BYTES),
        cost_estimate=pl.CostEstimate(flops=0, bytes_accessed=2**20, transcendentals=0),
        name="finish",
    )(total, late, *sums, grad)


def inner_and_outer(local_shard, global_weights, momentum, inputs_here, cotangent):
    depth, kv_width = local_shard.shape
    tokens, width = inputs_here.shape
    size = lax.axis_size("fsdp")
    ring = size // 2
    token_weight = 1.0 / (tokens * size)
    pairs = [(2 * at + side, 2 * ((at + 1) % ring) + side) for at in range(ring) for side in (0, 1)]

    def upward(array):
        return lax.ppermute(array, "fsdp", pairs)

    def downward(array):
        return lax.ppermute(array, "fsdp", [(target, source) for source, target in pairs])

    def across(array):
        return lax.ppermute(array, "fsdp", [(at, at ^ 1) for at in range(size)])

    from_below, from_above = upward(local_shard), downward(local_shard)
    partner_cotangent = across(cotangent)
    packed = pack(inputs_here, size, 0)

    bits = lax.axis_size("replica") // 2
    held = send_windows([local_shard], bits, kv_width, (packed,))
    partner_inputs = [across(packed), across(pack(inputs_here, size, 1, (partner_cotangent, from_below)))]

    early_blocks, late_blocks = {0: local_shard, 3: from_below}, {1: from_above, 2: upward(from_below)}
    operands = [inputs_here, cotangent, partner_inputs[0], partner_cotangent]
    first = token_terms(operands, size, [2, 1], BF16, token_weight)
    sum_down, sum_up = downward(first[0]), upward(first[1])
    while bits > 1:
        bits //= 2
        held = send_windows(held, bits, kv_width, first)
    near, leaving = near_grads(cotangent, partner_cotangent, early_blocks, (first[0], held[1]))
    early = across(leaving)
    operands[2] = partner_inputs[1]
    terms = token_terms(operands, size, [3, 0], F32, token_weight, (leaving,))
    totals = near_rows(inputs_here, partner_inputs, {**early_blocks, 1: from_above}, size, (leaving,))
    rows, last, leaving = last_products(
        inputs_here, cotangent, partner_inputs, partner_cotangent, late_blocks, totals, size
    )
    late = across(leaving)
    total_down = vmem_call(
        add_kernel, shape_of(depth, kv_width, BF16), [terms[0], sum_down], 0, "add_terms", (leaving,)
    )
    sum_down = downward(total_down)
    new_share, new_momentum = update_share(held, global_weights, momentum, (total_down, early))
    bits = lax.axis_size("replica")
    shares, joined = [new_share], [0]
    while bits > 1:
        bits //= 2
        shares = [shares[0] if len(shares) == 1 else jnp.concatenate(shares, axis=1)]
        shares.append(swap(shares[0], bits))
        joined += [place ^ bits for place in joined]
    grad, mark = collect([near, last, early], width, size, list(early_blocks), list(late_blocks))
    new_global = join_shares(shares, joined, kv_width, (mark,))
    kv_rows, grad_in, grad_rows = finish(
        rows, late, [terms[1], sum_up, sum_down], grad, size, list(late_blocks)
    )
    return kv_rows, grad_in, grad_rows, new_global, new_momentum


def plain_inner_and_outer(local_shard, global_weights, momentum, inputs_here, cotangent):
    depth, kv_width = local_shard.shape
    token_weight = 1.0 / (inputs_here.shape[0] * lax.axis_size("fsdp"))
    gathered = lax.all_gather(local_shard, "fsdp", axis=0, tiled=True)
    kv_rows = jnp.dot(inputs_here, gathered, preferred_element_type=F32).astype(BF16)
    grad_in = lax.dot_general(cotangent, gathered, (((1,), (1,)), ((), ())), preferred_element_type=F32).astype(BF16)
    terms = lax.dot_general(inputs_here, cotangent, (((0,), (0,)), ((), ())), preferred_element_type=F32)
    grad_rows = lax.psum_scatter(terms * token_weight, "fsdp", scatter_dimension=0, tiled=True).astype(BF16)
    bits = lax.axis_size("replica")
    held = [local_shard]
    while bits > 1:
        bits //= 2
        held = send_windows(held, bits, kv_width, ())
    new_share, new_momentum = update_share(held, global_weights, momentum, ())
    shares, joined = [new_share], [0]
    bits = lax.axis_size("replica")
    while bits > 1:
        bits //= 2
        shares = [jnp.concatenate(shares, axis=1)]
        shares.append(swap(shares[0], bits))
        joined += [place ^ bits for place in joined]
    return kv_rows, grad_in, grad_rows, join_shares(shares, joined, kv_width, ()), new_momentum


def per_device(local_weights, global_weights, momentum, activations, kv_cotangent):
    depth = local_weights.shape[1]
    pairs_fit = lax.axis_size("fsdp") == 8 and depth % LANES == 0 and local_weights.shape[2] % depth == 0
    step = inner_and_outer if pairs_fit else plain_inner_and_outer
    kv_rows, grad_in, grad_rows, new_global, new_momentum = step(
        local_weights[0], global_weights, momentum, activations[0], kv_cotangent[0]
    )
    return kv_rows[None], grad_in[None], grad_rows[None], new_global, new_momentum


def solution(mesh):
    placed = (
        P("replica", "fsdp", None),
        P("fsdp", None),
        P("fsdp", "replica"),
        P("replica", "fsdp", None),
        P("replica", "fsdp", None),
    )
    return jax.shard_map(
        per_device,
        mesh=mesh,
        in_specs=placed,
        out_specs=(
            P("replica", "fsdp", None),
            P("replica", "fsdp", None),
            P("replica", "fsdp", None),
            P("fsdp", None),
            P("fsdp", "replica"),
        ),
        check_vma=False,
    )
```

```python
import functools

import jax
import jax.numpy as jnp
from jax import lax
from jax.experimental import pallas as pl
from jax.experimental.pallas import tpu as pltpu
from jax.sharding import PartitionSpec as P

BLOCK = 64

outer_rate = 0.7
outer_momentum = 0.9
scale_epsilon = 1e-06

F32 = jnp.float32
BF16 = jnp.bfloat16
LANES = 128
VMEM_BYTES = 8 * 2**20


def ring_order(size):
    return list(range(0, size, 2)) + list(range(1, size, 2))[::-1]


def ring_place(index, size):
    return jnp.where((index & 1) == 0, index >> 1, size - 1 - (index >> 1))


def ring_index(place, size):
    place = lax.rem(place + size, size)
    evens = (size + 1) // 2
    return jnp.where(place < evens, 2 * place, 2 * (size - 1 - place) + 1)


def block_start(offset, size, depth, other=0):
    me = lax.axis_index("fsdp")
    row = ring_index(ring_place(me >> 1, size // 2) + offset, size // 2)
    return pl.multiple_of((2 * row + ((me & 1) ^ other)) * depth, depth)


def vmem_call(kernel, out_shape, operands, flops, name, after=(), moved=None):
    def body(*refs):
        kernel(*refs[: len(operands)], *refs[len(operands) + len(after) :])

    moved = moved or sum(x.size * x.dtype.itemsize for x in operands)
    whole = pl.BlockSpec(memory_space=pltpu.VMEM)
    return pl.pallas_call(
        body,
        out_shape=out_shape,
        in_specs=[whole] * len(operands) + [pl.BlockSpec(memory_space=pl.ANY)] * len(after),
        out_specs=jax.tree.map(lambda _: whole, out_shape),
        compiler_params=pltpu.CompilerParams(vmem_limit_bytes=VMEM_BYTES),
        cost_estimate=pl.CostEstimate(flops=flops, bytes_accessed=moved, transcendentals=0),
        name=name,
    )(*operands, *after)


def shape_of(rows, columns, dtype):
    return jax.ShapeDtypeStruct((rows, columns), dtype)


def column_window(array, start, width):
    if isinstance(array, jax.Array):
        return lax.dynamic_slice_in_dim(array, start, width, array.ndim - 1)
    return array[..., pl.ds(pl.multiple_of(start, width), width)]


def outer_kernel(replicas, share_cols, *refs):
    *held_refs, global_ref, momentum_ref, share_ref, new_momentum_ref = refs
    rows, window = held_refs[-1].shape[-2:]
    me = lax.axis_index("replica")

    def windows_of(ref):
        here = me * share_cols // window * window % ref.shape[-1]
        return ref[...] if ref.shape[-1] == window else column_window(ref, here, window)

    old = windows_of(global_ref).astype(F32)
    lane = lax.broadcasted_iota(jnp.int32, (rows, window), 1) // BLOCK
    total = jnp.zeros((rows, window), F32)
    for held_ref in held_refs:
        held = windows_of(held_ref).astype(F32)
        for local in [held] if held.ndim == 2 else list(held):
            drift = old - local
            size = jnp.abs(drift)
            scale = jnp.zeros((rows, window), F32)
            for block in range(window // BLOCK):
                top = jnp.max(jnp.where(lane == block, size, 0.0), axis=1, keepdims=True)
                top = (top + scale_epsilon).astype(BF16).astype(F32)
                scale = jnp.where(lane == block, top, scale)
            total = total + (drift / scale).astype(BF16).astype(F32) * scale
    mean_grad = total / replicas
    shares = window // share_cols
    mean_here, old_here = mean_grad[:, :share_cols], old[:, :share_cols]
    mine = me % shares
    for share in range(1, shares):
        columns = slice(share * share_cols, (share + 1) * share_cols)
        mean_here = jnp.where(mine == share, mean_grad[:, columns], mean_here)
        old_here = jnp.where(mine == share, old[:, columns], old_here)
    new_momentum = outer_momentum * momentum_ref[...] + mean_here
    new_momentum_ref[...] = new_momentum
    share_ref[...] = (old_here - outer_rate * (mean_here + outer_momentum * new_momentum)).astype(BF16)


def swap(array, bits):
    return lax.ppermute(array, "replica", [(at, at ^ bits) for at in range(lax.axis_size("replica"))])


def partner_kernel(bits, share_cols, width, *refs):
    *held_refs, out_ref = refs
    start = (lax.axis_index("replica") ^ bits) * share_cols // width * width
    at = 0
    for held_ref in held_refs:
        part = column_window(held_ref, start % held_ref.shape[-1], width)
        count = 1 if part.ndim == 2 else part.shape[0]
        out_ref[at : at + count] = part.reshape((count,) + part.shape[-2:])
        at += count


def send_windows(held, bits, kv_width, after):
    replicas = lax.axis_size("replica")
    share_cols = kv_width // replicas
    width = max(bits * share_cols, BLOCK)
    rows = held[0].shape[-2]
    count = sum(1 if array.ndim == 2 else array.shape[0] for array in held)
    if width % LANES == 0:
        leaving = vmem_call(
            functools.partial(partner_kernel, bits, share_cols, width),
            jax.ShapeDtypeStruct((count, rows, width), BF16),
            held,
            0,
            "partner_columns",
            after,
        )
    else:
        start = (lax.axis_index("replica") ^ bits) * share_cols // width * width
        parts = [column_window(array, start % array.shape[-1], width).reshape(-1, rows, width) for array in held]
        leaving = jnp.concatenate(parts)
    return held + [swap(leaving, bits)]


def update_share(held, global_weights, momentum, after):
    rows, share_cols = momentum.shape
    replicas = lax.axis_size("replica")
    window = held[-1].shape[-1]
    if window % LANES:
        start = lax.axis_index("replica") * share_cols // window * window
        held = [column_window(array, start % array.shape[-1], window) for array in held]
        global_weights = column_window(global_weights, start, window)
    return vmem_call(
        functools.partial(outer_kernel, replicas, share_cols),
        (shape_of(rows, share_cols, BF16), shape_of(rows, share_cols, F32)),
        held + [global_weights, momentum],
        0,
        "outer_update",
        after,
    )


def join_kernel(places, *refs):
    *held_refs, out_ref = refs
    width = out_ref.shape[1] // len(places)
    me = lax.axis_index("replica")
    at = 0
    for held_ref in held_refs:
        for start in range(0, held_ref.shape[1], width):
            columns = pl.ds(pl.multiple_of((me ^ places[at]) * width, width), width)
            out_ref[:, columns] = held_ref[:, start : start + width]
            at += 1


def join_shares(held, places, kv_width, after):
    rows = held[0].shape[0]
    width = kv_width // len(places)
    if width % LANES == 0:
        return vmem_call(
            functools.partial(join_kernel, places), shape_of(rows, kv_width, BF16), held, 0, "join_shares", after
        )
    whole = jnp.concatenate(held, axis=1)
    joined = jnp.zeros_like(whole)
    for at, place in enumerate(places):
        start = (lax.axis_index("replica") ^ place) * width
        joined = lax.dynamic_update_slice_in_dim(joined, whole[:, at * width : (at + 1) * width], start, 1)
    return joined


PARTNER = {2: (0, 0), 1: (0, 1), 3: (1, 0), 0: (1, 1)}


def pack_kernel(size, part, inputs_ref, out_ref):
    depth = inputs_ref.shape[1] // size
    for offset, (at, slot) in PARTNER.items():
        if at == part:
            out_ref[slot] = inputs_ref[:, pl.ds(block_start(offset, size, depth, 1), depth)]


def pack(inputs_here, size, part, after=()):
    tokens, width = inputs_here.shape
    shape = jax.ShapeDtypeStruct((2, tokens, width // size), BF16)
    return vmem_call(functools.partial(pack_kernel, size, part), shape, [inputs_here], 0, "pack_columns", after)


def terms_kernel(size, offsets, token_weight, inputs_ref, cotangent_ref, partner_ref, partner_cotangent_ref, *out_refs):
    depth = inputs_ref.shape[1] // size
    for offset, out_ref in zip(offsets, out_refs):
        here = inputs_ref[:, pl.ds(block_start(offset, size, depth), depth)]
        there = partner_ref[PARTNER[offset][1]]
        total = 0.0
        for columns, cotangent in ((here, cotangent_ref[...]), (there, partner_cotangent_ref[...])):
            total = total + lax.dot_general(
                columns, cotangent, (((0,), (0,)), ((), ())), preferred_element_type=F32
            )
        out_ref[...] = (total * token_weight).astype(out_ref.dtype)


def token_terms(operands, size, offsets, dtype, token_weight, after=()):
    tokens, width = operands[0].shape
    kv_width = operands[1].shape[1]
    depth = width // size
    return vmem_call(
        functools.partial(terms_kernel, size, offsets, token_weight),
        [shape_of(depth, kv_width, dtype)] * len(offsets),
        operands,
        4 * tokens * depth * len(offsets) * kv_width,
        "token_terms",
        after,
    )


def add_kernel(terms_ref, sum_ref, out_ref):
    out_ref[...] = (terms_ref[...] + sum_ref[...].astype(F32)).astype(BF16)


def back_product(cotangent, block):
    return lax.dot_general(cotangent, block, (((1,), (1,)), ((), ())), preferred_element_type=F32).astype(BF16)


def grads_kernel(cotangent_ref, partner_cotangent_ref, *refs):
    *block_refs, here_ref, leaving_ref = refs
    for number, block_ref in enumerate(block_refs):
        here_ref[number] = back_product(cotangent_ref[...], block_ref[...])
        leaving_ref[number] = back_product(partner_cotangent_ref[...], block_ref[...])


def near_grads(cotangent, partner_cotangent, blocks, after):
    tokens, kv_width = cotangent.shape
    depth = blocks[0].shape[0]
    shape = jax.ShapeDtypeStruct((len(blocks), tokens, depth), BF16)
    operands = [cotangent, partner_cotangent, *blocks.values()]
    flops = 4 * tokens * depth * len(blocks) * kv_width
    return vmem_call(grads_kernel, [shape] * 2, operands, flops, "near_grads", after)


def rows_kernel(size, offsets, inputs_ref, *refs):
    partner_refs, block_refs, (here_ref, there_ref) = refs[:2], refs[2:-2], refs[-2:]
    depth = inputs_ref.shape[1] // size
    here = there = 0.0
    for offset, block_ref in zip(offsets, block_refs):
        at, slot = PARTNER[offset]
        columns = inputs_ref[:, pl.ds(block_start(offset, size, depth), depth)]
        here = here + jnp.dot(columns, block_ref[...], preferred_element_type=F32)
        there = there + jnp.dot(partner_refs[at][slot], block_ref[...], preferred_element_type=F32)
    here_ref[...], there_ref[...] = here, there


def near_rows(inputs_here, partner_inputs, blocks, size, after):
    tokens, kv_width = inputs_here.shape[0], blocks[0].shape[1]
    return vmem_call(
        functools.partial(rows_kernel, size, list(blocks)),
        [shape_of(tokens, kv_width, F32)] * 2,
        [inputs_here, *partner_inputs, *blocks.values()],
        4 * tokens * blocks[0].shape[0] * len(blocks) * kv_width,
        "near_rows",
        after,
    )


def last_kernel(size, offsets, inputs_ref, cotangent_ref, partner_ref, partner_cotangent_ref, *refs):
    block_refs, (here_ref, there_ref, rows_ref, grad_ref, leaving_ref) = refs[: len(offsets)], refs[len(offsets) :]
    depth = block_refs[0].shape[0]
    for number, block_ref in enumerate(block_refs):
        leaving_ref[number] = back_product(partner_cotangent_ref[...], block_ref[...])
    last = block_refs[-1][...]
    there = there_ref[...] + jnp.dot(partner_ref[PARTNER[offsets[-1]][1]], last, preferred_element_type=F32)
    for part in range(there.shape[1] // depth):
        leaving_ref[len(offsets) + part] = there[:, part * depth : (part + 1) * depth].astype(BF16)
    for number, block_ref in enumerate(block_refs):
        grad_ref[number] = back_product(cotangent_ref[...], block_ref[...])
    columns = inputs_ref[:, pl.ds(block_start(offsets[-1], size, depth), depth)]
    rows_ref[...] = here_ref[...] + jnp.dot(columns, last, preferred_element_type=F32)


def last_products(inputs_here, cotangent, partner_inputs, partner_cotangent, blocks, totals, size):
    tokens = inputs_here.shape[0]
    offsets = list(blocks)
    depth, kv_width = blocks[offsets[-1]].shape
    partner = partner_inputs[PARTNER[offsets[-1]][0]]
    return vmem_call(
        functools.partial(last_kernel, size, offsets),
        [
            shape_of(tokens, kv_width, F32),
            jax.ShapeDtypeStruct((len(blocks), tokens, depth), BF16),
            jax.ShapeDtypeStruct((len(blocks) + kv_width // depth, tokens, depth), BF16),
        ],
        [inputs_here, cotangent, partner, partner_cotangent, *blocks.values(), *totals],
        8 * tokens * depth * kv_width,
        "last_products",
    )


def write_columns(size, sources, grad_ref, sems):
    depth = grad_ref.shape[1] // size
    copies = []
    for source_ref, number, offset, other in sources:
        columns = pl.ds(block_start(offset, size, depth, other), depth)
        copies.append(pltpu.make_async_copy(source_ref.at[number], grad_ref.at[:, columns], sems.at[len(copies)]))
        copies[-1].start()
    return copies


def collect_kernel(size, early, late, near_ref, last_ref, early_ref, grad_ref, mark_ref, sems):
    sources = [(near_ref, number, offset, 0) for number, offset in enumerate(early)]
    sources += [(last_ref, number, offset, 0) for number, offset in enumerate(late)]
    sources += [(early_ref, number, offset, 1) for number, offset in enumerate(early)]
    copies = write_columns(size, sources, grad_ref, sems)
    mark_ref[...] = jnp.zeros_like(mark_ref)
    for copy in copies:
        copy.wait()


def collect(grads, width, size, early, late):
    whole, anywhere = pl.BlockSpec(memory_space=pltpu.VMEM), pl.BlockSpec(memory_space=pl.ANY)
    return pl.pallas_call(
        functools.partial(collect_kernel, size, early, late),
        out_shape=(shape_of(grads[0].shape[1], width, BF16), shape_of(8, LANES, F32)),
        in_specs=[whole] * len(grads),
        out_specs=(anywhere, whole),
        scratch_shapes=[pltpu.SemaphoreType.DMA((2 * len(early) + len(late),))],
        compiler_params=pltpu.CompilerParams(vmem_limit_bytes=VMEM_BYTES),
        cost_estimate=pl.CostEstimate(flops=0, bytes_accessed=2**20, transcendentals=0),
        name="collect",
    )(*grads)


def finish_kernel(size, late, total_ref, late_ref, terms_ref, up_ref, down_ref, _, *refs):
    rows_ref, grad_ref, sum_ref, rows_held, sum_held, sems, sem_rows, sem_sum = refs
    copies = write_columns(size, [(late_ref, number, offset, 1) for number, offset in enumerate(late)], grad_ref, sems)
    depth = late_ref.shape[-1]
    for part in range(total_ref.shape[1] // depth):
        columns = slice(part * depth, (part + 1) * depth)
        rows_held[:, columns] = (total_ref[:, columns] + late_ref[len(late) + part].astype(F32)).astype(BF16)
    copies.append(pltpu.make_async_copy(rows_held, rows_ref, sem_rows))
    copies[-1].start()
    sum_held[...] = (terms_ref[...] + up_ref[...].astype(F32) + down_ref[...].astype(F32)).astype(BF16)
    copies.append(pltpu.make_async_copy(sum_held, sum_ref, sem_sum))
    copies[-1].start()
    for copy in copies:
        copy.wait()


def finish(total, late, sums, grad, size, offsets):
    whole, anywhere = pl.BlockSpec(memory_space=pltpu.VMEM), pl.BlockSpec(memory_space=pl.ANY)
    rows, summed = shape_of(*total.shape, BF16), shape_of(*sums[0].shape, BF16)
    return pl.pallas_call(
        functools.partial(finish_kernel, size, offsets),
        out_shape=(rows, shape_of(*grad.shape, BF16), summed),
        in_specs=[whole] * 5 + [anywhere],
        out_specs=(anywhere,) * 3,
        scratch_shapes=[
            pltpu.VMEM(rows.shape, BF16),
            pltpu.VMEM(summed.shape, BF16),
            pltpu.SemaphoreType.DMA((len(offsets),)),
            pltpu.SemaphoreType.DMA,
            pltpu.SemaphoreType.DMA,
        ],
        input_output_aliases={5: 1},
        compiler_params=pltpu.CompilerParams(vmem_limit_bytes=VMEM_BYTES),
        cost_estimate=pl.CostEstimate(flops=0, bytes_accessed=2**20, transcendentals=0),
        name="finish",
    )(total, late, *sums, grad)


def inner_and_outer(local_shard, global_weights, momentum, inputs_here, cotangent):
    depth, kv_width = local_shard.shape
    tokens, width = inputs_here.shape
    size = lax.axis_size("fsdp")
    ring = size // 2
    token_weight = 1.0 / (tokens * size)
    order = ring_order(ring)
    pairs = [(2 * order[at - 1] + side, 2 * order[at] + side) for at in range(ring) for side in (0, 1)]

    def upward(array):
        return lax.ppermute(array, "fsdp", pairs)

    def downward(array):
        return lax.ppermute(array, "fsdp", [(target, source) for source, target in pairs])

    def across(array):
        return lax.ppermute(array, "fsdp", [(at, at ^ 1) for at in range(size)])

    from_below, from_above = upward(local_shard), downward(local_shard)
    partner_cotangent = across(cotangent)
    packed = pack(inputs_here, size, 0)

    bits = lax.axis_size("replica") // 2
    held = send_windows([local_shard], bits, kv_width, (packed,))
    partner_inputs = [across(packed), across(pack(inputs_here, size, 1, (partner_cotangent, from_below)))]

    early_blocks, late_blocks = {0: local_shard, 3: from_below}, {1: from_above, 2: upward(from_below)}
    operands = [inputs_here, cotangent, partner_inputs[0], partner_cotangent]
    first = token_terms(operands, size, [2, 1], BF16, token_weight)
    sum_down, sum_up = downward(first[0]), upward(first[1])
    while bits > 1:
        bits //= 2
        held = send_windows(held, bits, kv_width, first)
    near, leaving = near_grads(cotangent, partner_cotangent, early_blocks, (first[0], held[1]))
    early = across(leaving)
    operands[2] = partner_inputs[1]
    terms = token_terms(operands, size, [3, 0], F32, token_weight, (leaving,))
    totals = near_rows(inputs_here, partner_inputs, {**early_blocks, 1: from_above}, size, (leaving,))
    rows, last, leaving = last_products(
        inputs_here, cotangent, partner_inputs, partner_cotangent, late_blocks, totals, size
    )
    late = across(leaving)
    total_down = vmem_call(
        add_kernel, shape_of(depth, kv_width, BF16), [terms[0], sum_down], 0, "add_terms", (leaving,)
    )
    sum_down = downward(total_down)
    new_share, new_momentum = update_share(held, global_weights, momentum, (total_down, early, sum_up))
    bits = lax.axis_size("replica")
    shares, joined = [new_share], [0]
    while bits > 1:
        bits //= 2
        shares = [shares[0] if len(shares) == 1 else jnp.concatenate(shares, axis=1)]
        shares.append(swap(shares[0], bits))
        joined += [place ^ bits for place in joined]
    grad, mark = collect([near, last, early], width, size, list(early_blocks), list(late_blocks))
    new_global = join_shares(shares, joined, kv_width, (mark,))
    kv_rows, grad_in, grad_rows = finish(
        rows, late, [terms[1], sum_up, sum_down], grad, size, list(late_blocks)
    )
    return kv_rows, grad_in, grad_rows, new_global, new_momentum


def plain_inner_and_outer(local_shard, global_weights, momentum, inputs_here, cotangent):
    depth, kv_width = local_shard.shape
    token_weight = 1.0 / (inputs_here.shape[0] * lax.axis_size("fsdp"))
    gathered = lax.all_gather(local_shard, "fsdp", axis=0, tiled=True)
    kv_rows = jnp.dot(inputs_here, gathered, preferred_element_type=F32).astype(BF16)
    grad_in = lax.dot_general(cotangent, gathered, (((1,), (1,)), ((), ())), preferred_element_type=F32).astype(BF16)
    terms = lax.dot_general(inputs_here, cotangent, (((0,), (0,)), ((), ())), preferred_element_type=F32)
    grad_rows = lax.psum_scatter(terms * token_weight, "fsdp", scatter_dimension=0, tiled=True).astype(BF16)
    bits = lax.axis_size("replica")
    held = [local_shard]
    while bits > 1:
        bits //= 2
        held = send_windows(held, bits, kv_width, ())
    new_share, new_momentum = update_share(held, global_weights, momentum, ())
    shares, joined = [new_share], [0]
    bits = lax.axis_size("replica")
    while bits > 1:
        bits //= 2
        shares = [jnp.concatenate(shares, axis=1)]
        shares.append(swap(shares[0], bits))
        joined += [place ^ bits for place in joined]
    return kv_rows, grad_in, grad_rows, join_shares(shares, joined, kv_width, ()), new_momentum


def per_device(local_weights, global_weights, momentum, activations, kv_cotangent):
    depth = local_weights.shape[1]
    pairs_fit = lax.axis_size("fsdp") == 8 and depth % LANES == 0 and local_weights.shape[2] % depth == 0
    step = inner_and_outer if pairs_fit else plain_inner_and_outer
    kv_rows, grad_in, grad_rows, new_global, new_momentum = step(
        local_weights[0], global_weights, momentum, activations[0], kv_cotangent[0]
    )
    return kv_rows[None], grad_in[None], grad_rows[None], new_global, new_momentum


def solution(mesh):
    placed = (
        P("replica", "fsdp", None),
        P("fsdp", None),
        P("fsdp", "replica"),
        P("replica", "fsdp", None),
        P("replica", "fsdp", None),
    )
    return jax.shard_map(
        per_device,
        mesh=mesh,
        in_specs=placed,
        out_specs=(
            P("replica", "fsdp", None),
            P("replica", "fsdp", None),
            P("replica", "fsdp", None),
            P("fsdp", None),
            P("fsdp", "replica"),
        ),
        check_vma=False,
    )
```

```python
import functools

import jax
import jax.numpy as jnp
from jax import lax
from jax.experimental import pallas as pl
from jax.experimental.pallas import tpu as pltpu
from jax.sharding import PartitionSpec as P

BLOCK = 64

outer_rate = 0.7
outer_momentum = 0.9
scale_epsilon = 1e-06

F32 = jnp.float32
BF16 = jnp.bfloat16
LANES = 128
VMEM_BYTES = 8 * 2**20


def ring_order(size):
    return list(range(0, size, 2)) + list(range(1, size, 2))[::-1]


def ring_place(index, size):
    return jnp.where((index & 1) == 0, index >> 1, size - 1 - (index >> 1))


def ring_index(place, size):
    place = lax.rem(place + size, size)
    evens = (size + 1) // 2
    return jnp.where(place < evens, 2 * place, 2 * (size - 1 - place) + 1)


def block_start(offset, size, depth, other=0):
    me = lax.axis_index("fsdp")
    row = ring_index(ring_place(me >> 1, size // 2) + offset, size // 2)
    return pl.multiple_of((2 * row + ((me & 1) ^ other)) * depth, depth)


def vmem_call(kernel, out_shape, operands, flops, name, after=(), moved=None):
    def body(*refs):
        kernel(*refs[: len(operands)], *refs[len(operands) + len(after) :])

    moved = moved or sum(x.size * x.dtype.itemsize for x in operands)
    whole = pl.BlockSpec(memory_space=pltpu.VMEM)
    return pl.pallas_call(
        body,
        out_shape=out_shape,
        in_specs=[whole] * len(operands) + [pl.BlockSpec(memory_space=pl.ANY)] * len(after),
        out_specs=jax.tree.map(lambda _: whole, out_shape),
        compiler_params=pltpu.CompilerParams(vmem_limit_bytes=VMEM_BYTES),
        cost_estimate=pl.CostEstimate(flops=flops, bytes_accessed=moved, transcendentals=0),
        name=name,
    )(*operands, *after)


def shape_of(rows, columns, dtype):
    return jax.ShapeDtypeStruct((rows, columns), dtype)


def column_window(array, start, width):
    if isinstance(array, jax.Array):
        return lax.dynamic_slice_in_dim(array, start, width, array.ndim - 1)
    return array[..., pl.ds(pl.multiple_of(start, width), width)]


def outer_kernel(replicas, share_cols, *refs):
    *held_refs, global_ref, momentum_ref, share_ref, new_momentum_ref = refs
    rows, window = held_refs[-1].shape[-2:]
    me = lax.axis_index("replica")

    def windows_of(ref):
        here = me * share_cols // window * window % ref.shape[-1]
        return ref[...] if ref.shape[-1] == window else column_window(ref, here, window)

    old = windows_of(global_ref).astype(F32)
    lane = lax.broadcasted_iota(jnp.int32, (rows, window), 1) // BLOCK
    total = jnp.zeros((rows, window), F32)
    for held_ref in held_refs:
        held = windows_of(held_ref).astype(F32)
        for local in [held] if held.ndim == 2 else list(held):
            drift = old - local
            size = jnp.abs(drift)
            scale = jnp.zeros((rows, window), F32)
            for block in range(window // BLOCK):
                top = jnp.max(jnp.where(lane == block, size, 0.0), axis=1, keepdims=True)
                top = (top + scale_epsilon).astype(BF16).astype(F32)
                scale = jnp.where(lane == block, top, scale)
            total = total + (drift / scale).astype(BF16).astype(F32) * scale
    mean_grad = total / replicas
    shares = window // share_cols
    mean_here, old_here = mean_grad[:, :share_cols], old[:, :share_cols]
    mine = me % shares
    for share in range(1, shares):
        columns = slice(share * share_cols, (share + 1) * share_cols)
        mean_here = jnp.where(mine == share, mean_grad[:, columns], mean_here)
        old_here = jnp.where(mine == share, old[:, columns], old_here)
    new_momentum = outer_momentum * momentum_ref[...] + mean_here
    new_momentum_ref[...] = new_momentum
    share_ref[...] = (old_here - outer_rate * (mean_here + outer_momentum * new_momentum)).astype(BF16)


def swap(array, bits):
    return lax.ppermute(array, "replica", [(at, at ^ bits) for at in range(lax.axis_size("replica"))])


def partner_kernel(bits, share_cols, width, *refs):
    *held_refs, out_ref = refs
    start = (lax.axis_index("replica") ^ bits) * share_cols // width * width
    at = 0
    for held_ref in held_refs:
        part = column_window(held_ref, start % held_ref.shape[-1], width)
        count = 1 if part.ndim == 2 else part.shape[0]
        out_ref[at : at + count] = part.reshape((count,) + part.shape[-2:])
        at += count


def send_windows(held, bits, kv_width, after):
    replicas = lax.axis_size("replica")
    share_cols = kv_width // replicas
    width = max(bits * share_cols, BLOCK)
    rows = held[0].shape[-2]
    count = sum(1 if array.ndim == 2 else array.shape[0] for array in held)
    if width % LANES == 0:
        leaving = vmem_call(
            functools.partial(partner_kernel, bits, share_cols, width),
            jax.ShapeDtypeStruct((count, rows, width), BF16),
            held,
            0,
            "partner_columns",
            after,
        )
    else:
        start = (lax.axis_index("replica") ^ bits) * share_cols // width * width
        parts = [column_window(array, start % array.shape[-1], width).reshape(-1, rows, width) for array in held]
        leaving = jnp.concatenate(parts)
    return held + [swap(leaving, bits)]


def update_share(held, global_weights, momentum, after):
    rows, share_cols = momentum.shape
    replicas = lax.axis_size("replica")
    window = held[-1].shape[-1]
    if window % LANES:
        start = lax.axis_index("replica") * share_cols // window * window
        held = [column_window(array, start % array.shape[-1], window) for array in held]
        global_weights = column_window(global_weights, start, window)
    return vmem_call(
        functools.partial(outer_kernel, replicas, share_cols),
        (shape_of(rows, share_cols, BF16), shape_of(rows, share_cols, F32)),
        held + [global_weights, momentum],
        0,
        "outer_update",
        after,
    )


def join_kernel(places, *refs):
    *held_refs, out_ref = refs
    width = out_ref.shape[1] // len(places)
    me = lax.axis_index("replica")
    at = 0
    for held_ref in held_refs:
        for start in range(0, held_ref.shape[1], width):
            columns = pl.ds(pl.multiple_of((me ^ places[at]) * width, width), width)
            out_ref[:, columns] = held_ref[:, start : start + width]
            at += 1


def beside_kernel(left_ref, right_ref, out_ref):
    width = left_ref.shape[1]
    out_ref[:, :width] = left_ref[...]
    out_ref[:, width:] = right_ref[...]


def beside(left, right, after):
    rows, width = left.shape
    if width % LANES:
        return jnp.concatenate([left, right], axis=1)
    return vmem_call(beside_kernel, shape_of(rows, 2 * width, BF16), [left, right], 0, "beside", after)


def join_shares(held, places, kv_width, after):
    rows = held[0].shape[0]
    width = kv_width // len(places)
    if width % LANES == 0:
        return vmem_call(
            functools.partial(join_kernel, places), shape_of(rows, kv_width, BF16), held, 0, "join_shares", after
        )
    whole = jnp.concatenate(held, axis=1)
    joined = jnp.zeros_like(whole)
    for at, place in enumerate(places):
        start = (lax.axis_index("replica") ^ place) * width
        joined = lax.dynamic_update_slice_in_dim(joined, whole[:, at * width : (at + 1) * width], start, 1)
    return joined


PARTNER = {2: (0, 0), 1: (0, 1), 3: (1, 0), 0: (1, 1)}


def mark_kernel(out_ref):
    out_ref[...] = jnp.zeros_like(out_ref)


def arrived(after):
    return vmem_call(mark_kernel, shape_of(8, LANES, F32), [], 0, "mark", after)


def pack_kernel(size, part, inputs_ref, out_ref):
    depth = inputs_ref.shape[1] // size
    for offset, (at, slot) in PARTNER.items():
        if at == part:
            out_ref[slot] = inputs_ref[:, pl.ds(block_start(offset, size, depth, 1), depth)]


def pack(inputs_here, size, part, after=()):
    tokens, width = inputs_here.shape
    shape = jax.ShapeDtypeStruct((2, tokens, width // size), BF16)
    return vmem_call(functools.partial(pack_kernel, size, part), shape, [inputs_here], 0, "pack_columns", after)


def terms_kernel(size, offsets, token_weight, inputs_ref, cotangent_ref, partner_ref, partner_cotangent_ref, *out_refs):
    depth = inputs_ref.shape[1] // size
    for offset, out_ref in zip(offsets, out_refs):
        here = inputs_ref[:, pl.ds(block_start(offset, size, depth), depth)]
        there = partner_ref[PARTNER[offset][1]]
        total = 0.0
        for columns, cotangent in ((here, cotangent_ref[...]), (there, partner_cotangent_ref[...])):
            total = total + lax.dot_general(
                columns, cotangent, (((0,), (0,)), ((), ())), preferred_element_type=F32
            )
        out_ref[...] = (total * token_weight).astype(out_ref.dtype)


def token_terms(operands, size, offsets, dtype, token_weight, after=()):
    tokens, width = operands[0].shape
    kv_width = operands[1].shape[1]
    depth = width // size
    return vmem_call(
        functools.partial(terms_kernel, size, offsets, token_weight),
        [shape_of(depth, kv_width, dtype)] * len(offsets),
        operands,
        4 * tokens * depth * len(offsets) * kv_width,
        "token_terms",
        after,
    )


def add_kernel(terms_ref, sum_ref, out_ref):
    out_ref[...] = (terms_ref[...] + sum_ref[...].astype(F32)).astype(BF16)


def back_product(cotangent, block):
    return lax.dot_general(cotangent, block, (((1,), (1,)), ((), ())), preferred_element_type=F32).astype(BF16)


def grads_kernel(cotangent_ref, partner_cotangent_ref, *refs):
    *block_refs, here_ref, leaving_ref = refs
    for number, block_ref in enumerate(block_refs):
        here_ref[number] = back_product(cotangent_ref[...], block_ref[...])
        leaving_ref[number] = back_product(partner_cotangent_ref[...], block_ref[...])


def near_grads(cotangent, partner_cotangent, blocks, after):
    tokens, kv_width = cotangent.shape
    depth = blocks[0].shape[0]
    shape = jax.ShapeDtypeStruct((len(blocks), tokens, depth), BF16)
    operands = [cotangent, partner_cotangent, *blocks.values()]
    flops = 4 * tokens * depth * len(blocks) * kv_width
    return vmem_call(grads_kernel, [shape] * 2, operands, flops, "near_grads", after)


def rows_kernel(size, offsets, inputs_ref, *refs):
    partner_refs, block_refs, (here_ref, there_ref) = refs[:2], refs[2:-2], refs[-2:]
    depth = inputs_ref.shape[1] // size
    here = there = 0.0
    for offset, block_ref in zip(offsets, block_refs):
        at, slot = PARTNER[offset]
        columns = inputs_ref[:, pl.ds(block_start(offset, size, depth), depth)]
        here = here + jnp.dot(columns, block_ref[...], preferred_element_type=F32)
        there = there + jnp.dot(partner_refs[at][slot], block_ref[...], preferred_element_type=F32)
    here_ref[...], there_ref[...] = here, there


def near_rows(inputs_here, partner_inputs, blocks, size, after):
    tokens, kv_width = inputs_here.shape[0], blocks[0].shape[1]
    return vmem_call(
        functools.partial(rows_kernel, size, list(blocks)),
        [shape_of(tokens, kv_width, F32)] * 2,
        [inputs_here, *partner_inputs, *blocks.values()],
        4 * tokens * blocks[0].shape[0] * len(blocks) * kv_width,
        "near_rows",
        after,
    )


def last_kernel(size, offsets, inputs_ref, cotangent_ref, partner_ref, partner_cotangent_ref, *refs):
    block_refs, (here_ref, there_ref, rows_ref, grad_ref, leaving_ref) = refs[: len(offsets)], refs[len(offsets) :]
    depth = block_refs[0].shape[0]
    for number, block_ref in enumerate(block_refs):
        leaving_ref[number] = back_product(partner_cotangent_ref[...], block_ref[...])
    last = block_refs[-1][...]
    there = there_ref[...] + jnp.dot(partner_ref[PARTNER[offsets[-1]][1]], last, preferred_element_type=F32)
    for part in range(there.shape[1] // depth):
        leaving_ref[len(offsets) + part] = there[:, part * depth : (part + 1) * depth].astype(BF16)
    for number, block_ref in enumerate(block_refs):
        grad_ref[number] = back_product(cotangent_ref[...], block_ref[...])
    columns = inputs_ref[:, pl.ds(block_start(offsets[-1], size, depth), depth)]
    rows_ref[...] = here_ref[...] + jnp.dot(columns, last, preferred_element_type=F32)


def last_products(inputs_here, cotangent, partner_inputs, partner_cotangent, blocks, totals, size, after):
    tokens = inputs_here.shape[0]
    offsets = list(blocks)
    depth, kv_width = blocks[offsets[-1]].shape
    partner = partner_inputs[PARTNER[offsets[-1]][0]]
    return vmem_call(
        functools.partial(last_kernel, size, offsets),
        [
            shape_of(tokens, kv_width, F32),
            jax.ShapeDtypeStruct((len(blocks), tokens, depth), BF16),
            jax.ShapeDtypeStruct((len(blocks) + kv_width // depth, tokens, depth), BF16),
        ],
        [inputs_here, cotangent, partner, partner_cotangent, *blocks.values(), *totals],
        8 * tokens * depth * kv_width,
        "last_products",
        after,
    )


def write_columns(size, sources, grad_ref, sems):
    depth = grad_ref.shape[1] // size
    copies = []
    for source_ref, number, offset, other in sources:
        columns = pl.ds(block_start(offset, size, depth, other), depth)
        copies.append(pltpu.make_async_copy(source_ref.at[number], grad_ref.at[:, columns], sems.at[len(copies)]))
        copies[-1].start()
    return copies


def collect_kernel(size, early, late, near_ref, last_ref, early_ref, grad_ref, mark_ref, sems):
    sources = [(near_ref, number, offset, 0) for number, offset in enumerate(early)]
    sources += [(last_ref, number, offset, 0) for number, offset in enumerate(late)]
    sources += [(early_ref, number, offset, 1) for number, offset in enumerate(early)]
    copies = write_columns(size, sources, grad_ref, sems)
    mark_ref[...] = jnp.zeros_like(mark_ref)
    for copy in copies:
        copy.wait()


def collect(grads, width, size, early, late):
    whole, anywhere = pl.BlockSpec(memory_space=pltpu.VMEM), pl.BlockSpec(memory_space=pl.ANY)
    return pl.pallas_call(
        functools.partial(collect_kernel, size, early, late),
        out_shape=(shape_of(grads[0].shape[1], width, BF16), shape_of(8, LANES, F32)),
        in_specs=[whole] * len(grads),
        out_specs=(anywhere, whole),
        scratch_shapes=[pltpu.SemaphoreType.DMA((2 * len(early) + len(late),))],
        compiler_params=pltpu.CompilerParams(vmem_limit_bytes=VMEM_BYTES),
        cost_estimate=pl.CostEstimate(flops=0, bytes_accessed=2**20, transcendentals=0),
        name="collect",
    )(*grads)


def finish_kernel(size, late, total_ref, late_ref, terms_ref, up_ref, down_ref, _, *refs):
    rows_ref, grad_ref, sum_ref, rows_held, sum_held, sems, sem_rows, sem_sum = refs
    copies = write_columns(size, [(late_ref, number, offset, 1) for number, offset in enumerate(late)], grad_ref, sems)
    depth = late_ref.shape[-1]
    for part in range(total_ref.shape[1] // depth):
        columns = slice(part * depth, (part + 1) * depth)
        rows_held[:, columns] = (total_ref[:, columns] + late_ref[len(late) + part].astype(F32)).astype(BF16)
    copies.append(pltpu.make_async_copy(rows_held, rows_ref, sem_rows))
    copies[-1].start()
    sum_held[...] = (terms_ref[...] + up_ref[...].astype(F32) + down_ref[...].astype(F32)).astype(BF16)
    copies.append(pltpu.make_async_copy(sum_held, sum_ref, sem_sum))
    copies[-1].start()
    for copy in copies:
        copy.wait()


def finish(total, late, sums, grad, size, offsets):
    whole, anywhere = pl.BlockSpec(memory_space=pltpu.VMEM), pl.BlockSpec(memory_space=pl.ANY)
    rows, summed = shape_of(*total.shape, BF16), shape_of(*sums[0].shape, BF16)
    return pl.pallas_call(
        functools.partial(finish_kernel, size, offsets),
        out_shape=(rows, shape_of(*grad.shape, BF16), summed),
        in_specs=[whole] * 5 + [anywhere],
        out_specs=(anywhere,) * 3,
        scratch_shapes=[
            pltpu.VMEM(rows.shape, BF16),
            pltpu.VMEM(summed.shape, BF16),
            pltpu.SemaphoreType.DMA((len(offsets),)),
            pltpu.SemaphoreType.DMA,
            pltpu.SemaphoreType.DMA,
        ],
        input_output_aliases={5: 1},
        compiler_params=pltpu.CompilerParams(vmem_limit_bytes=VMEM_BYTES),
        cost_estimate=pl.CostEstimate(flops=0, bytes_accessed=2**20, transcendentals=0),
        name="finish",
    )(total, late, *sums, grad)


def inner_and_outer(local_shard, global_weights, momentum, inputs_here, cotangent):
    depth, kv_width = local_shard.shape
    tokens, width = inputs_here.shape
    size = lax.axis_size("fsdp")
    ring = size // 2
    token_weight = 1.0 / (tokens * size)
    order = ring_order(ring)
    pairs = [(2 * order[at - 1] + side, 2 * order[at] + side) for at in range(ring) for side in (0, 1)]

    def upward(array):
        return lax.ppermute(array, "fsdp", pairs)

    def downward(array):
        return lax.ppermute(array, "fsdp", [(target, source) for source, target in pairs])

    def across(array):
        return lax.ppermute(array, "fsdp", [(at, at ^ 1) for at in range(size)])

    from_below, from_above = upward(local_shard), downward(local_shard)
    partner_cotangent = across(cotangent)
    packed = pack(inputs_here, size, 0)

    bits = lax.axis_size("replica") // 2
    held = send_windows([local_shard], bits, kv_width, (packed,))
    partner_inputs = [across(packed), across(pack(inputs_here, size, 1, (partner_cotangent, arrived((from_below,)))))]

    early_blocks, late_blocks = {0: local_shard, 3: from_below}, {1: from_above, 2: upward(from_below)}
    operands = [inputs_here, cotangent, partner_inputs[0], partner_cotangent]
    first = token_terms(operands, size, [2, 1], BF16, token_weight)
    sum_down, sum_up = downward(first[0]), upward(first[1])
    while bits > 1:
        bits //= 2
        held = send_windows(held, bits, kv_width, first)
    near, leaving = near_grads(cotangent, partner_cotangent, early_blocks, (first[0], held[1]))
    early = across(leaving)
    operands[2] = partner_inputs[1]
    terms = token_terms(operands, size, [3, 0], F32, token_weight, (leaving,))
    totals = near_rows(inputs_here, partner_inputs, {**early_blocks, 1: from_above}, size, (leaving,))
    rows, last, leaving = last_products(
        inputs_here, cotangent, partner_inputs, partner_cotangent, late_blocks, totals, size, ()
    )
    late = across(leaving)
    total_down = vmem_call(
        add_kernel, shape_of(depth, kv_width, BF16), [terms[0], sum_down], 0, "add_terms", (leaving, early)
    )
    sum_down = downward(total_down)
    new_share, new_momentum = update_share(held, global_weights, momentum, (total_down,))
    bits = lax.axis_size("replica")
    shares, joined = [new_share], [0]
    while bits > 1:
        bits //= 2
        shares = [shares[0] if len(shares) == 1 else beside(*shares, (sum_up,))]
        shares.append(swap(shares[0], bits))
        joined += [place ^ bits for place in joined]
    grad, mark = collect([near, last, early], width, size, list(early_blocks), list(late_blocks))
    new_global = join_shares(shares, joined, kv_width, (mark,))
    kv_rows, grad_in, grad_rows = finish(
        rows, late, [terms[1], sum_up, sum_down], grad, size, list(late_blocks)
    )
    return kv_rows, grad_in, grad_rows, new_global, new_momentum


def plain_inner_and_outer(local_shard, global_weights, momentum, inputs_here, cotangent):
    depth, kv_width = local_shard.shape
    token_weight = 1.0 / (inputs_here.shape[0] * lax.axis_size("fsdp"))
    gathered = lax.all_gather(local_shard, "fsdp", axis=0, tiled=True)
    kv_rows = jnp.dot(inputs_here, gathered, preferred_element_type=F32).astype(BF16)
    grad_in = lax.dot_general(cotangent, gathered, (((1,), (1,)), ((), ())), preferred_element_type=F32).astype(BF16)
    terms = lax.dot_general(inputs_here, cotangent, (((0,), (0,)), ((), ())), preferred_element_type=F32)
    grad_rows = lax.psum_scatter(terms * token_weight, "fsdp", scatter_dimension=0, tiled=True).astype(BF16)
    bits = lax.axis_size("replica")
    held = [local_shard]
    while bits > 1:
        bits //= 2
        held = send_windows(held, bits, kv_width, ())
    new_share, new_momentum = update_share(held, global_weights, momentum, ())
    shares, joined = [new_share], [0]
    bits = lax.axis_size("replica")
    while bits > 1:
        bits //= 2
        shares = [jnp.concatenate(shares, axis=1)]
        shares.append(swap(shares[0], bits))
        joined += [place ^ bits for place in joined]
    return kv_rows, grad_in, grad_rows, join_shares(shares, joined, kv_width, ()), new_momentum


def per_device(local_weights, global_weights, momentum, activations, kv_cotangent):
    depth = local_weights.shape[1]
    pairs_fit = lax.axis_size("fsdp") == 8 and depth % LANES == 0 and local_weights.shape[2] % depth == 0
    step = inner_and_outer if pairs_fit else plain_inner_and_outer
    kv_rows, grad_in, grad_rows, new_global, new_momentum = step(
        local_weights[0], global_weights, momentum, activations[0], kv_cotangent[0]
    )
    return kv_rows[None], grad_in[None], grad_rows[None], new_global, new_momentum


def solution(mesh):
    placed = (
        P("replica", "fsdp", None),
        P("fsdp", None),
        P("fsdp", "replica"),
        P("replica", "fsdp", None),
        P("replica", "fsdp", None),
    )
    return jax.shard_map(
        per_device,
        mesh=mesh,
        in_specs=placed,
        out_specs=(
            P("replica", "fsdp", None),
            P("replica", "fsdp", None),
            P("replica", "fsdp", None),
            P("fsdp", None),
            P("fsdp", "replica"),
        ),
        check_vma=False,
    )
```

```python
import functools

import jax
import jax.numpy as jnp
from jax import lax
from jax.experimental import pallas as pl
from jax.experimental.pallas import tpu as pltpu
from jax.sharding import PartitionSpec as P

BLOCK = 64

outer_rate = 0.7
outer_momentum = 0.9
scale_epsilon = 1e-06

F32 = jnp.float32
BF16 = jnp.bfloat16
LANES = 128
VMEM_BYTES = 8 * 2**20


def ring_order(size):
    return list(range(0, size, 2)) + list(range(1, size, 2))[::-1]


def ring_place(index, size):
    return jnp.where((index & 1) == 0, index >> 1, size - 1 - (index >> 1))


def ring_index(place, size):
    place = lax.rem(place + size, size)
    evens = (size + 1) // 2
    return jnp.where(place < evens, 2 * place, 2 * (size - 1 - place) + 1)


def block_start(offset, size, depth, other=0):
    me = lax.axis_index("fsdp")
    row = ring_index(ring_place(me >> 1, size // 2) + offset, size // 2)
    return pl.multiple_of((2 * row + ((me & 1) ^ other)) * depth, depth)


def vmem_call(kernel, out_shape, operands, flops, name, after=(), moved=None):
    def body(*refs):
        kernel(*refs[: len(operands)], *refs[len(operands) + len(after) :])

    moved = moved or sum(x.size * x.dtype.itemsize for x in operands)
    whole = pl.BlockSpec(memory_space=pltpu.VMEM)
    return pl.pallas_call(
        body,
        out_shape=out_shape,
        in_specs=[whole] * len(operands) + [pl.BlockSpec(memory_space=pl.ANY)] * len(after),
        out_specs=jax.tree.map(lambda _: whole, out_shape),
        compiler_params=pltpu.CompilerParams(vmem_limit_bytes=VMEM_BYTES),
        cost_estimate=pl.CostEstimate(flops=flops, bytes_accessed=moved, transcendentals=0),
        name=name,
    )(*operands, *after)


def shape_of(rows, columns, dtype):
    return jax.ShapeDtypeStruct((rows, columns), dtype)


def column_window(array, start, width):
    if isinstance(array, jax.Array):
        return lax.dynamic_slice_in_dim(array, start, width, array.ndim - 1)
    return array[..., pl.ds(pl.multiple_of(start, width), width)]


def outer_kernel(replicas, share_cols, *refs):
    *held_refs, global_ref, momentum_ref, share_ref, new_momentum_ref = refs
    rows, window = held_refs[-1].shape[-2:]
    me = lax.axis_index("replica")

    def windows_of(ref):
        here = me * share_cols // window * window % ref.shape[-1]
        return ref[...] if ref.shape[-1] == window else column_window(ref, here, window)

    old = windows_of(global_ref).astype(F32)
    lane = lax.broadcasted_iota(jnp.int32, (rows, window), 1) // BLOCK
    total = jnp.zeros((rows, window), F32)
    for held_ref in held_refs:
        held = windows_of(held_ref).astype(F32)
        for local in [held] if held.ndim == 2 else list(held):
            drift = old - local
            size = jnp.abs(drift)
            scale = jnp.zeros((rows, window), F32)
            for block in range(window // BLOCK):
                top = jnp.max(jnp.where(lane == block, size, 0.0), axis=1, keepdims=True)
                top = (top + scale_epsilon).astype(BF16).astype(F32)
                scale = jnp.where(lane == block, top, scale)
            total = total + (drift / scale).astype(BF16).astype(F32) * scale
    mean_grad = total / replicas
    shares = window // share_cols
    mean_here, old_here = mean_grad[:, :share_cols], old[:, :share_cols]
    mine = me % shares
    for share in range(1, shares):
        columns = slice(share * share_cols, (share + 1) * share_cols)
        mean_here = jnp.where(mine == share, mean_grad[:, columns], mean_here)
        old_here = jnp.where(mine == share, old[:, columns], old_here)
    new_momentum = outer_momentum * momentum_ref[...] + mean_here
    new_momentum_ref[...] = new_momentum
    share_ref[...] = (old_here - outer_rate * (mean_here + outer_momentum * new_momentum)).astype(BF16)


def swap(array, bits):
    return lax.ppermute(array, "replica", [(at, at ^ bits) for at in range(lax.axis_size("replica"))])


def partner_kernel(bits, share_cols, width, *refs):
    *held_refs, out_ref = refs
    start = (lax.axis_index("replica") ^ bits) * share_cols // width * width
    at = 0
    for held_ref in held_refs:
        part = column_window(held_ref, start % held_ref.shape[-1], width)
        count = 1 if part.ndim == 2 else part.shape[0]
        out_ref[at : at + count] = part.reshape((count,) + part.shape[-2:])
        at += count


def send_windows(held, bits, kv_width, after):
    replicas = lax.axis_size("replica")
    share_cols = kv_width // replicas
    width = max(bits * share_cols, BLOCK)
    rows = held[0].shape[-2]
    count = sum(1 if array.ndim == 2 else array.shape[0] for array in held)
    if width % LANES == 0:
        leaving = vmem_call(
            functools.partial(partner_kernel, bits, share_cols, width),
            jax.ShapeDtypeStruct((count, rows, width), BF16),
            held,
            0,
            "partner_columns",
            after,
        )
    else:
        start = (lax.axis_index("replica") ^ bits) * share_cols // width * width
        parts = [column_window(array, start % array.shape[-1], width).reshape(-1, rows, width) for array in held]
        leaving = jnp.concatenate(parts)
    return held + [swap(leaving, bits)]


def update_share(held, global_weights, momentum, after):
    rows, share_cols = momentum.shape
    replicas = lax.axis_size("replica")
    window = held[-1].shape[-1]
    if window % LANES:
        start = lax.axis_index("replica") * share_cols // window * window
        held = [column_window(array, start % array.shape[-1], window) for array in held]
        global_weights = column_window(global_weights, start, window)
    return vmem_call(
        functools.partial(outer_kernel, replicas, share_cols),
        (shape_of(rows, share_cols, BF16), shape_of(rows, share_cols, F32)),
        held + [global_weights, momentum],
        0,
        "outer_update",
        after,
    )


def join_kernel(places, *refs):
    *held_refs, out_ref = refs
    width = out_ref.shape[1] // len(places)
    me = lax.axis_index("replica")
    at = 0
    for held_ref in held_refs:
        for start in range(0, held_ref.shape[1], width):
            columns = pl.ds(pl.multiple_of((me ^ places[at]) * width, width), width)
            out_ref[:, columns] = held_ref[:, start : start + width]
            at += 1


def beside_kernel(left_ref, right_ref, out_ref):
    width = left_ref.shape[1]
    out_ref[:, :width] = left_ref[...]
    out_ref[:, width:] = right_ref[...]


def beside(left, right, after):
    rows, width = left.shape
    if width % LANES:
        return jnp.concatenate([left, right], axis=1)
    return vmem_call(beside_kernel, shape_of(rows, 2 * width, BF16), [left, right], 0, "beside", after)


def join_shares(held, places, kv_width, after):
    rows = held[0].shape[0]
    width = kv_width // len(places)
    if width % LANES == 0:
        return vmem_call(
            functools.partial(join_kernel, places), shape_of(rows, kv_width, BF16), held, 0, "join_shares", after
        )
    whole = jnp.concatenate(held, axis=1)
    joined = jnp.zeros_like(whole)
    for at, place in enumerate(places):
        start = (lax.axis_index("replica") ^ place) * width
        joined = lax.dynamic_update_slice_in_dim(joined, whole[:, at * width : (at + 1) * width], start, 1)
    return joined


PARTNER = {2: (0, 0), 1: (0, 1), 3: (1, 0), 0: (1, 1)}


def mark_kernel(out_ref):
    out_ref[...] = jnp.zeros_like(out_ref)


def arrived(after):
    return vmem_call(mark_kernel, shape_of(8, LANES, F32), [], 0, "mark", after)


def pack_kernel(size, part, inputs_ref, out_ref):
    depth = inputs_ref.shape[1] // size
    for offset, (at, slot) in PARTNER.items():
        if at == part:
            out_ref[slot] = inputs_ref[:, pl.ds(block_start(offset, size, depth, 1), depth)]


def pack(inputs_here, size, part, after=()):
    tokens, width = inputs_here.shape
    shape = jax.ShapeDtypeStruct((2, tokens, width // size), BF16)
    return vmem_call(functools.partial(pack_kernel, size, part), shape, [inputs_here], 0, "pack_columns", after)


def terms_kernel(size, offsets, token_weight, inputs_ref, cotangent_ref, partner_ref, partner_cotangent_ref, *out_refs):
    depth = inputs_ref.shape[1] // size
    for offset, out_ref in zip(offsets, out_refs):
        here = inputs_ref[:, pl.ds(block_start(offset, size, depth), depth)]
        there = partner_ref[PARTNER[offset][1]]
        total = 0.0
        for columns, cotangent in ((here, cotangent_ref[...]), (there, partner_cotangent_ref[...])):
            total = total + lax.dot_general(
                columns, cotangent, (((0,), (0,)), ((), ())), preferred_element_type=F32
            )
        out_ref[...] = (total * token_weight).astype(out_ref.dtype)


def token_terms(operands, size, offsets, dtype, token_weight, after=()):
    tokens, width = operands[0].shape
    kv_width = operands[1].shape[1]
    depth = width // size
    return vmem_call(
        functools.partial(terms_kernel, size, offsets, token_weight),
        [shape_of(depth, kv_width, dtype)] * len(offsets),
        operands,
        4 * tokens * depth * len(offsets) * kv_width,
        "token_terms",
        after,
    )


def add_kernel(terms_ref, sum_ref, out_ref):
    out_ref[...] = (terms_ref[...] + sum_ref[...].astype(F32)).astype(BF16)


def back_product(cotangent, block):
    return lax.dot_general(cotangent, block, (((1,), (1,)), ((), ())), preferred_element_type=F32).astype(BF16)


def grads_kernel(cotangent_ref, partner_cotangent_ref, *refs):
    *block_refs, here_ref, leaving_ref = refs
    for number, block_ref in enumerate(block_refs):
        here_ref[number] = back_product(cotangent_ref[...], block_ref[...])
        leaving_ref[number] = back_product(partner_cotangent_ref[...], block_ref[...])


def near_grads(cotangent, partner_cotangent, blocks, after):
    tokens, kv_width = cotangent.shape
    depth = blocks[0].shape[0]
    shape = jax.ShapeDtypeStruct((len(blocks), tokens, depth), BF16)
    operands = [cotangent, partner_cotangent, *blocks.values()]
    flops = 4 * tokens * depth * len(blocks) * kv_width
    return vmem_call(grads_kernel, [shape] * 2, operands, flops, "near_grads", after)


def rows_kernel(size, offsets, inputs_ref, *refs):
    partner_refs, block_refs, (here_ref, there_ref) = refs[:2], refs[2:-2], refs[-2:]
    depth = inputs_ref.shape[1] // size
    here = there = 0.0
    for offset, block_ref in zip(offsets, block_refs):
        at, slot = PARTNER[offset]
        columns = inputs_ref[:, pl.ds(block_start(offset, size, depth), depth)]
        here = here + jnp.dot(columns, block_ref[...], preferred_element_type=F32)
        there = there + jnp.dot(partner_refs[at][slot], block_ref[...], preferred_element_type=F32)
    here_ref[...], there_ref[...] = here, there


def near_rows(inputs_here, partner_inputs, blocks, size, after):
    tokens, kv_width = inputs_here.shape[0], blocks[0].shape[1]
    return vmem_call(
        functools.partial(rows_kernel, size, list(blocks)),
        [shape_of(tokens, kv_width, F32)] * 2,
        [inputs_here, *partner_inputs, *blocks.values()],
        4 * tokens * blocks[0].shape[0] * len(blocks) * kv_width,
        "near_rows",
        after,
    )


def last_kernel(size, offsets, inputs_ref, cotangent_ref, partner_ref, partner_cotangent_ref, *refs):
    block_refs, (here_ref, there_ref, rows_ref, grad_ref, leaving_ref) = refs[: len(offsets)], refs[len(offsets) :]
    depth = block_refs[0].shape[0]
    for number, block_ref in enumerate(block_refs):
        leaving_ref[number] = back_product(partner_cotangent_ref[...], block_ref[...])
    last = block_refs[-1][...]
    there = there_ref[...] + jnp.dot(partner_ref[PARTNER[offsets[-1]][1]], last, preferred_element_type=F32)
    for part in range(there.shape[1] // depth):
        leaving_ref[len(offsets) + part] = there[:, part * depth : (part + 1) * depth].astype(BF16)
    for number, block_ref in enumerate(block_refs):
        grad_ref[number] = back_product(cotangent_ref[...], block_ref[...])
    columns = inputs_ref[:, pl.ds(block_start(offsets[-1], size, depth), depth)]
    rows_ref[...] = here_ref[...] + jnp.dot(columns, last, preferred_element_type=F32)


def last_products(inputs_here, cotangent, partner_inputs, partner_cotangent, blocks, totals, size, after):
    tokens = inputs_here.shape[0]
    offsets = list(blocks)
    depth, kv_width = blocks[offsets[-1]].shape
    partner = partner_inputs[PARTNER[offsets[-1]][0]]
    return vmem_call(
        functools.partial(last_kernel, size, offsets),
        [
            shape_of(tokens, kv_width, F32),
            jax.ShapeDtypeStruct((len(blocks), tokens, depth), BF16),
            jax.ShapeDtypeStruct((len(blocks) + kv_width // depth, tokens, depth), BF16),
        ],
        [inputs_here, cotangent, partner, partner_cotangent, *blocks.values(), *totals],
        8 * tokens * depth * kv_width,
        "last_products",
        after,
    )


def write_columns(size, sources, grad_ref, sems):
    depth = grad_ref.shape[1] // size
    copies = []
    for source_ref, number, offset, other in sources:
        columns = pl.ds(block_start(offset, size, depth, other), depth)
        copies.append(pltpu.make_async_copy(source_ref.at[number], grad_ref.at[:, columns], sems.at[len(copies)]))
        copies[-1].start()
    return copies


def collect_kernel(size, early, late, near_ref, last_ref, early_ref, *refs):
    grad_ref, mark_ref, sems = refs[-3:]
    sources = [(near_ref, number, offset, 0) for number, offset in enumerate(early)]
    sources += [(last_ref, number, offset, 0) for number, offset in enumerate(late)]
    sources += [(early_ref, number, offset, 1) for number, offset in enumerate(early)]
    copies = write_columns(size, sources, grad_ref, sems)
    mark_ref[...] = jnp.zeros_like(mark_ref)
    for copy in copies:
        copy.wait()


def collect(grads, width, size, early, late, after):
    whole, anywhere = pl.BlockSpec(memory_space=pltpu.VMEM), pl.BlockSpec(memory_space=pl.ANY)
    return pl.pallas_call(
        functools.partial(collect_kernel, size, early, late),
        out_shape=(shape_of(grads[0].shape[1], width, BF16), shape_of(8, LANES, F32)),
        in_specs=[whole] * len(grads) + [anywhere] * len(after),
        out_specs=(anywhere, whole),
        scratch_shapes=[pltpu.SemaphoreType.DMA((2 * len(early) + len(late),))],
        compiler_params=pltpu.CompilerParams(vmem_limit_bytes=VMEM_BYTES),
        cost_estimate=pl.CostEstimate(flops=0, bytes_accessed=2**20, transcendentals=0),
        name="collect",
    )(*grads, *after)


def finish_kernel(size, late, total_ref, late_ref, terms_ref, up_ref, down_ref, _, *refs):
    rows_ref, grad_ref, sum_ref, rows_held, sum_held, sems, sem_rows, sem_sum = refs
    copies = write_columns(size, [(late_ref, number, offset, 1) for number, offset in enumerate(late)], grad_ref, sems)
    depth = late_ref.shape[-1]
    for part in range(total_ref.shape[1] // depth):
        columns = slice(part * depth, (part + 1) * depth)
        rows_held[:, columns] = (total_ref[:, columns] + late_ref[len(late) + part].astype(F32)).astype(BF16)
    copies.append(pltpu.make_async_copy(rows_held, rows_ref, sem_rows))
    copies[-1].start()
    sum_held[...] = (terms_ref[...] + up_ref[...].astype(F32) + down_ref[...].astype(F32)).astype(BF16)
    copies.append(pltpu.make_async_copy(sum_held, sum_ref, sem_sum))
    copies[-1].start()
    for copy in copies:
        copy.wait()


def finish(total, late, sums, grad, size, offsets):
    whole, anywhere = pl.BlockSpec(memory_space=pltpu.VMEM), pl.BlockSpec(memory_space=pl.ANY)
    rows, summed = shape_of(*total.shape, BF16), shape_of(*sums[0].shape, BF16)
    return pl.pallas_call(
        functools.partial(finish_kernel, size, offsets),
        out_shape=(rows, shape_of(*grad.shape, BF16), summed),
        in_specs=[whole] * 5 + [anywhere],
        out_specs=(anywhere,) * 3,
        scratch_shapes=[
            pltpu.VMEM(rows.shape, BF16),
            pltpu.VMEM(summed.shape, BF16),
            pltpu.SemaphoreType.DMA((len(offsets),)),
            pltpu.SemaphoreType.DMA,
            pltpu.SemaphoreType.DMA,
        ],
        input_output_aliases={5: 1},
        compiler_params=pltpu.CompilerParams(vmem_limit_bytes=VMEM_BYTES),
        cost_estimate=pl.CostEstimate(flops=0, bytes_accessed=2**20, transcendentals=0),
        name="finish",
    )(total, late, *sums, grad)


def inner_and_outer(local_shard, global_weights, momentum, inputs_here, cotangent):
    depth, kv_width = local_shard.shape
    tokens, width = inputs_here.shape
    size = lax.axis_size("fsdp")
    ring = size // 2
    token_weight = 1.0 / (tokens * size)
    order = ring_order(ring)
    pairs = [(2 * order[at - 1] + side, 2 * order[at] + side) for at in range(ring) for side in (0, 1)]

    def upward(array):
        return lax.ppermute(array, "fsdp", pairs)

    def downward(array):
        return lax.ppermute(array, "fsdp", [(target, source) for source, target in pairs])

    def across(array):
        return lax.ppermute(array, "fsdp", [(at, at ^ 1) for at in range(size)])

    from_below, from_above = upward(local_shard), downward(local_shard)
    partner_cotangent = across(cotangent)
    packed = pack(inputs_here, size, 0)

    bits = lax.axis_size("replica") // 2
    held = send_windows([local_shard], bits, kv_width, (packed,))
    partner_inputs = [across(packed), across(pack(inputs_here, size, 1, (partner_cotangent, arrived((from_below,)))))]

    early_blocks, late_blocks = {0: local_shard, 3: from_below}, {1: from_above, 2: upward(from_below)}
    operands = [inputs_here, cotangent, partner_inputs[0], partner_cotangent]
    first = token_terms(operands, size, [2, 1], BF16, token_weight)
    sum_down, sum_up = downward(first[0]), upward(first[1])
    while bits > 1:
        bits //= 2
        held = send_windows(held, bits, kv_width, first)
    near, leaving = near_grads(cotangent, partner_cotangent, early_blocks, (first[0], held[1]))
    early = across(leaving)
    operands[2] = partner_inputs[1]
    terms = token_terms(operands, size, [3, 0], F32, token_weight, (leaving,))
    totals = near_rows(inputs_here, partner_inputs, {**early_blocks, 1: from_above}, size, (leaving, held[-1]))
    rows, last, leaving = last_products(
        inputs_here, cotangent, partner_inputs, partner_cotangent, late_blocks, totals, size, ()
    )
    late = across(leaving)
    total_down = vmem_call(
        add_kernel, shape_of(depth, kv_width, BF16), [terms[0], sum_down], 0, "add_terms", (leaving,)
    )
    sum_down = downward(total_down)
    new_share, new_momentum = update_share(held, global_weights, momentum, (total_down, early))
    bits = lax.axis_size("replica")
    shares, joined = [new_share], [0]
    while bits > 1:
        bits //= 2
        shares = [shares[0] if len(shares) == 1 else jnp.concatenate(shares, axis=1)]
        shares.append(swap(shares[0], bits))
        joined += [place ^ bits for place in joined]
    grad, mark = collect([near, last, early], width, size, list(early_blocks), list(late_blocks), ())
    new_global = join_shares(shares, joined, kv_width, (mark,))
    kv_rows, grad_in, grad_rows = finish(
        rows, late, [terms[1], sum_up, sum_down], grad, size, list(late_blocks)
    )
    return kv_rows, grad_in, grad_rows, new_global, new_momentum


def plain_inner_and_outer(local_shard, global_weights, momentum, inputs_here, cotangent):
    depth, kv_width = local_shard.shape
    token_weight = 1.0 / (inputs_here.shape[0] * lax.axis_size("fsdp"))
    gathered = lax.all_gather(local_shard, "fsdp", axis=0, tiled=True)
    kv_rows = jnp.dot(inputs_here, gathered, preferred_element_type=F32).astype(BF16)
    grad_in = lax.dot_general(cotangent, gathered, (((1,), (1,)), ((), ())), preferred_element_type=F32).astype(BF16)
    terms = lax.dot_general(inputs_here, cotangent, (((0,), (0,)), ((), ())), preferred_element_type=F32)
    grad_rows = lax.psum_scatter(terms * token_weight, "fsdp", scatter_dimension=0, tiled=True).astype(BF16)
    bits = lax.axis_size("replica")
    held = [local_shard]
    while bits > 1:
        bits //= 2
        held = send_windows(held, bits, kv_width, ())
    new_share, new_momentum = update_share(held, global_weights, momentum, ())
    shares, joined = [new_share], [0]
    bits = lax.axis_size("replica")
    while bits > 1:
        bits //= 2
        shares = [jnp.concatenate(shares, axis=1)]
        shares.append(swap(shares[0], bits))
        joined += [place ^ bits for place in joined]
    return kv_rows, grad_in, grad_rows, join_shares(shares, joined, kv_width, ()), new_momentum


def per_device(local_weights, global_weights, momentum, activations, kv_cotangent):
    depth = local_weights.shape[1]
    pairs_fit = lax.axis_size("fsdp") == 8 and depth % LANES == 0 and local_weights.shape[2] % depth == 0
    step = inner_and_outer if pairs_fit else plain_inner_and_outer
    kv_rows, grad_in, grad_rows, new_global, new_momentum = step(
        local_weights[0], global_weights, momentum, activations[0], kv_cotangent[0]
    )
    return kv_rows[None], grad_in[None], grad_rows[None], new_global, new_momentum


def solution(mesh):
    placed = (
        P("replica", "fsdp", None),
        P("fsdp", None),
        P("fsdp", "replica"),
        P("replica", "fsdp", None),
        P("replica", "fsdp", None),
    )
    return jax.shard_map(
        per_device,
        mesh=mesh,
        in_specs=placed,
        out_specs=(
            P("replica", "fsdp", None),
            P("replica", "fsdp", None),
            P("replica", "fsdp", None),
            P("fsdp", None),
            P("fsdp", "replica"),
        ),
        check_vma=False,
    )
```

```python
import functools

import jax
import jax.numpy as jnp
from jax import lax
from jax.experimental import pallas as pl
from jax.experimental.pallas import tpu as pltpu
from jax.sharding import PartitionSpec as P

BLOCK = 64

outer_rate = 0.7
outer_momentum = 0.9
scale_epsilon = 1e-06

F32 = jnp.float32
BF16 = jnp.bfloat16
LANES = 128
VMEM_BYTES = 8 * 2**20


def ring_order(size):
    return list(range(0, size, 2)) + list(range(1, size, 2))[::-1]


def ring_place(index, size):
    return jnp.where((index & 1) == 0, index >> 1, size - 1 - (index >> 1))


def ring_index(place, size):
    place = lax.rem(place + size, size)
    evens = (size + 1) // 2
    return jnp.where(place < evens, 2 * place, 2 * (size - 1 - place) + 1)


def block_start(offset, size, depth, other=0):
    me = lax.axis_index("fsdp")
    row = ring_index(ring_place(me >> 1, size // 2) + offset, size // 2)
    return pl.multiple_of((2 * row + ((me & 1) ^ other)) * depth, depth)


def vmem_call(kernel, out_shape, operands, flops, name, after=(), moved=None):
    def body(*refs):
        kernel(*refs[: len(operands)], *refs[len(operands) + len(after) :])

    moved = moved or sum(x.size * x.dtype.itemsize for x in operands)
    whole = pl.BlockSpec(memory_space=pltpu.VMEM)
    return pl.pallas_call(
        body,
        out_shape=out_shape,
        in_specs=[whole] * len(operands) + [pl.BlockSpec(memory_space=pl.ANY)] * len(after),
        out_specs=jax.tree.map(lambda _: whole, out_shape),
        compiler_params=pltpu.CompilerParams(vmem_limit_bytes=VMEM_BYTES),
        cost_estimate=pl.CostEstimate(flops=flops, bytes_accessed=moved, transcendentals=0),
        name=name,
    )(*operands, *after)


def shape_of(rows, columns, dtype):
    return jax.ShapeDtypeStruct((rows, columns), dtype)


def column_window(array, start, width):
    if isinstance(array, jax.Array):
        return lax.dynamic_slice_in_dim(array, start, width, array.ndim - 1)
    return array[..., pl.ds(pl.multiple_of(start, width), width)]


def outer_kernel(replicas, share_cols, *refs):
    *held_refs, global_ref, momentum_ref, share_ref, new_momentum_ref = refs
    rows, window = held_refs[-1].shape[-2:]
    me = lax.axis_index("replica")

    def windows_of(ref):
        here = me * share_cols // window * window % ref.shape[-1]
        return ref[...] if ref.shape[-1] == window else column_window(ref, here, window)

    old = windows_of(global_ref).astype(F32)
    lane = lax.broadcasted_iota(jnp.int32, (rows, window), 1) // BLOCK
    total = jnp.zeros((rows, window), F32)
    for held_ref in held_refs:
        held = windows_of(held_ref).astype(F32)
        for local in [held] if held.ndim == 2 else list(held):
            drift = old - local
            size = jnp.abs(drift)
            scale = jnp.zeros((rows, window), F32)
            for block in range(window // BLOCK):
                top = jnp.max(jnp.where(lane == block, size, 0.0), axis=1, keepdims=True)
                top = (top + scale_epsilon).astype(BF16).astype(F32)
                scale = jnp.where(lane == block, top, scale)
            total = total + (drift / scale).astype(BF16).astype(F32) * scale
    mean_grad = total / replicas
    shares = window // share_cols
    mean_here, old_here = mean_grad[:, :share_cols], old[:, :share_cols]
    mine = me % shares
    for share in range(1, shares):
        columns = slice(share * share_cols, (share + 1) * share_cols)
        mean_here = jnp.where(mine == share, mean_grad[:, columns], mean_here)
        old_here = jnp.where(mine == share, old[:, columns], old_here)
    new_momentum = outer_momentum * momentum_ref[...] + mean_here
    new_momentum_ref[...] = new_momentum
    share_ref[...] = (old_here - outer_rate * (mean_here + outer_momentum * new_momentum)).astype(BF16)


def swap(array, bits):
    return lax.ppermute(array, "replica", [(at, at ^ bits) for at in range(lax.axis_size("replica"))])


def partner_kernel(bits, share_cols, width, *refs):
    *held_refs, out_ref = refs
    start = (lax.axis_index("replica") ^ bits) * share_cols // width * width
    at = 0
    for held_ref in held_refs:
        part = column_window(held_ref, start % held_ref.shape[-1], width)
        count = 1 if part.ndim == 2 else part.shape[0]
        out_ref[at : at + count] = part.reshape((count,) + part.shape[-2:])
        at += count


def send_windows(held, bits, kv_width, after):
    replicas = lax.axis_size("replica")
    share_cols = kv_width // replicas
    width = max(bits * share_cols, BLOCK)
    rows = held[0].shape[-2]
    count = sum(1 if array.ndim == 2 else array.shape[0] for array in held)
    if width % LANES == 0:
        leaving = vmem_call(
            functools.partial(partner_kernel, bits, share_cols, width),
            jax.ShapeDtypeStruct((count, rows, width), BF16),
            held,
            0,
            "partner_columns",
            after,
        )
    else:
        start = (lax.axis_index("replica") ^ bits) * share_cols // width * width
        parts = [column_window(array, start % array.shape[-1], width).reshape(-1, rows, width) for array in held]
        leaving = jnp.concatenate(parts)
    return held + [swap(leaving, bits)]


def update_share(held, global_weights, momentum, after):
    rows, share_cols = momentum.shape
    replicas = lax.axis_size("replica")
    window = held[-1].shape[-1]
    if window % LANES:
        start = lax.axis_index("replica") * share_cols // window * window
        held = [column_window(array, start % array.shape[-1], window) for array in held]
        global_weights = column_window(global_weights, start, window)
    return vmem_call(
        functools.partial(outer_kernel, replicas, share_cols),
        (shape_of(rows, share_cols, BF16), shape_of(rows, share_cols, F32)),
        held + [global_weights, momentum],
        0,
        "outer_update",
        after,
    )


def join_kernel(places, *refs):
    *held_refs, out_ref = refs
    width = out_ref.shape[1] // len(places)
    me = lax.axis_index("replica")
    at = 0
    for held_ref in held_refs:
        for start in range(0, held_ref.shape[1], width):
            columns = pl.ds(pl.multiple_of((me ^ places[at]) * width, width), width)
            out_ref[:, columns] = held_ref[:, start : start + width]
            at += 1


def beside_kernel(left_ref, right_ref, out_ref):
    width = left_ref.shape[1]
    out_ref[:, :width] = left_ref[...]
    out_ref[:, width:] = right_ref[...]


def beside(left, right, after):
    rows, width = left.shape
    if width % LANES:
        return jnp.concatenate([left, right], axis=1)
    return vmem_call(beside_kernel, shape_of(rows, 2 * width, BF16), [left, right], 0, "beside", after)


def join_shares(held, places, kv_width, after):
    rows = held[0].shape[0]
    width = kv_width // len(places)
    if width % LANES == 0:
        return vmem_call(
            functools.partial(join_kernel, places), shape_of(rows, kv_width, BF16), held, 0, "join_shares", after
        )
    whole = jnp.concatenate(held, axis=1)
    joined = jnp.zeros_like(whole)
    for at, place in enumerate(places):
        start = (lax.axis_index("replica") ^ place) * width
        joined = lax.dynamic_update_slice_in_dim(joined, whole[:, at * width : (at + 1) * width], start, 1)
    return joined


PARTNER = {2: (0, 0), 1: (0, 1), 3: (1, 0), 0: (1, 1)}


def mark_kernel(out_ref):
    out_ref[...] = jnp.zeros_like(out_ref)


def arrived(after):
    return vmem_call(mark_kernel, shape_of(8, LANES, F32), [], 0, "mark", after)


def pack_kernel(size, part, inputs_ref, out_ref):
    depth = inputs_ref.shape[1] // size
    for offset, (at, slot) in PARTNER.items():
        if at == part:
            out_ref[slot] = inputs_ref[:, pl.ds(block_start(offset, size, depth, 1), depth)]


def pack(inputs_here, size, part, after=()):
    tokens, width = inputs_here.shape
    shape = jax.ShapeDtypeStruct((2, tokens, width // size), BF16)
    return vmem_call(functools.partial(pack_kernel, size, part), shape, [inputs_here], 0, "pack_columns", after)


def terms_kernel(size, offsets, token_weight, inputs_ref, cotangent_ref, partner_ref, partner_cotangent_ref, *out_refs):
    depth = inputs_ref.shape[1] // size
    for offset, out_ref in zip(offsets, out_refs):
        here = inputs_ref[:, pl.ds(block_start(offset, size, depth), depth)]
        there = partner_ref[PARTNER[offset][1]]
        total = 0.0
        for columns, cotangent in ((here, cotangent_ref[...]), (there, partner_cotangent_ref[...])):
            total = total + lax.dot_general(
                columns, cotangent, (((0,), (0,)), ((), ())), preferred_element_type=F32
            )
        out_ref[...] = (total * token_weight).astype(out_ref.dtype)


def token_terms(operands, size, offsets, dtype, token_weight, after=()):
    tokens, width = operands[0].shape
    kv_width = operands[1].shape[1]
    depth = width // size
    return vmem_call(
        functools.partial(terms_kernel, size, offsets, token_weight),
        [shape_of(depth, kv_width, dtype)] * len(offsets),
        operands,
        4 * tokens * depth * len(offsets) * kv_width,
        "token_terms",
        after,
    )


def add_kernel(terms_ref, sum_ref, out_ref):
    out_ref[...] = (terms_ref[...] + sum_ref[...].astype(F32)).astype(BF16)


def back_product(cotangent, block):
    return lax.dot_general(cotangent, block, (((1,), (1,)), ((), ())), preferred_element_type=F32).astype(BF16)


def grads_kernel(cotangent_ref, partner_cotangent_ref, *refs):
    *block_refs, here_ref, leaving_ref = refs
    for number, block_ref in enumerate(block_refs):
        here_ref[number] = back_product(cotangent_ref[...], block_ref[...])
        leaving_ref[number] = back_product(partner_cotangent_ref[...], block_ref[...])


def near_grads(cotangent, partner_cotangent, blocks, after):
    tokens, kv_width = cotangent.shape
    depth = blocks[0].shape[0]
    shape = jax.ShapeDtypeStruct((len(blocks), tokens, depth), BF16)
    operands = [cotangent, partner_cotangent, *blocks.values()]
    flops = 4 * tokens * depth * len(blocks) * kv_width
    return vmem_call(grads_kernel, [shape] * 2, operands, flops, "near_grads", after)


def rows_kernel(size, offsets, inputs_ref, *refs):
    partner_refs, block_refs, (here_ref, there_ref) = refs[:2], refs[2:-2], refs[-2:]
    depth = inputs_ref.shape[1] // size
    here = there = 0.0
    for offset, block_ref in zip(offsets, block_refs):
        at, slot = PARTNER[offset]
        columns = inputs_ref[:, pl.ds(block_start(offset, size, depth), depth)]
        here = here + jnp.dot(columns, block_ref[...], preferred_element_type=F32)
        there = there + jnp.dot(partner_refs[at][slot], block_ref[...], preferred_element_type=F32)
    here_ref[...], there_ref[...] = here, there


def near_rows(inputs_here, partner_inputs, blocks, size, after):
    tokens, kv_width = inputs_here.shape[0], blocks[0].shape[1]
    return vmem_call(
        functools.partial(rows_kernel, size, list(blocks)),
        [shape_of(tokens, kv_width, F32)] * 2,
        [inputs_here, *partner_inputs, *blocks.values()],
        4 * tokens * blocks[0].shape[0] * len(blocks) * kv_width,
        "near_rows",
        after,
    )


def last_kernel(size, offsets, inputs_ref, cotangent_ref, partner_ref, partner_cotangent_ref, *refs):
    block_refs, (here_ref, there_ref, rows_ref, grad_ref, leaving_ref) = refs[: len(offsets)], refs[len(offsets) :]
    depth = block_refs[0].shape[0]
    for number, block_ref in enumerate(block_refs):
        leaving_ref[number] = back_product(partner_cotangent_ref[...], block_ref[...])
    last = block_refs[-1][...]
    there = there_ref[...] + jnp.dot(partner_ref[PARTNER[offsets[-1]][1]], last, preferred_element_type=F32)
    for part in range(there.shape[1] // depth):
        leaving_ref[len(offsets) + part] = there[:, part * depth : (part + 1) * depth].astype(BF16)
    for number, block_ref in enumerate(block_refs):
        grad_ref[number] = back_product(cotangent_ref[...], block_ref[...])
    columns = inputs_ref[:, pl.ds(block_start(offsets[-1], size, depth), depth)]
    rows_ref[...] = here_ref[...] + jnp.dot(columns, last, preferred_element_type=F32)


def last_products(inputs_here, cotangent, partner_inputs, partner_cotangent, blocks, totals, size, after):
    tokens = inputs_here.shape[0]
    offsets = list(blocks)
    depth, kv_width = blocks[offsets[-1]].shape
    partner = partner_inputs[PARTNER[offsets[-1]][0]]
    return vmem_call(
        functools.partial(last_kernel, size, offsets),
        [
            shape_of(tokens, kv_width, F32),
            jax.ShapeDtypeStruct((len(blocks), tokens, depth), BF16),
            jax.ShapeDtypeStruct((len(blocks) + kv_width // depth, tokens, depth), BF16),
        ],
        [inputs_here, cotangent, partner, partner_cotangent, *blocks.values(), *totals],
        8 * tokens * depth * kv_width,
        "last_products",
        after,
    )


def write_columns(size, sources, grad_ref, sems):
    depth = grad_ref.shape[1] // size
    copies = []
    for source_ref, number, offset, other in sources:
        columns = pl.ds(block_start(offset, size, depth, other), depth)
        copies.append(pltpu.make_async_copy(source_ref.at[number], grad_ref.at[:, columns], sems.at[len(copies)]))
        copies[-1].start()
    return copies


def collect_kernel(size, early, late, near_ref, last_ref, early_ref, *refs):
    grad_ref, mark_ref, sems = refs[-3:]
    sources = [(near_ref, number, offset, 0) for number, offset in enumerate(early)]
    sources += [(last_ref, number, offset, 0) for number, offset in enumerate(late)]
    sources += [(early_ref, number, offset, 1) for number, offset in enumerate(early)]
    copies = write_columns(size, sources, grad_ref, sems)
    mark_ref[...] = jnp.zeros_like(mark_ref)
    for copy in copies:
        copy.wait()


def collect(grads, width, size, early, late, after):
    whole, anywhere = pl.BlockSpec(memory_space=pltpu.VMEM), pl.BlockSpec(memory_space=pl.ANY)
    return pl.pallas_call(
        functools.partial(collect_kernel, size, early, late),
        out_shape=(shape_of(grads[0].shape[1], width, BF16), shape_of(8, LANES, F32)),
        in_specs=[whole] * len(grads) + [anywhere] * len(after),
        out_specs=(anywhere, whole),
        scratch_shapes=[pltpu.SemaphoreType.DMA((2 * len(early) + len(late),))],
        compiler_params=pltpu.CompilerParams(vmem_limit_bytes=VMEM_BYTES),
        cost_estimate=pl.CostEstimate(flops=0, bytes_accessed=2**20, transcendentals=0),
        name="collect",
    )(*grads, *after)


def finish_kernel(size, late, total_ref, late_ref, terms_ref, up_ref, down_ref, _, *refs):
    rows_ref, grad_ref, sum_ref, rows_held, sum_held, sems, sem_rows, sem_sum = refs
    copies = write_columns(size, [(late_ref, number, offset, 1) for number, offset in enumerate(late)], grad_ref, sems)
    depth = late_ref.shape[-1]
    for part in range(total_ref.shape[1] // depth):
        columns = slice(part * depth, (part + 1) * depth)
        rows_held[:, columns] = (total_ref[:, columns] + late_ref[len(late) + part].astype(F32)).astype(BF16)
    copies.append(pltpu.make_async_copy(rows_held, rows_ref, sem_rows))
    copies[-1].start()
    sum_held[...] = (terms_ref[...] + up_ref[...].astype(F32) + down_ref[...].astype(F32)).astype(BF16)
    copies.append(pltpu.make_async_copy(sum_held, sum_ref, sem_sum))
    copies[-1].start()
    for copy in copies:
        copy.wait()


def finish(total, late, sums, grad, size, offsets):
    whole, anywhere = pl.BlockSpec(memory_space=pltpu.VMEM), pl.BlockSpec(memory_space=pl.ANY)
    rows, summed = shape_of(*total.shape, BF16), shape_of(*sums[0].shape, BF16)
    return pl.pallas_call(
        functools.partial(finish_kernel, size, offsets),
        out_shape=(rows, shape_of(*grad.shape, BF16), summed),
        in_specs=[whole] * 5 + [anywhere],
        out_specs=(anywhere,) * 3,
        scratch_shapes=[
            pltpu.VMEM(rows.shape, BF16),
            pltpu.VMEM(summed.shape, BF16),
            pltpu.SemaphoreType.DMA((len(offsets),)),
            pltpu.SemaphoreType.DMA,
            pltpu.SemaphoreType.DMA,
        ],
        input_output_aliases={5: 1},
        compiler_params=pltpu.CompilerParams(vmem_limit_bytes=VMEM_BYTES),
        cost_estimate=pl.CostEstimate(flops=0, bytes_accessed=2**20, transcendentals=0),
        name="finish",
    )(total, late, *sums, grad)


def inner_and_outer(local_shard, global_weights, momentum, inputs_here, cotangent):
    depth, kv_width = local_shard.shape
    tokens, width = inputs_here.shape
    size = lax.axis_size("fsdp")
    ring = size // 2
    token_weight = 1.0 / (tokens * size)
    order = ring_order(ring)
    pairs = [(2 * order[at - 1] + side, 2 * order[at] + side) for at in range(ring) for side in (0, 1)]

    def upward(array):
        return lax.ppermute(array, "fsdp", pairs)

    def downward(array):
        return lax.ppermute(array, "fsdp", [(target, source) for source, target in pairs])

    def across(array):
        return lax.ppermute(array, "fsdp", [(at, at ^ 1) for at in range(size)])

    from_below, from_above = upward(local_shard), downward(local_shard)
    partner_cotangent = across(cotangent)
    packed = pack(inputs_here, size, 0)

    bits = lax.axis_size("replica") // 2
    held = send_windows([local_shard], bits, kv_width, (packed,))
    partner_inputs = [across(packed), across(pack(inputs_here, size, 1, (partner_cotangent, arrived((from_below,)))))]

    early_blocks, late_blocks = {0: local_shard, 3: from_below}, {1: from_above, 2: upward(from_below)}
    operands = [inputs_here, cotangent, partner_inputs[0], partner_cotangent]
    first = token_terms(operands, size, [2, 1], BF16, token_weight)
    sum_down, sum_up = downward(first[0]), upward(first[1])
    while bits > 1:
        bits //= 2
        held = send_windows(held, bits, kv_width, first)
    near, leaving = near_grads(cotangent, partner_cotangent, early_blocks, (first[0], held[1]))
    early = across(leaving)
    operands[2] = partner_inputs[1]
    terms = token_terms(operands, size, [3, 0], F32, token_weight, (leaving,))
    totals = near_rows(inputs_here, partner_inputs, {**early_blocks, 1: from_above}, size, (leaving, arrived((late_blocks[2],))))
    rows, last, leaving = last_products(
        inputs_here, cotangent, partner_inputs, partner_cotangent, late_blocks, totals, size, ()
    )
    late = across(leaving)
    total_down = vmem_call(
        add_kernel, shape_of(depth, kv_width, BF16), [terms[0], sum_down], 0, "add_terms", (leaving,)
    )
    sum_down = downward(total_down)
    new_share, new_momentum = update_share(held, global_weights, momentum, (total_down, early))
    bits = lax.axis_size("replica")
    shares, joined = [new_share], [0]
    while bits > 1:
        bits //= 2
        shares = [shares[0] if len(shares) == 1 else jnp.concatenate(shares, axis=1)]
        shares.append(swap(shares[0], bits))
        joined += [place ^ bits for place in joined]
    grad, mark = collect([near, last, early], width, size, list(early_blocks), list(late_blocks), ())
    new_global = join_shares(shares, joined, kv_width, (mark,))
    kv_rows, grad_in, grad_rows = finish(
        rows, late, [terms[1], sum_up, sum_down], grad, size, list(late_blocks)
    )
    return kv_rows, grad_in, grad_rows, new_global, new_momentum


def plain_inner_and_outer(local_shard, global_weights, momentum, inputs_here, cotangent):
    depth, kv_width = local_shard.shape
    token_weight = 1.0 / (inputs_here.shape[0] * lax.axis_size("fsdp"))
    gathered = lax.all_gather(local_shard, "fsdp", axis=0, tiled=True)
    kv_rows = jnp.dot(inputs_here, gathered, preferred_element_type=F32).astype(BF16)
    grad_in = lax.dot_general(cotangent, gathered, (((1,), (1,)), ((), ())), preferred_element_type=F32).astype(BF16)
    terms = lax.dot_general(inputs_here, cotangent, (((0,), (0,)), ((), ())), preferred_element_type=F32)
    grad_rows = lax.psum_scatter(terms * token_weight, "fsdp", scatter_dimension=0, tiled=True).astype(BF16)
    bits = lax.axis_size("replica")
    held = [local_shard]
    while bits > 1:
        bits //= 2
        held = send_windows(held, bits, kv_width, ())
    new_share, new_momentum = update_share(held, global_weights, momentum, ())
    shares, joined = [new_share], [0]
    bits = lax.axis_size("replica")
    while bits > 1:
        bits //= 2
        shares = [jnp.concatenate(shares, axis=1)]
        shares.append(swap(shares[0], bits))
        joined += [place ^ bits for place in joined]
    return kv_rows, grad_in, grad_rows, join_shares(shares, joined, kv_width, ()), new_momentum


def per_device(local_weights, global_weights, momentum, activations, kv_cotangent):
    depth = local_weights.shape[1]
    pairs_fit = lax.axis_size("fsdp") == 8 and depth % LANES == 0 and local_weights.shape[2] % depth == 0
    step = inner_and_outer if pairs_fit else plain_inner_and_outer
    kv_rows, grad_in, grad_rows, new_global, new_momentum = step(
        local_weights[0], global_weights, momentum, activations[0], kv_cotangent[0]
    )
    return kv_rows[None], grad_in[None], grad_rows[None], new_global, new_momentum


def solution(mesh):
    placed = (
        P("replica", "fsdp", None),
        P("fsdp", None),
        P("fsdp", "replica"),
        P("replica", "fsdp", None),
        P("replica", "fsdp", None),
    )
    return jax.shard_map(
        per_device,
        mesh=mesh,
        in_specs=placed,
        out_specs=(
            P("replica", "fsdp", None),
            P("replica", "fsdp", None),
            P("replica", "fsdp", None),
            P("fsdp", None),
            P("fsdp", "replica"),
        ),
        check_vma=False,
    )
```

```python
import functools

import jax
import jax.numpy as jnp
from jax import lax
from jax.experimental import pallas as pl
from jax.experimental.pallas import tpu as pltpu
from jax.sharding import PartitionSpec as P

BLOCK = 64

outer_rate = 0.7
outer_momentum = 0.9
scale_epsilon = 1e-06

F32 = jnp.float32
BF16 = jnp.bfloat16
LANES = 128
VMEM_BYTES = 8 * 2**20


def ring_order(size):
    return list(range(0, size, 2)) + list(range(1, size, 2))[::-1]


def ring_place(index, size):
    return jnp.where((index & 1) == 0, index >> 1, size - 1 - (index >> 1))


def ring_index(place, size):
    place = lax.rem(place + size, size)
    evens = (size + 1) // 2
    return jnp.where(place < evens, 2 * place, 2 * (size - 1 - place) + 1)


def block_start(offset, size, depth, other=0):
    me = lax.axis_index("fsdp")
    row = ring_index(ring_place(me >> 1, size // 2) + offset, size // 2)
    return pl.multiple_of((2 * row + ((me & 1) ^ other)) * depth, depth)


def vmem_call(kernel, out_shape, operands, flops, name, after=(), moved=None):
    def body(*refs):
        kernel(*refs[: len(operands)], *refs[len(operands) + len(after) :])

    moved = moved or sum(x.size * x.dtype.itemsize for x in operands)
    whole = pl.BlockSpec(memory_space=pltpu.VMEM)
    return pl.pallas_call(
        body,
        out_shape=out_shape,
        in_specs=[whole] * len(operands) + [pl.BlockSpec(memory_space=pl.ANY)] * len(after),
        out_specs=jax.tree.map(lambda _: whole, out_shape),
        compiler_params=pltpu.CompilerParams(vmem_limit_bytes=VMEM_BYTES),
        cost_estimate=pl.CostEstimate(flops=flops, bytes_accessed=moved, transcendentals=0),
        name=name,
    )(*operands, *after)


def shape_of(rows, columns, dtype):
    return jax.ShapeDtypeStruct((rows, columns), dtype)


def column_window(array, start, width):
    if isinstance(array, jax.Array):
        return lax.dynamic_slice_in_dim(array, start, width, array.ndim - 1)
    return array[..., pl.ds(pl.multiple_of(start, width), width)]


def outer_kernel(replicas, share_cols, *refs):
    *held_refs, global_ref, momentum_ref, share_ref, new_momentum_ref = refs
    rows, window = held_refs[-1].shape[-2:]
    me = lax.axis_index("replica")

    def windows_of(ref):
        here = me * share_cols // window * window % ref.shape[-1]
        return ref[...] if ref.shape[-1] == window else column_window(ref, here, window)

    old = windows_of(global_ref).astype(F32)
    lane = lax.broadcasted_iota(jnp.int32, (rows, window), 1) // BLOCK
    total = jnp.zeros((rows, window), F32)
    for held_ref in held_refs:
        held = windows_of(held_ref).astype(F32)
        for local in [held] if held.ndim == 2 else list(held):
            drift = old - local
            size = jnp.abs(drift)
            scale = jnp.zeros((rows, window), F32)
            for block in range(window // BLOCK):
                top = jnp.max(jnp.where(lane == block, size, 0.0), axis=1, keepdims=True)
                top = (top + scale_epsilon).astype(BF16).astype(F32)
                scale = jnp.where(lane == block, top, scale)
            total = total + (drift / scale).astype(BF16).astype(F32) * scale
    mean_grad = total / replicas
    shares = window // share_cols
    mean_here, old_here = mean_grad[:, :share_cols], old[:, :share_cols]
    mine = me % shares
    for share in range(1, shares):
        columns = slice(share * share_cols, (share + 1) * share_cols)
        mean_here = jnp.where(mine == share, mean_grad[:, columns], mean_here)
        old_here = jnp.where(mine == share, old[:, columns], old_here)
    new_momentum = outer_momentum * momentum_ref[...] + mean_here
    new_momentum_ref[...] = new_momentum
    share_ref[...] = (old_here - outer_rate * (mean_here + outer_momentum * new_momentum)).astype(BF16)


def swap(array, bits):
    return lax.ppermute(array, "replica", [(at, at ^ bits) for at in range(lax.axis_size("replica"))])


def partner_kernel(bits, share_cols, width, *refs):
    *held_refs, out_ref = refs
    start = (lax.axis_index("replica") ^ bits) * share_cols // width * width
    at = 0
    for held_ref in held_refs:
        part = column_window(held_ref, start % held_ref.shape[-1], width)
        count = 1 if part.ndim == 2 else part.shape[0]
        out_ref[at : at + count] = part.reshape((count,) + part.shape[-2:])
        at += count


def send_windows(held, bits, kv_width, after):
    replicas = lax.axis_size("replica")
    share_cols = kv_width // replicas
    width = max(bits * share_cols, BLOCK)
    rows = held[0].shape[-2]
    count = sum(1 if array.ndim == 2 else array.shape[0] for array in held)
    if width % LANES == 0:
        leaving = vmem_call(
            functools.partial(partner_kernel, bits, share_cols, width),
            jax.ShapeDtypeStruct((count, rows, width), BF16),
            held,
            0,
            "partner_columns",
            after,
        )
    else:
        start = (lax.axis_index("replica") ^ bits) * share_cols // width * width
        parts = [column_window(array, start % array.shape[-1], width).reshape(-1, rows, width) for array in held]
        leaving = jnp.concatenate(parts)
    return held + [swap(leaving, bits)]


def update_share(held, global_weights, momentum, after):
    rows, share_cols = momentum.shape
    replicas = lax.axis_size("replica")
    window = held[-1].shape[-1]
    if window % LANES:
        start = lax.axis_index("replica") * share_cols // window * window
        held = [column_window(array, start % array.shape[-1], window) for array in held]
        global_weights = column_window(global_weights, start, window)
    return vmem_call(
        functools.partial(outer_kernel, replicas, share_cols),
        (shape_of(rows, share_cols, BF16), shape_of(rows, share_cols, F32)),
        held + [global_weights, momentum],
        0,
        "outer_update",
        after,
    )


def join_kernel(places, *refs):
    *held_refs, out_ref = refs
    width = out_ref.shape[1] // len(places)
    me = lax.axis_index("replica")
    at = 0
    for held_ref in held_refs:
        for start in range(0, held_ref.shape[1], width):
            columns = pl.ds(pl.multiple_of((me ^ places[at]) * width, width), width)
            out_ref[:, columns] = held_ref[:, start : start + width]
            at += 1


def beside_kernel(left_ref, right_ref, out_ref):
    width = left_ref.shape[1]
    out_ref[:, :width] = left_ref[...]
    out_ref[:, width:] = right_ref[...]


def beside(left, right, after):
    rows, width = left.shape
    if width % LANES:
        return jnp.concatenate([left, right], axis=1)
    return vmem_call(beside_kernel, shape_of(rows, 2 * width, BF16), [left, right], 0, "beside", after)


def join_shares(held, places, kv_width, after):
    rows = held[0].shape[0]
    width = kv_width // len(places)
    if width % LANES == 0:
        return vmem_call(
            functools.partial(join_kernel, places), shape_of(rows, kv_width, BF16), held, 0, "join_shares", after
        )
    whole = jnp.concatenate(held, axis=1)
    joined = jnp.zeros_like(whole)
    for at, place in enumerate(places):
        start = (lax.axis_index("replica") ^ place) * width
        joined = lax.dynamic_update_slice_in_dim(joined, whole[:, at * width : (at + 1) * width], start, 1)
    return joined


PARTNER = {2: (0, 0), 1: (0, 1), 3: (1, 0), 0: (1, 1)}


def mark_kernel(out_ref):
    out_ref[...] = jnp.zeros_like(out_ref)


def arrived(after):
    return vmem_call(mark_kernel, shape_of(8, LANES, F32), [], 0, "mark", after)


def pack_kernel(size, part, inputs_ref, out_ref):
    depth = inputs_ref.shape[1] // size
    for offset, (at, slot) in PARTNER.items():
        if at == part:
            out_ref[slot] = inputs_ref[:, pl.ds(block_start(offset, size, depth, 1), depth)]


def pack(inputs_here, size, part, after=()):
    tokens, width = inputs_here.shape
    shape = jax.ShapeDtypeStruct((2, tokens, width // size), BF16)
    return vmem_call(functools.partial(pack_kernel, size, part), shape, [inputs_here], 0, "pack_columns", after)


def terms_kernel(size, offsets, token_weight, inputs_ref, cotangent_ref, partner_ref, partner_cotangent_ref, *out_refs):
    depth = inputs_ref.shape[1] // size
    for offset, out_ref in zip(offsets, out_refs):
        here = inputs_ref[:, pl.ds(block_start(offset, size, depth), depth)]
        there = partner_ref[PARTNER[offset][1]]
        total = 0.0
        for columns, cotangent in ((here, cotangent_ref[...]), (there, partner_cotangent_ref[...])):
            total = total + lax.dot_general(
                columns, cotangent, (((0,), (0,)), ((), ())), preferred_element_type=F32
            )
        out_ref[...] = (total * token_weight).astype(out_ref.dtype)


def token_terms(operands, size, offsets, dtype, token_weight, after=()):
    tokens, width = operands[0].shape
    kv_width = operands[1].shape[1]
    depth = width // size
    return vmem_call(
        functools.partial(terms_kernel, size, offsets, token_weight),
        [shape_of(depth, kv_width, dtype)] * len(offsets),
        operands,
        4 * tokens * depth * len(offsets) * kv_width,
        "token_terms",
        after,
    )


def add_kernel(terms_ref, sum_ref, out_ref):
    out_ref[...] = (terms_ref[...] + sum_ref[...].astype(F32)).astype(BF16)


def back_product(cotangent, block):
    return lax.dot_general(cotangent, block, (((1,), (1,)), ((), ())), preferred_element_type=F32).astype(BF16)


def grads_kernel(cotangent_ref, partner_cotangent_ref, *refs):
    *block_refs, here_ref, leaving_ref = refs
    for number, block_ref in enumerate(block_refs):
        here_ref[number] = back_product(cotangent_ref[...], block_ref[...])
        leaving_ref[number] = back_product(partner_cotangent_ref[...], block_ref[...])


def near_grads(cotangent, partner_cotangent, blocks, after):
    tokens, kv_width = cotangent.shape
    depth = blocks[0].shape[0]
    shape = jax.ShapeDtypeStruct((len(blocks), tokens, depth), BF16)
    operands = [cotangent, partner_cotangent, *blocks.values()]
    flops = 4 * tokens * depth * len(blocks) * kv_width
    return vmem_call(grads_kernel, [shape] * 2, operands, flops, "near_grads", after)


def rows_kernel(size, offsets, inputs_ref, *refs):
    partner_refs, block_refs, (here_ref, there_ref) = refs[:2], refs[2:-2], refs[-2:]
    depth = inputs_ref.shape[1] // size
    here = there = 0.0
    for offset, block_ref in zip(offsets, block_refs):
        at, slot = PARTNER[offset]
        columns = inputs_ref[:, pl.ds(block_start(offset, size, depth), depth)]
        here = here + jnp.dot(columns, block_ref[...], preferred_element_type=F32)
        there = there + jnp.dot(partner_refs[at][slot], block_ref[...], preferred_element_type=F32)
    here_ref[...], there_ref[...] = here, there


def near_rows(inputs_here, partner_inputs, blocks, size, after):
    tokens, kv_width = inputs_here.shape[0], blocks[0].shape[1]
    return vmem_call(
        functools.partial(rows_kernel, size, list(blocks)),
        [shape_of(tokens, kv_width, F32)] * 2,
        [inputs_here, *partner_inputs, *blocks.values()],
        4 * tokens * blocks[0].shape[0] * len(blocks) * kv_width,
        "near_rows",
        after,
    )


def last_kernel(size, offsets, inputs_ref, cotangent_ref, partner_ref, partner_cotangent_ref, *refs):
    block_refs, (here_ref, there_ref, rows_ref, grad_ref, leaving_ref) = refs[: len(offsets)], refs[len(offsets) :]
    depth = block_refs[0].shape[0]
    for number, block_ref in enumerate(block_refs):
        leaving_ref[number] = back_product(partner_cotangent_ref[...], block_ref[...])
    last = block_refs[-1][...]
    there = there_ref[...] + jnp.dot(partner_ref[PARTNER[offsets[-1]][1]], last, preferred_element_type=F32)
    for part in range(there.shape[1] // depth):
        leaving_ref[len(offsets) + part] = there[:, part * depth : (part + 1) * depth].astype(BF16)
    for number, block_ref in enumerate(block_refs):
        grad_ref[number] = back_product(cotangent_ref[...], block_ref[...])
    columns = inputs_ref[:, pl.ds(block_start(offsets[-1], size, depth), depth)]
    rows_ref[...] = here_ref[...] + jnp.dot(columns, last, preferred_element_type=F32)


def last_products(inputs_here, cotangent, partner_inputs, partner_cotangent, blocks, totals, size, after):
    tokens = inputs_here.shape[0]
    offsets = list(blocks)
    depth, kv_width = blocks[offsets[-1]].shape
    partner = partner_inputs[PARTNER[offsets[-1]][0]]
    return vmem_call(
        functools.partial(last_kernel, size, offsets),
        [
            shape_of(tokens, kv_width, F32),
            jax.ShapeDtypeStruct((len(blocks), tokens, depth), BF16),
            jax.ShapeDtypeStruct((len(blocks) + kv_width // depth, tokens, depth), BF16),
        ],
        [inputs_here, cotangent, partner, partner_cotangent, *blocks.values(), *totals],
        8 * tokens * depth * kv_width,
        "last_products",
        after,
    )


def write_columns(size, sources, grad_ref, sems):
    depth = grad_ref.shape[1] // size
    copies = []
    for source_ref, number, offset, other in sources:
        columns = pl.ds(block_start(offset, size, depth, other), depth)
        copies.append(pltpu.make_async_copy(source_ref.at[number], grad_ref.at[:, columns], sems.at[len(copies)]))
        copies[-1].start()
    return copies


def collect_kernel(size, early, late, near_ref, last_ref, early_ref, *refs):
    grad_ref, mark_ref, sems = refs[-3:]
    sources = [(near_ref, number, offset, 0) for number, offset in enumerate(early)]
    sources += [(last_ref, number, offset, 0) for number, offset in enumerate(late)]
    sources += [(early_ref, number, offset, 1) for number, offset in enumerate(early)]
    copies = write_columns(size, sources, grad_ref, sems)
    mark_ref[...] = jnp.zeros_like(mark_ref)
    for copy in copies:
        copy.wait()


def collect(grads, width, size, early, late, after):
    whole, anywhere = pl.BlockSpec(memory_space=pltpu.VMEM), pl.BlockSpec(memory_space=pl.ANY)
    return pl.pallas_call(
        functools.partial(collect_kernel, size, early, late),
        out_shape=(shape_of(grads[0].shape[1], width, BF16), shape_of(8, LANES, F32)),
        in_specs=[whole] * len(grads) + [anywhere] * len(after),
        out_specs=(anywhere, whole),
        scratch_shapes=[pltpu.SemaphoreType.DMA((2 * len(early) + len(late),))],
        compiler_params=pltpu.CompilerParams(vmem_limit_bytes=VMEM_BYTES),
        cost_estimate=pl.CostEstimate(flops=0, bytes_accessed=2**20, transcendentals=0),
        name="collect",
    )(*grads, *after)


def finish_kernel(size, late, total_ref, late_ref, terms_ref, up_ref, down_ref, _, *refs):
    rows_ref, grad_ref, sum_ref, rows_held, sum_held, sems, sem_rows, sem_sum = refs
    copies = write_columns(size, [(late_ref, number, offset, 1) for number, offset in enumerate(late)], grad_ref, sems)
    depth = late_ref.shape[-1]
    for part in range(total_ref.shape[1] // depth):
        columns = slice(part * depth, (part + 1) * depth)
        rows_held[:, columns] = (total_ref[:, columns] + late_ref[len(late) + part].astype(F32)).astype(BF16)
    copies.append(pltpu.make_async_copy(rows_held, rows_ref, sem_rows))
    copies[-1].start()
    sum_held[...] = (terms_ref[...] + up_ref[...].astype(F32) + down_ref[...].astype(F32)).astype(BF16)
    copies.append(pltpu.make_async_copy(sum_held, sum_ref, sem_sum))
    copies[-1].start()
    for copy in copies:
        copy.wait()


def finish(total, late, sums, grad, size, offsets):
    whole, anywhere = pl.BlockSpec(memory_space=pltpu.VMEM), pl.BlockSpec(memory_space=pl.ANY)
    rows, summed = shape_of(*total.shape, BF16), shape_of(*sums[0].shape, BF16)
    return pl.pallas_call(
        functools.partial(finish_kernel, size, offsets),
        out_shape=(rows, shape_of(*grad.shape, BF16), summed),
        in_specs=[whole] * 5 + [anywhere],
        out_specs=(anywhere,) * 3,
        scratch_shapes=[
            pltpu.VMEM(rows.shape, BF16),
            pltpu.VMEM(summed.shape, BF16),
            pltpu.SemaphoreType.DMA((len(offsets),)),
            pltpu.SemaphoreType.DMA,
            pltpu.SemaphoreType.DMA,
        ],
        input_output_aliases={5: 1},
        compiler_params=pltpu.CompilerParams(vmem_limit_bytes=VMEM_BYTES),
        cost_estimate=pl.CostEstimate(flops=0, bytes_accessed=2**20, transcendentals=0),
        name="finish",
    )(total, late, *sums, grad)


def inner_and_outer(local_shard, global_weights, momentum, inputs_here, cotangent):
    depth, kv_width = local_shard.shape
    tokens, width = inputs_here.shape
    size = lax.axis_size("fsdp")
    ring = size // 2
    token_weight = 1.0 / (tokens * size)
    order = ring_order(ring)
    pairs = [(2 * order[at - 1] + side, 2 * order[at] + side) for at in range(ring) for side in (0, 1)]

    def upward(array):
        return lax.ppermute(array, "fsdp", pairs)

    def downward(array):
        return lax.ppermute(array, "fsdp", [(target, source) for source, target in pairs])

    def across(array):
        return lax.ppermute(array, "fsdp", [(at, at ^ 1) for at in range(size)])

    from_below, from_above = upward(local_shard), downward(local_shard)
    partner_cotangent = across(cotangent)
    packed = pack(inputs_here, size, 0)

    bits = lax.axis_size("replica") // 2
    held = send_windows([local_shard], bits, kv_width, (packed,))
    partner_inputs = [across(packed), across(pack(inputs_here, size, 1, (partner_cotangent, arrived((from_below,)))))]

    early_blocks, late_blocks = {0: local_shard, 3: from_below}, {1: from_above, 2: upward(from_below)}
    operands = [inputs_here, cotangent, partner_inputs[0], partner_cotangent]
    first = token_terms(operands, size, [2, 1], BF16, token_weight)
    sum_down, sum_up = downward(first[0]), upward(first[1])
    while bits > 1:
        bits //= 2
        held = send_windows(held, bits, kv_width, first)
    near, leaving = near_grads(cotangent, partner_cotangent, early_blocks, (first[0], held[1]))
    early = across(leaving)
    operands[2] = partner_inputs[1]
    terms = token_terms(operands, size, [3, 0], F32, token_weight, (leaving,))
    totals = near_rows(inputs_here, partner_inputs, {**early_blocks, 1: from_above}, size, (leaving, held[-1], arrived((late_blocks[2],))))
    rows, last, leaving = last_products(
        inputs_here, cotangent, partner_inputs, partner_cotangent, late_blocks, totals, size, ()
    )
    late = across(leaving)
    total_down = vmem_call(
        add_kernel, shape_of(depth, kv_width, BF16), [terms[0], sum_down], 0, "add_terms", (leaving,)
    )
    sum_down = downward(total_down)
    new_share, new_momentum = update_share(held, global_weights, momentum, (total_down, early, sum_up))
    bits = lax.axis_size("replica")
    shares, joined = [new_share], [0]
    while bits > 1:
        bits //= 2
        shares = [shares[0] if len(shares) == 1 else jnp.concatenate(shares, axis=1)]
        shares.append(swap(shares[0], bits))
        joined += [place ^ bits for place in joined]
    grad, mark = collect([near, last, early], width, size, list(early_blocks), list(late_blocks), ())
    new_global = join_shares(shares, joined, kv_width, (mark,))
    kv_rows, grad_in, grad_rows = finish(
        rows, late, [terms[1], sum_up, sum_down], grad, size, list(late_blocks)
    )
    return kv_rows, grad_in, grad_rows, new_global, new_momentum


def plain_inner_and_outer(local_shard, global_weights, momentum, inputs_here, cotangent):
    depth, kv_width = local_shard.shape
    token_weight = 1.0 / (inputs_here.shape[0] * lax.axis_size("fsdp"))
    gathered = lax.all_gather(local_shard, "fsdp", axis=0, tiled=True)
    kv_rows = jnp.dot(inputs_here, gathered, preferred_element_type=F32).astype(BF16)
    grad_in = lax.dot_general(cotangent, gathered, (((1,), (1,)), ((), ())), preferred_element_type=F32).astype(BF16)
    terms = lax.dot_general(inputs_here, cotangent, (((0,), (0,)), ((), ())), preferred_element_type=F32)
    grad_rows = lax.psum_scatter(terms * token_weight, "fsdp", scatter_dimension=0, tiled=True).astype(BF16)
    bits = lax.axis_size("replica")
    held = [local_shard]
    while bits > 1:
        bits //= 2
        held = send_windows(held, bits, kv_width, ())
    new_share, new_momentum = update_share(held, global_weights, momentum, ())
    shares, joined = [new_share], [0]
    bits = lax.axis_size("replica")
    while bits > 1:
        bits //= 2
        shares = [jnp.concatenate(shares, axis=1)]
        shares.append(swap(shares[0], bits))
        joined += [place ^ bits for place in joined]
    return kv_rows, grad_in, grad_rows, join_shares(shares, joined, kv_width, ()), new_momentum


def per_device(local_weights, global_weights, momentum, activations, kv_cotangent):
    depth = local_weights.shape[1]
    pairs_fit = lax.axis_size("fsdp") == 8 and depth % LANES == 0 and local_weights.shape[2] % depth == 0
    step = inner_and_outer if pairs_fit else plain_inner_and_outer
    kv_rows, grad_in, grad_rows, new_global, new_momentum = step(
        local_weights[0], global_weights, momentum, activations[0], kv_cotangent[0]
    )
    return kv_rows[None], grad_in[None], grad_rows[None], new_global, new_momentum


def solution(mesh):
    placed = (
        P("replica", "fsdp", None),
        P("fsdp", None),
        P("fsdp", "replica"),
        P("replica", "fsdp", None),
        P("replica", "fsdp", None),
    )
    return jax.shard_map(
        per_device,
        mesh=mesh,
        in_specs=placed,
        out_specs=(
            P("replica", "fsdp", None),
            P("replica", "fsdp", None),
            P("replica", "fsdp", None),
            P("fsdp", None),
            P("fsdp", "replica"),
        ),
        check_vma=False,
    )
```

```python
import functools

import jax
import jax.numpy as jnp
from jax import lax
from jax.experimental import pallas as pl
from jax.experimental.pallas import tpu as pltpu
from jax.sharding import PartitionSpec as P

BLOCK = 64

outer_rate = 0.7
outer_momentum = 0.9
scale_epsilon = 1e-06

F32 = jnp.float32
BF16 = jnp.bfloat16
LANES = 128
VMEM_BYTES = 8 * 2**20


def ring_order(size):
    return list(range(0, size, 2)) + list(range(1, size, 2))[::-1]


def ring_place(index, size):
    return jnp.where((index & 1) == 0, index >> 1, size - 1 - (index >> 1))


def ring_index(place, size):
    place = lax.rem(place + size, size)
    evens = (size + 1) // 2
    return jnp.where(place < evens, 2 * place, 2 * (size - 1 - place) + 1)


def block_start(offset, size, depth, other=0):
    me = lax.axis_index("fsdp")
    row = ring_index(ring_place(me >> 1, size // 2) + offset, size // 2)
    return pl.multiple_of((2 * row + ((me & 1) ^ other)) * depth, depth)


def vmem_call(kernel, out_shape, operands, flops, name, after=(), moved=None):
    def body(*refs):
        kernel(*refs[: len(operands)], *refs[len(operands) + len(after) :])

    moved = moved or sum(x.size * x.dtype.itemsize for x in operands)
    whole = pl.BlockSpec(memory_space=pltpu.VMEM)
    return pl.pallas_call(
        body,
        out_shape=out_shape,
        in_specs=[whole] * len(operands) + [pl.BlockSpec(memory_space=pl.ANY)] * len(after),
        out_specs=jax.tree.map(lambda _: whole, out_shape),
        compiler_params=pltpu.CompilerParams(vmem_limit_bytes=VMEM_BYTES),
        cost_estimate=pl.CostEstimate(flops=flops, bytes_accessed=moved, transcendentals=0),
        name=name,
    )(*operands, *after)


def shape_of(rows, columns, dtype):
    return jax.ShapeDtypeStruct((rows, columns), dtype)


def column_window(array, start, width):
    if isinstance(array, jax.Array):
        return lax.dynamic_slice_in_dim(array, start, width, array.ndim - 1)
    return array[..., pl.ds(pl.multiple_of(start, width), width)]


def outer_kernel(replicas, share_cols, *refs):
    *held_refs, global_ref, momentum_ref, share_ref, new_momentum_ref = refs
    rows, window = held_refs[-1].shape[-2:]
    me = lax.axis_index("replica")

    def windows_of(ref):
        here = me * share_cols // window * window % ref.shape[-1]
        return ref[...] if ref.shape[-1] == window else column_window(ref, here, window)

    old = windows_of(global_ref).astype(F32)
    lane = lax.broadcasted_iota(jnp.int32, (rows, window), 1) // BLOCK
    total = jnp.zeros((rows, window), F32)
    for held_ref in held_refs:
        held = windows_of(held_ref).astype(F32)
        for local in [held] if held.ndim == 2 else list(held):
            drift = old - local
            size = jnp.abs(drift)
            scale = jnp.zeros((rows, window), F32)
            for block in range(window // BLOCK):
                top = jnp.max(jnp.where(lane == block, size, 0.0), axis=1, keepdims=True)
                top = (top + scale_epsilon).astype(BF16).astype(F32)
                scale = jnp.where(lane == block, top, scale)
            total = total + (drift / scale).astype(BF16).astype(F32) * scale
    mean_grad = total / replicas
    shares = window // share_cols
    mean_here, old_here = mean_grad[:, :share_cols], old[:, :share_cols]
    mine = me % shares
    for share in range(1, shares):
        columns = slice(share * share_cols, (share + 1) * share_cols)
        mean_here = jnp.where(mine == share, mean_grad[:, columns], mean_here)
        old_here = jnp.where(mine == share, old[:, columns], old_here)
    new_momentum = outer_momentum * momentum_ref[...] + mean_here
    new_momentum_ref[...] = new_momentum
    share_ref[...] = (old_here - outer_rate * (mean_here + outer_momentum * new_momentum)).astype(BF16)


def swap(array, bits):
    return lax.ppermute(array, "replica", [(at, at ^ bits) for at in range(lax.axis_size("replica"))])


def partner_kernel(bits, share_cols, width, *refs):
    *held_refs, out_ref = refs
    start = (lax.axis_index("replica") ^ bits) * share_cols // width * width
    at = 0
    for held_ref in held_refs:
        part = column_window(held_ref, start % held_ref.shape[-1], width)
        count = 1 if part.ndim == 2 else part.shape[0]
        out_ref[at : at + count] = part.reshape((count,) + part.shape[-2:])
        at += count


def send_windows(held, bits, kv_width, after):
    replicas = lax.axis_size("replica")
    share_cols = kv_width // replicas
    width = max(bits * share_cols, BLOCK)
    rows = held[0].shape[-2]
    count = sum(1 if array.ndim == 2 else array.shape[0] for array in held)
    if width % LANES == 0:
        leaving = vmem_call(
            functools.partial(partner_kernel, bits, share_cols, width),
            jax.ShapeDtypeStruct((count, rows, width), BF16),
            held,
            0,
            "partner_columns",
            after,
        )
    else:
        start = (lax.axis_index("replica") ^ bits) * share_cols // width * width
        parts = [column_window(array, start % array.shape[-1], width).reshape(-1, rows, width) for array in held]
        leaving = jnp.concatenate(parts)
    return held + [swap(leaving, bits)]


def update_share(held, global_weights, momentum, after):
    rows, share_cols = momentum.shape
    replicas = lax.axis_size("replica")
    window = held[-1].shape[-1]
    if window % LANES:
        start = lax.axis_index("replica") * share_cols // window * window
        held = [column_window(array, start % array.shape[-1], window) for array in held]
        global_weights = column_window(global_weights, start, window)
    return vmem_call(
        functools.partial(outer_kernel, replicas, share_cols),
        (shape_of(rows, share_cols, BF16), shape_of(rows, share_cols, F32)),
        held + [global_weights, momentum],
        0,
        "outer_update",
        after,
    )


def join_kernel(places, *refs):
    *held_refs, out_ref = refs
    width = out_ref.shape[1] // len(places)
    me = lax.axis_index("replica")
    at = 0
    for held_ref in held_refs:
        for start in range(0, held_ref.shape[1], width):
            columns = pl.ds(pl.multiple_of((me ^ places[at]) * width, width), width)
            out_ref[:, columns] = held_ref[:, start : start + width]
            at += 1


def beside_kernel(left_ref, right_ref, out_ref):
    width = left_ref.shape[1]
    out_ref[:, :width] = left_ref[...]
    out_ref[:, width:] = right_ref[...]


def beside(left, right, after):
    rows, width = left.shape
    if width % LANES:
        return jnp.concatenate([left, right], axis=1)
    return vmem_call(beside_kernel, shape_of(rows, 2 * width, BF16), [left, right], 0, "beside", after)


def join_shares(held, places, kv_width, after):
    rows = held[0].shape[0]
    width = kv_width // len(places)
    if width % LANES == 0:
        return vmem_call(
            functools.partial(join_kernel, places), shape_of(rows, kv_width, BF16), held, 0, "join_shares", after
        )
    whole = jnp.concatenate(held, axis=1)
    joined = jnp.zeros_like(whole)
    for at, place in enumerate(places):
        start = (lax.axis_index("replica") ^ place) * width
        joined = lax.dynamic_update_slice_in_dim(joined, whole[:, at * width : (at + 1) * width], start, 1)
    return joined


PARTNER = {2: (0, 0), 1: (0, 1), 3: (1, 0), 0: (1, 1)}


def mark_kernel(out_ref):
    out_ref[...] = jnp.zeros_like(out_ref)


def arrived(after):
    return vmem_call(mark_kernel, shape_of(8, LANES, F32), [], 0, "mark", after)


def pack_kernel(size, part, inputs_ref, out_ref):
    depth = inputs_ref.shape[1] // size
    for offset, (at, slot) in PARTNER.items():
        if at == part:
            out_ref[slot] = inputs_ref[:, pl.ds(block_start(offset, size, depth, 1), depth)]


def pack(inputs_here, size, part, after=()):
    tokens, width = inputs_here.shape
    shape = jax.ShapeDtypeStruct((2, tokens, width // size), BF16)
    return vmem_call(functools.partial(pack_kernel, size, part), shape, [inputs_here], 0, "pack_columns", after)


def terms_kernel(size, offsets, token_weight, inputs_ref, cotangent_ref, partner_ref, partner_cotangent_ref, *out_refs):
    depth = inputs_ref.shape[1] // size
    for offset, out_ref in zip(offsets, out_refs):
        here = inputs_ref[:, pl.ds(block_start(offset, size, depth), depth)]
        there = partner_ref[PARTNER[offset][1]]
        total = 0.0
        for columns, cotangent in ((here, cotangent_ref[...]), (there, partner_cotangent_ref[...])):
            total = total + lax.dot_general(
                columns, cotangent, (((0,), (0,)), ((), ())), preferred_element_type=F32
            )
        out_ref[...] = (total * token_weight).astype(out_ref.dtype)


def token_terms(operands, size, offsets, dtype, token_weight, after=()):
    tokens, width = operands[0].shape
    kv_width = operands[1].shape[1]
    depth = width // size
    return vmem_call(
        functools.partial(terms_kernel, size, offsets, token_weight),
        [shape_of(depth, kv_width, dtype)] * len(offsets),
        operands,
        4 * tokens * depth * len(offsets) * kv_width,
        "token_terms",
        after,
    )


def add_kernel(terms_ref, sum_ref, out_ref):
    out_ref[...] = (terms_ref[...] + sum_ref[...].astype(F32)).astype(BF16)


def back_product(cotangent, block):
    return lax.dot_general(cotangent, block, (((1,), (1,)), ((), ())), preferred_element_type=F32).astype(BF16)


def grads_kernel(cotangent_ref, partner_cotangent_ref, *refs):
    *block_refs, here_ref, leaving_ref = refs
    for number, block_ref in enumerate(block_refs):
        here_ref[number] = back_product(cotangent_ref[...], block_ref[...])
        leaving_ref[number] = back_product(partner_cotangent_ref[...], block_ref[...])


def near_grads(cotangent, partner_cotangent, blocks, after):
    tokens, kv_width = cotangent.shape
    depth = blocks[0].shape[0]
    shape = jax.ShapeDtypeStruct((len(blocks), tokens, depth), BF16)
    operands = [cotangent, partner_cotangent, *blocks.values()]
    flops = 4 * tokens * depth * len(blocks) * kv_width
    return vmem_call(grads_kernel, [shape] * 2, operands, flops, "near_grads", after)


def rows_kernel(size, offsets, inputs_ref, *refs):
    partner_refs, block_refs, (here_ref, there_ref) = refs[:2], refs[2:-2], refs[-2:]
    depth = inputs_ref.shape[1] // size
    here = there = 0.0
    for offset, block_ref in zip(offsets, block_refs):
        at, slot = PARTNER[offset]
        columns = inputs_ref[:, pl.ds(block_start(offset, size, depth), depth)]
        here = here + jnp.dot(columns, block_ref[...], preferred_element_type=F32)
        there = there + jnp.dot(partner_refs[at][slot], block_ref[...], preferred_element_type=F32)
    here_ref[...], there_ref[...] = here, there


def near_rows(inputs_here, partner_inputs, blocks, size, after):
    tokens, kv_width = inputs_here.shape[0], blocks[0].shape[1]
    return vmem_call(
        functools.partial(rows_kernel, size, list(blocks)),
        [shape_of(tokens, kv_width, F32)] * 2,
        [inputs_here, *partner_inputs, *blocks.values()],
        4 * tokens * blocks[0].shape[0] * len(blocks) * kv_width,
        "near_rows",
        after,
    )


def last_kernel(size, offsets, inputs_ref, cotangent_ref, partner_ref, partner_cotangent_ref, *refs):
    block_refs, (here_ref, there_ref, rows_ref, grad_ref, leaving_ref) = refs[: len(offsets)], refs[len(offsets) :]
    depth = block_refs[0].shape[0]
    for number, block_ref in enumerate(block_refs):
        leaving_ref[number] = back_product(partner_cotangent_ref[...], block_ref[...])
    last = block_refs[-1][...]
    there = there_ref[...] + jnp.dot(partner_ref[PARTNER[offsets[-1]][1]], last, preferred_element_type=F32)
    for part in range(there.shape[1] // depth):
        leaving_ref[len(offsets) + part] = there[:, part * depth : (part + 1) * depth].astype(BF16)
    for number, block_ref in enumerate(block_refs):
        grad_ref[number] = back_product(cotangent_ref[...], block_ref[...])
    columns = inputs_ref[:, pl.ds(block_start(offsets[-1], size, depth), depth)]
    rows_ref[...] = here_ref[...] + jnp.dot(columns, last, preferred_element_type=F32)


def last_products(inputs_here, cotangent, partner_inputs, partner_cotangent, blocks, totals, size, after):
    tokens = inputs_here.shape[0]
    offsets = list(blocks)
    depth, kv_width = blocks[offsets[-1]].shape
    partner = partner_inputs[PARTNER[offsets[-1]][0]]
    return vmem_call(
        functools.partial(last_kernel, size, offsets),
        [
            shape_of(tokens, kv_width, F32),
            jax.ShapeDtypeStruct((len(blocks), tokens, depth), BF16),
            jax.ShapeDtypeStruct((len(blocks) + kv_width // depth, tokens, depth), BF16),
        ],
        [inputs_here, cotangent, partner, partner_cotangent, *blocks.values(), *totals],
        8 * tokens * depth * kv_width,
        "last_products",
        after,
    )


def write_columns(size, sources, grad_ref, sems):
    depth = grad_ref.shape[1] // size
    copies = []
    for source_ref, number, offset, other in sources:
        columns = pl.ds(block_start(offset, size, depth, other), depth)
        copies.append(pltpu.make_async_copy(source_ref.at[number], grad_ref.at[:, columns], sems.at[len(copies)]))
        copies[-1].start()
    return copies


def collect_kernel(size, early, late, near_ref, last_ref, early_ref, *refs):
    grad_ref, mark_ref, sems = refs[-3:]
    sources = [(near_ref, number, offset, 0) for number, offset in enumerate(early)]
    sources += [(last_ref, number, offset, 0) for number, offset in enumerate(late)]
    sources += [(early_ref, number, offset, 1) for number, offset in enumerate(early)]
    copies = write_columns(size, sources, grad_ref, sems)
    mark_ref[...] = jnp.zeros_like(mark_ref)
    for copy in copies:
        copy.wait()


def collect(grads, width, size, early, late, after):
    whole, anywhere = pl.BlockSpec(memory_space=pltpu.VMEM), pl.BlockSpec(memory_space=pl.ANY)
    return pl.pallas_call(
        functools.partial(collect_kernel, size, early, late),
        out_shape=(shape_of(grads[0].shape[1], width, BF16), shape_of(8, LANES, F32)),
        in_specs=[whole] * len(grads) + [anywhere] * len(after),
        out_specs=(anywhere, whole),
        scratch_shapes=[pltpu.SemaphoreType.DMA((2 * len(early) + len(late),))],
        compiler_params=pltpu.CompilerParams(vmem_limit_bytes=VMEM_BYTES),
        cost_estimate=pl.CostEstimate(flops=0, bytes_accessed=2**20, transcendentals=0),
        name="collect",
    )(*grads, *after)


def finish_kernel(size, late, total_ref, late_ref, terms_ref, up_ref, down_ref, _, *refs):
    rows_ref, grad_ref, sum_ref, rows_held, sum_held, sems, sem_rows, sem_sum = refs
    copies = write_columns(size, [(late_ref, number, offset, 1) for number, offset in enumerate(late)], grad_ref, sems)
    depth = late_ref.shape[-1]
    for part in range(total_ref.shape[1] // depth):
        columns = slice(part * depth, (part + 1) * depth)
        rows_held[:, columns] = (total_ref[:, columns] + late_ref[len(late) + part].astype(F32)).astype(BF16)
    copies.append(pltpu.make_async_copy(rows_held, rows_ref, sem_rows))
    copies[-1].start()
    sum_held[...] = (terms_ref[...] + up_ref[...].astype(F32) + down_ref[...].astype(F32)).astype(BF16)
    copies.append(pltpu.make_async_copy(sum_held, sum_ref, sem_sum))
    copies[-1].start()
    for copy in copies:
        copy.wait()


def finish(total, late, sums, grad, size, offsets):
    whole, anywhere = pl.BlockSpec(memory_space=pltpu.VMEM), pl.BlockSpec(memory_space=pl.ANY)
    rows, summed = shape_of(*total.shape, BF16), shape_of(*sums[0].shape, BF16)
    return pl.pallas_call(
        functools.partial(finish_kernel, size, offsets),
        out_shape=(rows, shape_of(*grad.shape, BF16), summed),
        in_specs=[whole] * 5 + [anywhere],
        out_specs=(anywhere,) * 3,
        scratch_shapes=[
            pltpu.VMEM(rows.shape, BF16),
            pltpu.VMEM(summed.shape, BF16),
            pltpu.SemaphoreType.DMA((len(offsets),)),
            pltpu.SemaphoreType.DMA,
            pltpu.SemaphoreType.DMA,
        ],
        input_output_aliases={5: 1},
        compiler_params=pltpu.CompilerParams(vmem_limit_bytes=VMEM_BYTES),
        cost_estimate=pl.CostEstimate(flops=0, bytes_accessed=2**20, transcendentals=0),
        name="finish",
    )(total, late, *sums, grad)


def inner_and_outer(local_shard, global_weights, momentum, inputs_here, cotangent):
    depth, kv_width = local_shard.shape
    tokens, width = inputs_here.shape
    size = lax.axis_size("fsdp")
    ring = size // 2
    token_weight = 1.0 / (tokens * size)
    order = ring_order(ring)
    pairs = [(2 * order[at - 1] + side, 2 * order[at] + side) for at in range(ring) for side in (0, 1)]

    def upward(array):
        return lax.ppermute(array, "fsdp", pairs)

    def downward(array):
        return lax.ppermute(array, "fsdp", [(target, source) for source, target in pairs])

    def across(array):
        return lax.ppermute(array, "fsdp", [(at, at ^ 1) for at in range(size)])

    from_below, from_above = upward(local_shard), downward(local_shard)
    partner_cotangent = across(cotangent)
    packed = pack(inputs_here, size, 0)

    bits = lax.axis_size("replica") // 2
    held = send_windows([local_shard], bits, kv_width, (packed,))
    partner_inputs = [across(packed), across(pack(inputs_here, size, 1, (partner_cotangent, arrived((from_below,)))))]

    early_blocks, late_blocks = {0: local_shard, 3: from_below}, {1: from_above, 2: upward(from_below)}
    operands = [inputs_here, cotangent, partner_inputs[0], partner_cotangent]
    first = token_terms(operands, size, [2, 1], BF16, token_weight)
    sum_down, sum_up = downward(first[0]), upward(first[1])
    while bits > 1:
        bits //= 2
        held = send_windows(held, bits, kv_width, first)
    near, leaving = near_grads(cotangent, partner_cotangent, early_blocks, (first[0], held[1]))
    early = across(leaving)
    operands[2] = partner_inputs[1]
    terms = token_terms(operands, size, [3, 0], F32, token_weight, (leaving,))
    totals = near_rows(inputs_here, partner_inputs, {**early_blocks, 1: from_above}, size, (leaving, arrived((late_blocks[2],))))
    new_share, new_momentum = update_share(held, global_weights, momentum, (totals[0],))
    rows, last, leaving = last_products(
        inputs_here, cotangent, partner_inputs, partner_cotangent, late_blocks, totals, size, (new_share,)
    )
    late = across(leaving)
    total_down = vmem_call(
        add_kernel, shape_of(depth, kv_width, BF16), [terms[0], sum_down], 0, "add_terms", (leaving, early)
    )
    sum_down = downward(total_down)
    bits = lax.axis_size("replica")
    shares, joined = [new_share], [0]
    while bits > 1:
        bits //= 2
        shares = [shares[0] if len(shares) == 1 else jnp.concatenate(shares, axis=1)]
        shares.append(swap(shares[0], bits))
        joined += [place ^ bits for place in joined]
    grad, mark = collect([near, last, early], width, size, list(early_blocks), list(late_blocks), ())
    new_global = join_shares(shares, joined, kv_width, (mark,))
    kv_rows, grad_in, grad_rows = finish(
        rows, late, [terms[1], sum_up, sum_down], grad, size, list(late_blocks)
    )
    return kv_rows, grad_in, grad_rows, new_global, new_momentum


def plain_inner_and_outer(local_shard, global_weights, momentum, inputs_here, cotangent):
    depth, kv_width = local_shard.shape
    token_weight = 1.0 / (inputs_here.shape[0] * lax.axis_size("fsdp"))
    gathered = lax.all_gather(local_shard, "fsdp", axis=0, tiled=True)
    kv_rows = jnp.dot(inputs_here, gathered, preferred_element_type=F32).astype(BF16)
    grad_in = lax.dot_general(cotangent, gathered, (((1,), (1,)), ((), ())), preferred_element_type=F32).astype(BF16)
    terms = lax.dot_general(inputs_here, cotangent, (((0,), (0,)), ((), ())), preferred_element_type=F32)
    grad_rows = lax.psum_scatter(terms * token_weight, "fsdp", scatter_dimension=0, tiled=True).astype(BF16)
    bits = lax.axis_size("replica")
    held = [local_shard]
    while bits > 1:
        bits //= 2
        held = send_windows(held, bits, kv_width, ())
    new_share, new_momentum = update_share(held, global_weights, momentum, ())
    shares, joined = [new_share], [0]
    bits = lax.axis_size("replica")
    while bits > 1:
        bits //= 2
        shares = [jnp.concatenate(shares, axis=1)]
        shares.append(swap(shares[0], bits))
        joined += [place ^ bits for place in joined]
    return kv_rows, grad_in, grad_rows, join_shares(shares, joined, kv_width, ()), new_momentum


def per_device(local_weights, global_weights, momentum, activations, kv_cotangent):
    depth = local_weights.shape[1]
    pairs_fit = lax.axis_size("fsdp") == 8 and depth % LANES == 0 and local_weights.shape[2] % depth == 0
    step = inner_and_outer if pairs_fit else plain_inner_and_outer
    kv_rows, grad_in, grad_rows, new_global, new_momentum = step(
        local_weights[0], global_weights, momentum, activations[0], kv_cotangent[0]
    )
    return kv_rows[None], grad_in[None], grad_rows[None], new_global, new_momentum


def solution(mesh):
    placed = (
        P("replica", "fsdp", None),
        P("fsdp", None),
        P("fsdp", "replica"),
        P("replica", "fsdp", None),
        P("replica", "fsdp", None),
    )
    return jax.shard_map(
        per_device,
        mesh=mesh,
        in_specs=placed,
        out_specs=(
            P("replica", "fsdp", None),
            P("replica", "fsdp", None),
            P("replica", "fsdp", None),
            P("fsdp", None),
            P("fsdp", "replica"),
        ),
        check_vma=False,
    )
```

```python
import functools

import jax
import jax.numpy as jnp
from jax import lax
from jax.experimental import pallas as pl
from jax.experimental.pallas import tpu as pltpu
from jax.sharding import PartitionSpec as P

BLOCK = 64

outer_rate = 0.7
outer_momentum = 0.9
scale_epsilon = 1e-06

F32 = jnp.float32
BF16 = jnp.bfloat16
LANES = 128
VMEM_BYTES = 8 * 2**20


def ring_order(size):
    return list(range(0, size, 2)) + list(range(1, size, 2))[::-1]


def ring_place(index, size):
    return jnp.where((index & 1) == 0, index >> 1, size - 1 - (index >> 1))


def ring_index(place, size):
    place = lax.rem(place + size, size)
    evens = (size + 1) // 2
    return jnp.where(place < evens, 2 * place, 2 * (size - 1 - place) + 1)


def block_start(offset, size, depth, other=0):
    me = lax.axis_index("fsdp")
    row = ring_index(ring_place(me >> 1, size // 2) + offset, size // 2)
    return pl.multiple_of((2 * row + ((me & 1) ^ other)) * depth, depth)


def vmem_call(kernel, out_shape, operands, flops, name, after=(), moved=None):
    def body(*refs):
        kernel(*refs[: len(operands)], *refs[len(operands) + len(after) :])

    moved = moved or sum(x.size * x.dtype.itemsize for x in operands)
    whole = pl.BlockSpec(memory_space=pltpu.VMEM)
    return pl.pallas_call(
        body,
        out_shape=out_shape,
        in_specs=[whole] * len(operands) + [pl.BlockSpec(memory_space=pl.ANY)] * len(after),
        out_specs=jax.tree.map(lambda _: whole, out_shape),
        compiler_params=pltpu.CompilerParams(vmem_limit_bytes=VMEM_BYTES),
        cost_estimate=pl.CostEstimate(flops=flops, bytes_accessed=moved, transcendentals=0),
        name=name,
    )(*operands, *after)


def shape_of(rows, columns, dtype):
    return jax.ShapeDtypeStruct((rows, columns), dtype)


def column_window(array, start, width):
    if isinstance(array, jax.Array):
        return lax.dynamic_slice_in_dim(array, start, width, array.ndim - 1)
    return array[..., pl.ds(pl.multiple_of(start, width), width)]


def outer_kernel(replicas, share_cols, *refs):
    *held_refs, global_ref, momentum_ref, share_ref, new_momentum_ref = refs
    rows, window = held_refs[-1].shape[-2:]
    me = lax.axis_index("replica")

    def windows_of(ref):
        here = me * share_cols // window * window % ref.shape[-1]
        return ref[...] if ref.shape[-1] == window else column_window(ref, here, window)

    old = windows_of(global_ref).astype(F32)
    lane = lax.broadcasted_iota(jnp.int32, (rows, window), 1) // BLOCK
    total = jnp.zeros((rows, window), F32)
    for held_ref in held_refs:
        held = windows_of(held_ref).astype(F32)
        for local in [held] if held.ndim == 2 else list(held):
            drift = old - local
            size = jnp.abs(drift)
            scale = jnp.zeros((rows, window), F32)
            for block in range(window // BLOCK):
                top = jnp.max(jnp.where(lane == block, size, 0.0), axis=1, keepdims=True)
                top = (top + scale_epsilon).astype(BF16).astype(F32)
                scale = jnp.where(lane == block, top, scale)
            total = total + (drift / scale).astype(BF16).astype(F32) * scale
    mean_grad = total / replicas
    shares = window // share_cols
    mean_here, old_here = mean_grad[:, :share_cols], old[:, :share_cols]
    mine = me % shares
    for share in range(1, shares):
        columns = slice(share * share_cols, (share + 1) * share_cols)
        mean_here = jnp.where(mine == share, mean_grad[:, columns], mean_here)
        old_here = jnp.where(mine == share, old[:, columns], old_here)
    new_momentum = outer_momentum * momentum_ref[...] + mean_here
    new_momentum_ref[...] = new_momentum
    share_ref[...] = (old_here - outer_rate * (mean_here + outer_momentum * new_momentum)).astype(BF16)


def swap(array, bits):
    return lax.ppermute(array, "replica", [(at, at ^ bits) for at in range(lax.axis_size("replica"))])


def partner_kernel(bits, share_cols, width, *refs):
    *held_refs, out_ref = refs
    start = (lax.axis_index("replica") ^ bits) * share_cols // width * width
    at = 0
    for held_ref in held_refs:
        part = column_window(held_ref, start % held_ref.shape[-1], width)
        count = 1 if part.ndim == 2 else part.shape[0]
        out_ref[at : at + count] = part.reshape((count,) + part.shape[-2:])
        at += count


def send_windows(held, bits, kv_width, after):
    replicas = lax.axis_size("replica")
    share_cols = kv_width // replicas
    width = max(bits * share_cols, BLOCK)
    rows = held[0].shape[-2]
    count = sum(1 if array.ndim == 2 else array.shape[0] for array in held)
    if width % LANES == 0:
        leaving = vmem_call(
            functools.partial(partner_kernel, bits, share_cols, width),
            jax.ShapeDtypeStruct((count, rows, width), BF16),
            held,
            0,
            "partner_columns",
            after,
        )
    else:
        start = (lax.axis_index("replica") ^ bits) * share_cols // width * width
        parts = [column_window(array, start % array.shape[-1], width).reshape(-1, rows, width) for array in held]
        leaving = jnp.concatenate(parts)
    return held + [swap(leaving, bits)]


def update_share(held, global_weights, momentum, after):
    rows, share_cols = momentum.shape
    replicas = lax.axis_size("replica")
    window = held[-1].shape[-1]
    if window % LANES:
        start = lax.axis_index("replica") * share_cols // window * window
        held = [column_window(array, start % array.shape[-1], window) for array in held]
        global_weights = column_window(global_weights, start, window)
    return vmem_call(
        functools.partial(outer_kernel, replicas, share_cols),
        (shape_of(rows, share_cols, BF16), shape_of(rows, share_cols, F32)),
        held + [global_weights, momentum],
        0,
        "outer_update",
        after,
    )


def join_kernel(places, *refs):
    *held_refs, out_ref = refs
    width = out_ref.shape[1] // len(places)
    me = lax.axis_index("replica")
    at = 0
    for held_ref in held_refs:
        for start in range(0, held_ref.shape[1], width):
            columns = pl.ds(pl.multiple_of((me ^ places[at]) * width, width), width)
            out_ref[:, columns] = held_ref[:, start : start + width]
            at += 1


def beside_kernel(left_ref, right_ref, out_ref):
    width = left_ref.shape[1]
    out_ref[:, :width] = left_ref[...]
    out_ref[:, width:] = right_ref[...]


def beside(left, right, after):
    rows, width = left.shape
    if width % LANES:
        return jnp.concatenate([left, right], axis=1)
    return vmem_call(beside_kernel, shape_of(rows, 2 * width, BF16), [left, right], 0, "beside", after)


def join_shares(held, places, kv_width, after):
    rows = held[0].shape[0]
    width = kv_width // len(places)
    if width % LANES == 0:
        return vmem_call(
            functools.partial(join_kernel, places), shape_of(rows, kv_width, BF16), held, 0, "join_shares", after
        )
    whole = jnp.concatenate(held, axis=1)
    joined = jnp.zeros_like(whole)
    for at, place in enumerate(places):
        start = (lax.axis_index("replica") ^ place) * width
        joined = lax.dynamic_update_slice_in_dim(joined, whole[:, at * width : (at + 1) * width], start, 1)
    return joined


PARTNER = {2: (0, 0), 1: (0, 1), 3: (1, 0), 0: (1, 1)}


def mark_kernel(out_ref):
    out_ref[...] = jnp.zeros_like(out_ref)


def arrived(after):
    return vmem_call(mark_kernel, shape_of(8, LANES, F32), [], 0, "mark", after)


def pack_kernel(size, part, inputs_ref, out_ref):
    depth = inputs_ref.shape[1] // size
    for offset, (at, slot) in PARTNER.items():
        if at == part:
            out_ref[slot] = inputs_ref[:, pl.ds(block_start(offset, size, depth, 1), depth)]


def pack(inputs_here, size, part, after=()):
    tokens, width = inputs_here.shape
    shape = jax.ShapeDtypeStruct((2, tokens, width // size), BF16)
    return vmem_call(functools.partial(pack_kernel, size, part), shape, [inputs_here], 0, "pack_columns", after)


def terms_kernel(size, offsets, token_weight, inputs_ref, cotangent_ref, partner_ref, partner_cotangent_ref, *out_refs):
    depth = inputs_ref.shape[1] // size
    for offset, out_ref in zip(offsets, out_refs):
        here = inputs_ref[:, pl.ds(block_start(offset, size, depth), depth)]
        there = partner_ref[PARTNER[offset][1]]
        total = 0.0
        for columns, cotangent in ((here, cotangent_ref[...]), (there, partner_cotangent_ref[...])):
            total = total + lax.dot_general(
                columns, cotangent, (((0,), (0,)), ((), ())), preferred_element_type=F32
            )
        out_ref[...] = (total * token_weight).astype(out_ref.dtype)


def token_terms(operands, size, offsets, dtype, token_weight, after=()):
    tokens, width = operands[0].shape
    kv_width = operands[1].shape[1]
    depth = width // size
    return vmem_call(
        functools.partial(terms_kernel, size, offsets, token_weight),
        [shape_of(depth, kv_width, dtype)] * len(offsets),
        operands,
        4 * tokens * depth * len(offsets) * kv_width,
        "token_terms",
        after,
    )


def add_kernel(terms_ref, sum_ref, out_ref):
    out_ref[...] = (terms_ref[...] + sum_ref[...].astype(F32)).astype(BF16)


def back_product(cotangent, block):
    return lax.dot_general(cotangent, block, (((1,), (1,)), ((), ())), preferred_element_type=F32).astype(BF16)


def grads_kernel(cotangent_ref, partner_cotangent_ref, *refs):
    *block_refs, here_ref, leaving_ref = refs
    for number, block_ref in enumerate(block_refs):
        here_ref[number] = back_product(cotangent_ref[...], block_ref[...])
        leaving_ref[number] = back_product(partner_cotangent_ref[...], block_ref[...])


def near_grads(cotangent, partner_cotangent, blocks, after):
    tokens, kv_width = cotangent.shape
    depth = blocks[0].shape[0]
    shape = jax.ShapeDtypeStruct((len(blocks), tokens, depth), BF16)
    operands = [cotangent, partner_cotangent, *blocks.values()]
    flops = 4 * tokens * depth * len(blocks) * kv_width
    return vmem_call(grads_kernel, [shape] * 2, operands, flops, "near_grads", after)


def rows_kernel(size, offsets, inputs_ref, *refs):
    partner_refs, block_refs, (here_ref, there_ref) = refs[:2], refs[2:-2], refs[-2:]
    depth = inputs_ref.shape[1] // size
    here = there = 0.0
    for offset, block_ref in zip(offsets, block_refs):
        at, slot = PARTNER[offset]
        columns = inputs_ref[:, pl.ds(block_start(offset, size, depth), depth)]
        here = here + jnp.dot(columns, block_ref[...], preferred_element_type=F32)
        there = there + jnp.dot(partner_refs[at][slot], block_ref[...], preferred_element_type=F32)
    here_ref[...], there_ref[...] = here, there


def near_rows(inputs_here, partner_inputs, blocks, size, after):
    tokens, kv_width = inputs_here.shape[0], blocks[0].shape[1]
    return vmem_call(
        functools.partial(rows_kernel, size, list(blocks)),
        [shape_of(tokens, kv_width, F32)] * 2,
        [inputs_here, *partner_inputs, *blocks.values()],
        4 * tokens * blocks[0].shape[0] * len(blocks) * kv_width,
        "near_rows",
        after,
    )


def last_kernel(size, offsets, inputs_ref, cotangent_ref, partner_ref, partner_cotangent_ref, *refs):
    block_refs, (here_ref, there_ref, rows_ref, grad_ref, leaving_ref) = refs[: len(offsets)], refs[len(offsets) :]
    depth = block_refs[0].shape[0]
    for number, block_ref in enumerate(block_refs):
        leaving_ref[number] = back_product(partner_cotangent_ref[...], block_ref[...])
    last = block_refs[-1][...]
    there = there_ref[...] + jnp.dot(partner_ref[PARTNER[offsets[-1]][1]], last, preferred_element_type=F32)
    for part in range(there.shape[1] // depth):
        leaving_ref[len(offsets) + part] = there[:, part * depth : (part + 1) * depth].astype(BF16)
    for number, block_ref in enumerate(block_refs):
        grad_ref[number] = back_product(cotangent_ref[...], block_ref[...])
    columns = inputs_ref[:, pl.ds(block_start(offsets[-1], size, depth), depth)]
    rows_ref[...] = here_ref[...] + jnp.dot(columns, last, preferred_element_type=F32)


def last_products(inputs_here, cotangent, partner_inputs, partner_cotangent, blocks, totals, size, after):
    tokens = inputs_here.shape[0]
    offsets = list(blocks)
    depth, kv_width = blocks[offsets[-1]].shape
    partner = partner_inputs[PARTNER[offsets[-1]][0]]
    return vmem_call(
        functools.partial(last_kernel, size, offsets),
        [
            shape_of(tokens, kv_width, F32),
            jax.ShapeDtypeStruct((len(blocks), tokens, depth), BF16),
            jax.ShapeDtypeStruct((len(blocks) + kv_width // depth, tokens, depth), BF16),
        ],
        [inputs_here, cotangent, partner, partner_cotangent, *blocks.values(), *totals],
        8 * tokens * depth * kv_width,
        "last_products",
        after,
    )


def write_columns(size, sources, grad_ref, sems):
    depth = grad_ref.shape[1] // size
    copies = []
    for source_ref, number, offset, other in sources:
        columns = pl.ds(block_start(offset, size, depth, other), depth)
        copies.append(pltpu.make_async_copy(source_ref.at[number], grad_ref.at[:, columns], sems.at[len(copies)]))
        copies[-1].start()
    return copies


def collect_kernel(size, early, late, near_ref, last_ref, early_ref, grad_ref, mark_ref, sems):
    sources = [(near_ref, number, offset, 0) for number, offset in enumerate(early)]
    sources += [(last_ref, number, offset, 0) for number, offset in enumerate(late)]
    sources += [(early_ref, number, offset, 1) for number, offset in enumerate(early)]
    copies = write_columns(size, sources, grad_ref, sems)
    mark_ref[...] = jnp.zeros_like(mark_ref)
    for copy in copies:
        copy.wait()


def collect(grads, width, size, early, late):
    whole, anywhere = pl.BlockSpec(memory_space=pltpu.VMEM), pl.BlockSpec(memory_space=pl.ANY)
    return pl.pallas_call(
        functools.partial(collect_kernel, size, early, late),
        out_shape=(shape_of(grads[0].shape[1], width, BF16), shape_of(8, LANES, F32)),
        in_specs=[whole] * len(grads),
        out_specs=(anywhere, whole),
        scratch_shapes=[pltpu.SemaphoreType.DMA((2 * len(early) + len(late),))],
        compiler_params=pltpu.CompilerParams(vmem_limit_bytes=VMEM_BYTES),
        cost_estimate=pl.CostEstimate(flops=0, bytes_accessed=2**20, transcendentals=0),
        name="collect",
    )(*grads)


def finish_kernel(size, late, total_ref, late_ref, terms_ref, up_ref, down_ref, _, *refs):
    rows_ref, grad_ref, sum_ref, rows_held, sum_held, sems, sem_rows, sem_sum = refs
    copies = write_columns(size, [(late_ref, number, offset, 1) for number, offset in enumerate(late)], grad_ref, sems)
    depth = late_ref.shape[-1]
    for part in range(total_ref.shape[1] // depth):
        columns = slice(part * depth, (part + 1) * depth)
        rows_held[:, columns] = (total_ref[:, columns] + late_ref[len(late) + part].astype(F32)).astype(BF16)
    copies.append(pltpu.make_async_copy(rows_held, rows_ref, sem_rows))
    copies[-1].start()
    sum_held[...] = (terms_ref[...] + up_ref[...].astype(F32) + down_ref[...].astype(F32)).astype(BF16)
    copies.append(pltpu.make_async_copy(sum_held, sum_ref, sem_sum))
    copies[-1].start()
    for copy in copies:
        copy.wait()


def finish(total, late, sums, grad, size, offsets):
    whole, anywhere = pl.BlockSpec(memory_space=pltpu.VMEM), pl.BlockSpec(memory_space=pl.ANY)
    rows, summed = shape_of(*total.shape, BF16), shape_of(*sums[0].shape, BF16)
    return pl.pallas_call(
        functools.partial(finish_kernel, size, offsets),
        out_shape=(rows, shape_of(*grad.shape, BF16), summed),
        in_specs=[whole] * 5 + [anywhere],
        out_specs=(anywhere,) * 3,
        scratch_shapes=[
            pltpu.VMEM(rows.shape, BF16),
            pltpu.VMEM(summed.shape, BF16),
            pltpu.SemaphoreType.DMA((len(offsets),)),
            pltpu.SemaphoreType.DMA,
            pltpu.SemaphoreType.DMA,
        ],
        input_output_aliases={5: 1},
        compiler_params=pltpu.CompilerParams(vmem_limit_bytes=VMEM_BYTES),
        cost_estimate=pl.CostEstimate(flops=0, bytes_accessed=2**20, transcendentals=0),
        name="finish",
    )(total, late, *sums, grad)


def inner_and_outer(local_shard, global_weights, momentum, inputs_here, cotangent):
    depth, kv_width = local_shard.shape
    tokens, width = inputs_here.shape
    size = lax.axis_size("fsdp")
    ring = size // 2
    token_weight = 1.0 / (tokens * size)
    order = ring_order(ring)
    pairs = [(2 * order[at - 1] + side, 2 * order[at] + side) for at in range(ring) for side in (0, 1)]

    def upward(array):
        return lax.ppermute(array, "fsdp", pairs)

    def downward(array):
        return lax.ppermute(array, "fsdp", [(target, source) for source, target in pairs])

    def across(array):
        return lax.ppermute(array, "fsdp", [(at, at ^ 1) for at in range(size)])

    from_below, from_above = upward(local_shard), downward(local_shard)
    partner_cotangent = across(cotangent)
    packed = pack(inputs_here, size, 0)

    bits = lax.axis_size("replica") // 2
    held = send_windows([local_shard], bits, kv_width, (packed,))
    partner_inputs = [across(packed), across(pack(inputs_here, size, 1, (partner_cotangent, arrived((from_below,)))))]

    early_blocks, late_blocks = {0: local_shard, 3: from_below}, {1: from_above, 2: upward(from_below)}
    operands = [inputs_here, cotangent, partner_inputs[0], partner_cotangent]
    first = token_terms(operands, size, [2, 1], BF16, token_weight)
    sum_down, sum_up = downward(first[0]), upward(first[1])
    while bits > 1:
        bits //= 2
        held = send_windows(held, bits, kv_width, first)
    near, leaving = near_grads(cotangent, partner_cotangent, early_blocks, (first[0], held[1]))
    early = across(leaving)
    operands[2] = partner_inputs[1]
    terms = token_terms(operands, size, [3, 0], F32, token_weight, (leaving,))
    totals = near_rows(inputs_here, partner_inputs, {**early_blocks, 1: from_above}, size, (leaving, arrived((late_blocks[2],))))
    rows, last, leaving = last_products(
        inputs_here, cotangent, partner_inputs, partner_cotangent, late_blocks, totals, size, ()
    )
    late = across(leaving)
    total_down = vmem_call(
        add_kernel, shape_of(depth, kv_width, BF16), [terms[0], sum_down], 0, "add_terms", (leaving, early)
    )
    sum_down = downward(total_down)
    new_share, new_momentum = update_share(held, global_weights, momentum, (total_down,))
    bits = lax.axis_size("replica")
    shares, joined = [new_share], [0]
    while bits > 1:
        bits //= 2
        shares = [shares[0] if len(shares) == 1 else beside(*shares, (sum_up,))]
        shares.append(swap(shares[0], bits))
        joined += [place ^ bits for place in joined]
    grad, mark = collect([near, last, early], width, size, list(early_blocks), list(late_blocks))
    new_global = join_shares(shares, joined, kv_width, (mark,))
    kv_rows, grad_in, grad_rows = finish(
        rows, late, [terms[1], sum_up, sum_down], grad, size, list(late_blocks)
    )
    return kv_rows, grad_in, grad_rows, new_global, new_momentum


def plain_inner_and_outer(local_shard, global_weights, momentum, inputs_here, cotangent):
    depth, kv_width = local_shard.shape
    token_weight = 1.0 / (inputs_here.shape[0] * lax.axis_size("fsdp"))
    gathered = lax.all_gather(local_shard, "fsdp", axis=0, tiled=True)
    kv_rows = jnp.dot(inputs_here, gathered, preferred_element_type=F32).astype(BF16)
    grad_in = lax.dot_general(cotangent, gathered, (((1,), (1,)), ((), ())), preferred_element_type=F32).astype(BF16)
    terms = lax.dot_general(inputs_here, cotangent, (((0,), (0,)), ((), ())), preferred_element_type=F32)
    grad_rows = lax.psum_scatter(terms * token_weight, "fsdp", scatter_dimension=0, tiled=True).astype(BF16)
    bits = lax.axis_size("replica")
    held = [local_shard]
    while bits > 1:
        bits //= 2
        held = send_windows(held, bits, kv_width, ())
    new_share, new_momentum = update_share(held, global_weights, momentum, ())
    shares, joined = [new_share], [0]
    bits = lax.axis_size("replica")
    while bits > 1:
        bits //= 2
        shares = [jnp.concatenate(shares, axis=1)]
        shares.append(swap(shares[0], bits))
        joined += [place ^ bits for place in joined]
    return kv_rows, grad_in, grad_rows, join_shares(shares, joined, kv_width, ()), new_momentum


def per_device(local_weights, global_weights, momentum, activations, kv_cotangent):
    depth = local_weights.shape[1]
    pairs_fit = lax.axis_size("fsdp") == 8 and depth % LANES == 0 and local_weights.shape[2] % depth == 0
    step = inner_and_outer if pairs_fit else plain_inner_and_outer
    kv_rows, grad_in, grad_rows, new_global, new_momentum = step(
        local_weights[0], global_weights, momentum, activations[0], kv_cotangent[0]
    )
    return kv_rows[None], grad_in[None], grad_rows[None], new_global, new_momentum


def solution(mesh):
    placed = (
        P("replica", "fsdp", None),
        P("fsdp", None),
        P("fsdp", "replica"),
        P("replica", "fsdp", None),
        P("replica", "fsdp", None),
    )
    return jax.shard_map(
        per_device,
        mesh=mesh,
        in_specs=placed,
        out_specs=(
            P("replica", "fsdp", None),
            P("replica", "fsdp", None),
            P("replica", "fsdp", None),
            P("fsdp", None),
            P("fsdp", "replica"),
        ),
        check_vma=False,
    )
```

```python
import functools

import jax
import jax.numpy as jnp
from jax import lax
from jax.experimental import pallas as pl
from jax.experimental.pallas import tpu as pltpu
from jax.sharding import PartitionSpec as P

BLOCK = 64

outer_rate = 0.7
outer_momentum = 0.9
scale_epsilon = 1e-06

F32 = jnp.float32
BF16 = jnp.bfloat16
LANES = 128
VMEM_BYTES = 8 * 2**20


def ring_order(size):
    return list(range(0, size, 2)) + list(range(1, size, 2))[::-1]


def ring_place(index, size):
    return jnp.where((index & 1) == 0, index >> 1, size - 1 - (index >> 1))


def ring_index(place, size):
    place = lax.rem(place + size, size)
    evens = (size + 1) // 2
    return jnp.where(place < evens, 2 * place, 2 * (size - 1 - place) + 1)


def block_start(offset, size, depth, other=0):
    me = lax.axis_index("fsdp")
    row = ring_index(ring_place(me >> 1, size // 2) + offset, size // 2)
    return pl.multiple_of((2 * row + ((me & 1) ^ other)) * depth, depth)


def vmem_call(kernel, out_shape, operands, flops, name, after=(), moved=None):
    def body(*refs):
        kernel(*refs[: len(operands)], *refs[len(operands) + len(after) :])

    moved = moved or sum(x.size * x.dtype.itemsize for x in operands)
    whole = pl.BlockSpec(memory_space=pltpu.VMEM)
    return pl.pallas_call(
        body,
        out_shape=out_shape,
        in_specs=[whole] * len(operands) + [pl.BlockSpec(memory_space=pl.ANY)] * len(after),
        out_specs=jax.tree.map(lambda _: whole, out_shape),
        compiler_params=pltpu.CompilerParams(vmem_limit_bytes=VMEM_BYTES),
        cost_estimate=pl.CostEstimate(flops=flops, bytes_accessed=moved, transcendentals=0),
        name=name,
    )(*operands, *after)


def shape_of(rows, columns, dtype):
    return jax.ShapeDtypeStruct((rows, columns), dtype)


def column_window(array, start, width):
    if isinstance(array, jax.Array):
        return lax.dynamic_slice_in_dim(array, start, width, array.ndim - 1)
    return array[..., pl.ds(pl.multiple_of(start, width), width)]


def outer_kernel(replicas, share_cols, *refs):
    *held_refs, global_ref, momentum_ref, share_ref, new_momentum_ref = refs
    rows, window = held_refs[-1].shape[-2:]
    me = lax.axis_index("replica")

    def windows_of(ref):
        here = me * share_cols // window * window % ref.shape[-1]
        return ref[...] if ref.shape[-1] == window else column_window(ref, here, window)

    old = windows_of(global_ref).astype(F32)
    lane = lax.broadcasted_iota(jnp.int32, (rows, window), 1) // BLOCK
    total = jnp.zeros((rows, window), F32)
    for held_ref in held_refs:
        held = windows_of(held_ref).astype(F32)
        for local in [held] if held.ndim == 2 else list(held):
            drift = old - local
            size = jnp.abs(drift)
            scale = jnp.zeros((rows, window), F32)
            for block in range(window // BLOCK):
                top = jnp.max(jnp.where(lane == block, size, 0.0), axis=1, keepdims=True)
                top = (top + scale_epsilon).astype(BF16).astype(F32)
                scale = jnp.where(lane == block, top, scale)
            total = total + (drift / scale).astype(BF16).astype(F32) * scale
    mean_grad = total / replicas
    shares = window // share_cols
    mean_here, old_here = mean_grad[:, :share_cols], old[:, :share_cols]
    mine = me % shares
    for share in range(1, shares):
        columns = slice(share * share_cols, (share + 1) * share_cols)
        mean_here = jnp.where(mine == share, mean_grad[:, columns], mean_here)
        old_here = jnp.where(mine == share, old[:, columns], old_here)
    new_momentum = outer_momentum * momentum_ref[...] + mean_here
    new_momentum_ref[...] = new_momentum
    share_ref[...] = (old_here - outer_rate * (mean_here + outer_momentum * new_momentum)).astype(BF16)


def swap(array, bits):
    return lax.ppermute(array, "replica", [(at, at ^ bits) for at in range(lax.axis_size("replica"))])


def partner_kernel(bits, share_cols, width, *refs):
    *held_refs, out_ref = refs
    start = (lax.axis_index("replica") ^ bits) * share_cols // width * width
    at = 0
    for held_ref in held_refs:
        part = column_window(held_ref, start % held_ref.shape[-1], width)
        count = 1 if part.ndim == 2 else part.shape[0]
        out_ref[at : at + count] = part.reshape((count,) + part.shape[-2:])
        at += count


def send_windows(held, bits, kv_width, after):
    replicas = lax.axis_size("replica")
    share_cols = kv_width // replicas
    width = max(bits * share_cols, BLOCK)
    rows = held[0].shape[-2]
    count = sum(1 if array.ndim == 2 else array.shape[0] for array in held)
    if width % LANES == 0:
        leaving = vmem_call(
            functools.partial(partner_kernel, bits, share_cols, width),
            jax.ShapeDtypeStruct((count, rows, width), BF16),
            held,
            0,
            "partner_columns",
            after,
        )
    else:
        start = (lax.axis_index("replica") ^ bits) * share_cols // width * width
        parts = [column_window(array, start % array.shape[-1], width).reshape(-1, rows, width) for array in held]
        leaving = jnp.concatenate(parts)
    return held + [swap(leaving, bits)]


def update_share(held, global_weights, momentum, after):
    rows, share_cols = momentum.shape
    replicas = lax.axis_size("replica")
    window = held[-1].shape[-1]
    if window % LANES:
        start = lax.axis_index("replica") * share_cols // window * window
        held = [column_window(array, start % array.shape[-1], window) for array in held]
        global_weights = column_window(global_weights, start, window)
    return vmem_call(
        functools.partial(outer_kernel, replicas, share_cols),
        (shape_of(rows, share_cols, BF16), shape_of(rows, share_cols, F32)),
        held + [global_weights, momentum],
        0,
        "outer_update",
        after,
    )


def join_kernel(places, *refs):
    *held_refs, out_ref = refs
    width = out_ref.shape[1] // len(places)
    me = lax.axis_index("replica")
    at = 0
    for held_ref in held_refs:
        for start in range(0, held_ref.shape[1], width):
            columns = pl.ds(pl.multiple_of((me ^ places[at]) * width, width), width)
            out_ref[:, columns] = held_ref[:, start : start + width]
            at += 1


def beside_kernel(left_ref, right_ref, out_ref):
    width = left_ref.shape[1]
    out_ref[:, :width] = left_ref[...]
    out_ref[:, width:] = right_ref[...]


def beside(left, right, after):
    rows, width = left.shape
    if width % LANES:
        return jnp.concatenate([left, right], axis=1)
    return vmem_call(beside_kernel, shape_of(rows, 2 * width, BF16), [left, right], 0, "beside", after)


def join_shares(held, places, kv_width, after):
    rows = held[0].shape[0]
    width = kv_width // len(places)
    if width % LANES == 0:
        return vmem_call(
            functools.partial(join_kernel, places), shape_of(rows, kv_width, BF16), held, 0, "join_shares", after
        )
    whole = jnp.concatenate(held, axis=1)
    joined = jnp.zeros_like(whole)
    for at, place in enumerate(places):
        start = (lax.axis_index("replica") ^ place) * width
        joined = lax.dynamic_update_slice_in_dim(joined, whole[:, at * width : (at + 1) * width], start, 1)
    return joined


PARTNER = {2: (0, 0), 1: (0, 1), 3: (1, 0), 0: (1, 1)}


def mark_kernel(out_ref):
    out_ref[...] = jnp.zeros_like(out_ref)


def arrived(after):
    return vmem_call(mark_kernel, shape_of(8, LANES, F32), [], 0, "mark", after)


def pack_kernel(size, part, inputs_ref, out_ref):
    depth = inputs_ref.shape[1] // size
    for offset, (at, slot) in PARTNER.items():
        if at == part:
            out_ref[slot] = inputs_ref[:, pl.ds(block_start(offset, size, depth, 1), depth)]


def pack(inputs_here, size, part, after=()):
    tokens, width = inputs_here.shape
    shape = jax.ShapeDtypeStruct((2, tokens, width // size), BF16)
    return vmem_call(functools.partial(pack_kernel, size, part), shape, [inputs_here], 0, "pack_columns", after)


def terms_kernel(size, offsets, token_weight, inputs_ref, cotangent_ref, partner_ref, partner_cotangent_ref, *out_refs):
    depth = inputs_ref.shape[1] // size
    for offset, out_ref in zip(offsets, out_refs):
        here = inputs_ref[:, pl.ds(block_start(offset, size, depth), depth)]
        there = partner_ref[PARTNER[offset][1]]
        total = 0.0
        for columns, cotangent in ((here, cotangent_ref[...]), (there, partner_cotangent_ref[...])):
            total = total + lax.dot_general(
                columns, cotangent, (((0,), (0,)), ((), ())), preferred_element_type=F32
            )
        out_ref[...] = (total * token_weight).astype(out_ref.dtype)


def token_terms(operands, size, offsets, dtype, token_weight, after=()):
    tokens, width = operands[0].shape
    kv_width = operands[1].shape[1]
    depth = width // size
    return vmem_call(
        functools.partial(terms_kernel, size, offsets, token_weight),
        [shape_of(depth, kv_width, dtype)] * len(offsets),
        operands,
        4 * tokens * depth * len(offsets) * kv_width,
        "token_terms",
        after,
    )


def add_kernel(terms_ref, sum_ref, out_ref):
    out_ref[...] = (terms_ref[...] + sum_ref[...].astype(F32)).astype(BF16)


def back_product(cotangent, block):
    return lax.dot_general(cotangent, block, (((1,), (1,)), ((), ())), preferred_element_type=F32).astype(BF16)


def grads_kernel(cotangent_ref, partner_cotangent_ref, *refs):
    *block_refs, here_ref, leaving_ref = refs
    for number, block_ref in enumerate(block_refs):
        here_ref[number] = back_product(cotangent_ref[...], block_ref[...])
        leaving_ref[number] = back_product(partner_cotangent_ref[...], block_ref[...])


def near_grads(cotangent, partner_cotangent, blocks, after):
    tokens, kv_width = cotangent.shape
    depth = blocks[0].shape[0]
    shape = jax.ShapeDtypeStruct((len(blocks), tokens, depth), BF16)
    operands = [cotangent, partner_cotangent, *blocks.values()]
    flops = 4 * tokens * depth * len(blocks) * kv_width
    return vmem_call(grads_kernel, [shape] * 2, operands, flops, "near_grads", after)


def rows_kernel(size, offsets, inputs_ref, *refs):
    partner_refs, block_refs, (here_ref, there_ref) = refs[:2], refs[2:-2], refs[-2:]
    depth = inputs_ref.shape[1] // size
    here = there = 0.0
    for offset, block_ref in zip(offsets, block_refs):
        at, slot = PARTNER[offset]
        columns = inputs_ref[:, pl.ds(block_start(offset, size, depth), depth)]
        here = here + jnp.dot(columns, block_ref[...], preferred_element_type=F32)
        there = there + jnp.dot(partner_refs[at][slot], block_ref[...], preferred_element_type=F32)
    here_ref[...], there_ref[...] = here, there


def near_rows(inputs_here, partner_inputs, blocks, size, after):
    tokens, kv_width = inputs_here.shape[0], blocks[0].shape[1]
    return vmem_call(
        functools.partial(rows_kernel, size, list(blocks)),
        [shape_of(tokens, kv_width, F32)] * 2,
        [inputs_here, *partner_inputs, *blocks.values()],
        4 * tokens * blocks[0].shape[0] * len(blocks) * kv_width,
        "near_rows",
        after,
    )


def last_kernel(size, offsets, inputs_ref, cotangent_ref, partner_ref, partner_cotangent_ref, *refs):
    block_refs, (here_ref, there_ref, rows_ref, grad_ref, leaving_ref) = refs[: len(offsets)], refs[len(offsets) :]
    depth = block_refs[0].shape[0]
    for number, block_ref in enumerate(block_refs):
        leaving_ref[number] = back_product(partner_cotangent_ref[...], block_ref[...])
    last = block_refs[-1][...]
    there = there_ref[...] + jnp.dot(partner_ref[PARTNER[offsets[-1]][1]], last, preferred_element_type=F32)
    for part in range(there.shape[1] // depth):
        leaving_ref[len(offsets) + part] = there[:, part * depth : (part + 1) * depth].astype(BF16)
    for number, block_ref in enumerate(block_refs):
        grad_ref[number] = back_product(cotangent_ref[...], block_ref[...])
    columns = inputs_ref[:, pl.ds(block_start(offsets[-1], size, depth), depth)]
    rows_ref[...] = here_ref[...] + jnp.dot(columns, last, preferred_element_type=F32)


def last_products(inputs_here, cotangent, partner_inputs, partner_cotangent, blocks, totals, size, after):
    tokens = inputs_here.shape[0]
    offsets = list(blocks)
    depth, kv_width = blocks[offsets[-1]].shape
    partner = partner_inputs[PARTNER[offsets[-1]][0]]
    return vmem_call(
        functools.partial(last_kernel, size, offsets),
        [
            shape_of(tokens, kv_width, F32),
            jax.ShapeDtypeStruct((len(blocks), tokens, depth), BF16),
            jax.ShapeDtypeStruct((len(blocks) + kv_width // depth, tokens, depth), BF16),
        ],
        [inputs_here, cotangent, partner, partner_cotangent, *blocks.values(), *totals],
        8 * tokens * depth * kv_width,
        "last_products",
        after,
    )


def write_columns(size, sources, grad_ref, sems):
    depth = grad_ref.shape[1] // size
    copies = []
    for source_ref, number, offset, other in sources:
        columns = pl.ds(block_start(offset, size, depth, other), depth)
        copies.append(pltpu.make_async_copy(source_ref.at[number], grad_ref.at[:, columns], sems.at[len(copies)]))
        copies[-1].start()
    return copies


def collect_kernel(size, early, late, near_ref, last_ref, early_ref, grad_ref, mark_ref, sems):
    sources = [(near_ref, number, offset, 0) for number, offset in enumerate(early)]
    sources += [(last_ref, number, offset, 0) for number, offset in enumerate(late)]
    sources += [(early_ref, number, offset, 1) for number, offset in enumerate(early)]
    copies = write_columns(size, sources, grad_ref, sems)
    mark_ref[...] = jnp.zeros_like(mark_ref)
    for copy in copies:
        copy.wait()


def collect(grads, width, size, early, late):
    whole, anywhere = pl.BlockSpec(memory_space=pltpu.VMEM), pl.BlockSpec(memory_space=pl.ANY)
    return pl.pallas_call(
        functools.partial(collect_kernel, size, early, late),
        out_shape=(shape_of(grads[0].shape[1], width, BF16), shape_of(8, LANES, F32)),
        in_specs=[whole] * len(grads),
        out_specs=(anywhere, whole),
        scratch_shapes=[pltpu.SemaphoreType.DMA((2 * len(early) + len(late),))],
        compiler_params=pltpu.CompilerParams(vmem_limit_bytes=VMEM_BYTES),
        cost_estimate=pl.CostEstimate(flops=0, bytes_accessed=2**20, transcendentals=0),
        name="collect",
    )(*grads)


def finish_kernel(size, late, total_ref, late_ref, terms_ref, up_ref, down_ref, _, *refs):
    rows_ref, grad_ref, sum_ref, rows_held, sum_held, sems, sem_rows, sem_sum = refs
    copies = write_columns(size, [(late_ref, number, offset, 1) for number, offset in enumerate(late)], grad_ref, sems)
    depth = late_ref.shape[-1]
    for part in range(total_ref.shape[1] // depth):
        columns = slice(part * depth, (part + 1) * depth)
        rows_held[:, columns] = (total_ref[:, columns] + late_ref[len(late) + part].astype(F32)).astype(BF16)
    copies.append(pltpu.make_async_copy(rows_held, rows_ref, sem_rows))
    copies[-1].start()
    sum_held[...] = (terms_ref[...] + up_ref[...].astype(F32) + down_ref[...].astype(F32)).astype(BF16)
    copies.append(pltpu.make_async_copy(sum_held, sum_ref, sem_sum))
    copies[-1].start()
    for copy in copies:
        copy.wait()


def finish(total, late, sums, grad, size, offsets):
    whole, anywhere = pl.BlockSpec(memory_space=pltpu.VMEM), pl.BlockSpec(memory_space=pl.ANY)
    rows, summed = shape_of(*total.shape, BF16), shape_of(*sums[0].shape, BF16)
    return pl.pallas_call(
        functools.partial(finish_kernel, size, offsets),
        out_shape=(rows, shape_of(*grad.shape, BF16), summed),
        in_specs=[whole] * 5 + [anywhere],
        out_specs=(anywhere,) * 3,
        scratch_shapes=[
            pltpu.VMEM(rows.shape, BF16),
            pltpu.VMEM(summed.shape, BF16),
            pltpu.SemaphoreType.DMA((len(offsets),)),
            pltpu.SemaphoreType.DMA,
            pltpu.SemaphoreType.DMA,
        ],
        input_output_aliases={5: 1},
        compiler_params=pltpu.CompilerParams(vmem_limit_bytes=VMEM_BYTES),
        cost_estimate=pl.CostEstimate(flops=0, bytes_accessed=2**20, transcendentals=0),
        name="finish",
    )(total, late, *sums, grad)


def inner_and_outer(local_shard, global_weights, momentum, inputs_here, cotangent):
    depth, kv_width = local_shard.shape
    tokens, width = inputs_here.shape
    size = lax.axis_size("fsdp")
    ring = size // 2
    token_weight = 1.0 / (tokens * size)
    order = ring_order(ring)
    pairs = [(2 * order[at - 1] + side, 2 * order[at] + side) for at in range(ring) for side in (0, 1)]

    def upward(array):
        return lax.ppermute(array, "fsdp", pairs)

    def downward(array):
        return lax.ppermute(array, "fsdp", [(target, source) for source, target in pairs])

    def across(array):
        return lax.ppermute(array, "fsdp", [(at, at ^ 1) for at in range(size)])

    from_below, from_above = upward(local_shard), downward(local_shard)
    partner_cotangent = across(cotangent)
    packed = pack(inputs_here, size, 0)

    bits = lax.axis_size("replica") // 2
    held = send_windows([local_shard], bits, kv_width, (packed,))
    partner_inputs = [across(packed), across(pack(inputs_here, size, 1, (partner_cotangent, arrived((from_below,)))))]

    early_blocks, late_blocks = {0: local_shard, 3: from_below}, {1: from_above, 2: upward(from_below)}
    operands = [inputs_here, cotangent, partner_inputs[0], partner_cotangent]
    first = token_terms(operands, size, [2, 1], BF16, token_weight)
    sum_down, sum_up = downward(first[0]), upward(first[1])
    while bits > 1:
        bits //= 2
        held = send_windows(held, bits, kv_width, first)
    near, leaving = near_grads(cotangent, partner_cotangent, early_blocks, (first[0], held[1]))
    early = across(leaving)
    operands[2] = partner_inputs[1]
    terms = token_terms(operands, size, [3, 0], F32, token_weight, (leaving,))
    totals = near_rows(inputs_here, partner_inputs, {**early_blocks, 1: from_above}, size, (leaving, arrived((late_blocks[2],))))
    rows, last, leaving = last_products(
        inputs_here, cotangent, partner_inputs, partner_cotangent, late_blocks, totals, size, ()
    )
    late = across(leaving)
    new_share, new_momentum = update_share(held, global_weights, momentum, (leaving,))
    total_down = vmem_call(
        add_kernel, shape_of(depth, kv_width, BF16), [terms[0], sum_down], 0, "add_terms", (new_share, early, sum_up)
    )
    sum_down = downward(total_down)
    bits = lax.axis_size("replica")
    shares, joined = [new_share], [0]
    while bits > 1:
        bits //= 2
        shares = [shares[0] if len(shares) == 1 else beside(*shares, ())]
        shares.append(swap(shares[0], bits))
        joined += [place ^ bits for place in joined]
    grad, mark = collect([near, last, early], width, size, list(early_blocks), list(late_blocks))
    new_global = join_shares(shares, joined, kv_width, (mark,))
    kv_rows, grad_in, grad_rows = finish(
        rows, late, [terms[1], sum_up, sum_down], grad, size, list(late_blocks)
    )
    return kv_rows, grad_in, grad_rows, new_global, new_momentum


def plain_inner_and_outer(local_shard, global_weights, momentum, inputs_here, cotangent):
    depth, kv_width = local_shard.shape
    token_weight = 1.0 / (inputs_here.shape[0] * lax.axis_size("fsdp"))
    gathered = lax.all_gather(local_shard, "fsdp", axis=0, tiled=True)
    kv_rows = jnp.dot(inputs_here, gathered, preferred_element_type=F32).astype(BF16)
    grad_in = lax.dot_general(cotangent, gathered, (((1,), (1,)), ((), ())), preferred_element_type=F32).astype(BF16)
    terms = lax.dot_general(inputs_here, cotangent, (((0,), (0,)), ((), ())), preferred_element_type=F32)
    grad_rows = lax.psum_scatter(terms * token_weight, "fsdp", scatter_dimension=0, tiled=True).astype(BF16)
    bits = lax.axis_size("replica")
    held = [local_shard]
    while bits > 1:
        bits //= 2
        held = send_windows(held, bits, kv_width, ())
    new_share, new_momentum = update_share(held, global_weights, momentum, ())
    shares, joined = [new_share], [0]
    bits = lax.axis_size("replica")
    while bits > 1:
        bits //= 2
        shares = [jnp.concatenate(shares, axis=1)]
        shares.append(swap(shares[0], bits))
        joined += [place ^ bits for place in joined]
    return kv_rows, grad_in, grad_rows, join_shares(shares, joined, kv_width, ()), new_momentum


def per_device(local_weights, global_weights, momentum, activations, kv_cotangent):
    depth = local_weights.shape[1]
    pairs_fit = lax.axis_size("fsdp") == 8 and depth % LANES == 0 and local_weights.shape[2] % depth == 0
    step = inner_and_outer if pairs_fit else plain_inner_and_outer
    kv_rows, grad_in, grad_rows, new_global, new_momentum = step(
        local_weights[0], global_weights, momentum, activations[0], kv_cotangent[0]
    )
    return kv_rows[None], grad_in[None], grad_rows[None], new_global, new_momentum


def solution(mesh):
    placed = (
        P("replica", "fsdp", None),
        P("fsdp", None),
        P("fsdp", "replica"),
        P("replica", "fsdp", None),
        P("replica", "fsdp", None),
    )
    return jax.shard_map(
        per_device,
        mesh=mesh,
        in_specs=placed,
        out_specs=(
            P("replica", "fsdp", None),
            P("replica", "fsdp", None),
            P("replica", "fsdp", None),
            P("fsdp", None),
            P("fsdp", "replica"),
        ),
        check_vma=False,
    )
```
